128 devices in a mesh: seq: 16 (over y, z_lo, core), batch: 8 (over z_hi, x).
Axes of the slice: x: 4, y: 4, z: 4 (z_hi: 2, z_lo: 2; z = z_hi * 2 + z_lo), core: 2. Of those that a mesh axis runs over, the one named last changes fastest.
Arguments:
- tokens: bfloat16 [2048, 16, 768], P('seq', 'batch'), may hold values from -6 to 6
- lengths: int32 [16], P('batch'), may hold values from 64 to 2048, as said below
- gain_one: bfloat16 [768], P(('seq', 'batch')), may hold values from 0.5 to 1.5
- bias_one: bfloat16 [768], P(('seq', 'batch')), may hold values from -3 to 3
- w_qkv: bfloat16 [768, 2304], P(('seq', 'batch')), may hold values from -0.21875 to 0.21875
- w_out: bfloat16 [768, 768], P(('seq', 'batch')), may hold values from -0.875 to 0.875
- gain_two: bfloat16 [768], P(('seq', 'batch')), may hold values from 0.5 to 1.5
- bias_two: bfloat16 [768], P(('seq', 'batch')), may hold values from -3 to 3
- w_up: bfloat16 [768, 3072], P(('seq', 'batch')), may hold values from -0.21875 to 0.21875
- w_down: bfloat16 [3072, 768], P(('seq', 'batch')), may hold values from -0.109375 to 0.109375
- d_out: bfloat16 [2048, 16, 768], P('seq', 'batch'), may hold values from -6 to 6
Outputs:
- output: bfloat16 [2048, 16, 768], P('seq', 'batch')
- d_tokens: bfloat16 [2048, 16, 768], P('seq', 'batch')
- d_gain_one: float32 [768], P(('seq', 'batch'))
- d_bias_one: float32 [768], P(('seq', 'batch'))
- d_w_qkv: float32 [768, 2304], P(('seq', 'batch'))
- d_w_out: float32 [768, 768], P(('seq', 'batch'))
- d_gain_two: float32 [768], P(('seq', 'batch'))
- d_bias_two: float32 [768], P(('seq', 'batch'))
- d_w_up: float32 [768, 3072], P(('seq', 'batch'))
- d_w_down: float32 [3072, 768], P(('seq', 'batch'))
The draws below stay inside these ranges and needn't reach their ends.
Inputs may be any that keep to these rules, and one draw needn't show every extreme that they name: `lengths`: one sequence has 2048 valid tokens and another 64, in every draw.
All inputs are finite; a program needn't handle non-finite values.
Results may differ from the reference program's by a relative error of at most 0.033.
Values may be sent and summed in bfloat16 or wider, within the bound.
No kernel may reach another device: no remote copies, remote signals or barrier semaphores. Data moves between devices by JAX's collectives and lax.ppermute only.
A program may use at most 192 MiB of HBM per device.

```python
import math
import jax
import jax.numpy as jnp
from jax import lax

D = 768
H = 12
HD = 64
FF = 3072
LEN = 2048
MINLEN = 64
B = 16


def draw_lengths(key, part):
    key = jax.random.fold_in(key, 11)
    keys = jax.random.split(key, 3)
    counts = jax.random.randint(keys[0], (B,), MINLEN, LEN + 1)
    longest = jax.random.randint(keys[1], (), 0, B)
    shortest = (longest + jax.random.randint(keys[2], (), 1, B)) % B
    counts = counts.at[longest].set(LEN).at[shortest].set(MINLEN)
    return counts.astype(jnp.int32)


def block_scale(key, shape, cuts, smallest, high):
    def one(position, blocks):
        draws = jax.random.uniform(jax.random.fold_in(jax.random.fold_in(key, 6), position), (blocks,), jnp.float32, smallest / len(cuts), high / len(cuts))
        return jnp.repeat(jnp.exp(draws), shape[position] // blocks).reshape((-1,) + (1,) * (len(shape) - position - 1))

    level = one(*cuts[0])
    for cut in cuts[1:]:
        level = level * one(*cut)
    return level


def gaussian(rng, shape, deviation, reach, cuts=(), held_as=jnp.bfloat16):
    level = block_scale(rng, shape, cuts, -0.22, 0.18) if cuts else 1.0
    values = jax.random.normal(rng, shape, jnp.float32) * deviation * level
    return jnp.minimum(jnp.maximum(values, -reach), reach).astype(held_as)


def setup_inputs(seed: int = 0) -> dict:
    splits = jax.random.split(jax.random.key(seed), 12)
    tokens = gaussian(splits[0], (LEN, B, D), 1.0, 6.0, ((0, 16), (1, 8)))
    lengths = draw_lengths(jax.random.fold_in(splits[11], 71), 0)
    gain_one = jnp.clip(1.0 + 0.1 * jax.random.normal(splits[2], (D,), jnp.float32), 0.5, 1.5).astype(jnp.bfloat16)
    bias_one = gaussian(splits[3], (D,), 0.5, 3.0, ((0, 128),))
    w_qkv = gaussian(splits[4], (D, 3 * D), D ** -0.5, 0.21875, ((0, 128),))
    w_out = gaussian(splits[5], (D, D), (D // 16) ** -0.5, 0.875, ((0, 128),))
    gain_two = jnp.clip(1.0 + 0.1 * jax.random.normal(splits[6], (D,), jnp.float32), 0.5, 1.5).astype(jnp.bfloat16)
    bias_two = gaussian(splits[7], (D,), 0.5, 3.0, ((0, 128),))
    w_up = gaussian(splits[8], (D, FF), D ** -0.5, 0.21875, ((0, 128),))
    w_down = gaussian(splits[9], (FF, D), FF ** -0.5, 0.109375, ((0, 128),))
    d_out = gaussian(splits[10], (LEN, B, D), 1.0, 6.0, ((0, 16), (1, 8)))
    return dict(tokens=tokens, lengths=lengths, gain_one=gain_one, bias_one=bias_one, w_qkv=w_qkv, w_out=w_out, gain_two=gain_two, bias_two=bias_two, w_up=w_up, w_down=w_down, d_out=d_out)


@jax.custom_vjp
def low(v):
    return lax.optimization_barrier(v.astype(jnp.bfloat16)).astype(jnp.float32)

@jax.custom_vjp
def low_back(v):
    return v

def low_keep(v):
    return (low(v), None)

def low_pass(kept, grad):
    return (grad,)

def back_keep(v):
    return (v, None)

def back_low(kept, grad):
    return (low(grad),)
low.defvjp(low_keep, low_pass)
low_back.defvjp(back_keep, back_low)
EPSILON = 1e-05

def layer_norm(values, gain, bias):
    center = lax.optimization_barrier(jnp.mean(values, axis=-1, keepdims=True))
    shifted = values - center
    spread = lax.optimization_barrier(jnp.mean(shifted * shifted, axis=-1, keepdims=True))
    return shifted * lax.rsqrt(spread + EPSILON) * gain + bias

def matmul(left, right):
    return jnp.dot(left, right, precision=lax.Precision.HIGHEST)

def attend_one(inputs):
    queries, keys, values, length = inputs
    factor = 1.0 / math.sqrt(HD)
    scores = jnp.einsum('qhd,khd->hqk', queries, keys, precision=lax.Precision.HIGHEST) * factor
    scores = low_back(scores)
    smooth = jnp.sqrt(scores * scores + 1.0)
    slope = scores / smooth
    places = jnp.arange(LEN, dtype=jnp.int32)
    allowed = (places[None, :] <= places[:, None]) & (places[None, :] < length)
    allowed = allowed[None, :, :]
    highest = lax.optimization_barrier(jnp.max(jnp.where(allowed, smooth, 0.0), axis=-1, keepdims=True))
    expo = jnp.where(allowed, jnp.exp(jnp.where(allowed, smooth - highest, -30.0)), 0.0)
    totals = lax.optimization_barrier(jnp.sum(expo, axis=-1, keepdims=True))
    weights = low(slope * expo / totals)
    return jnp.einsum('hqk,khd->qhd', weights, values, precision=lax.Precision.HIGHEST)

def reference(tokens, lengths, gain_one, bias_one, w_qkv, w_out, gain_two, bias_two, w_up, w_down, d_out):

    def forward(inputs, gain_a, bias_a, qkv_weight, out_weight, gain_b, bias_b, up_weight, down_weight):
        normed = low(layer_norm(inputs, gain_a, bias_a))
        mixed = low_back(low(matmul(normed, qkv_weight)))
        heads = mixed.reshape(LEN, B, 3, H, HD)
        queries = jnp.moveaxis(heads[:, :, 0], 1, 0)
        keys = jnp.moveaxis(heads[:, :, 1], 1, 0)
        values = jnp.moveaxis(heads[:, :, 2], 1, 0)
        attended = lax.map(jax.checkpoint(attend_one), (queries, keys, values, lengths))
        attended = jnp.moveaxis(attended, 0, 1).reshape(LEN, B, D)
        attended = low_back(low(attended))
        first = inputs + low_back(matmul(attended, out_weight))
        normed_two = low(layer_norm(first, gain_b, bias_b))
        hidden = low_back(matmul(normed_two, up_weight))
        active = low(jax.nn.gelu(hidden))
        return first + low_back(matmul(active, down_weight))
    floats = tuple((item.astype(jnp.float32) for item in (tokens, gain_one, bias_one, w_qkv, w_out, gain_two, bias_two, w_up, w_down)))
    result, pull = jax.vjp(forward, *floats)
    grads = pull(d_out.astype(jnp.float32))
    return (result.astype(jnp.bfloat16), grads[0].astype(jnp.bfloat16), grads[1], grads[2], grads[3], grads[4], grads[5], grads[6], grads[7], grads[8])
```

```python
import functools
import math

import jax
import jax.numpy as jnp
import numpy as np
from jax import lax
from jax.experimental import pallas as pl
from jax.experimental.pallas import tpu as pltpu
from jax.sharding import PartitionSpec as P

H = 12
HD = 64
EPSILON = 1e-05
BF = jnp.bfloat16
F32 = jnp.float32
VMEM_LIMIT = 50 * 1024 * 1024
BOTH = ("seq", "batch")
SAME_CORE = [[2 * k + c for k in range(8)] for c in range(2)]
SWAP_CORE = [(i, i ^ 1) for i in range(16)]
TURNS = [(0, 0), (0, 1), (0, 2), (0, 3), (1, 3), (1, 2), (1, 1), (1, 0)]
RING = [(c ^ (i & 1), z, x) for i, (z, x) in enumerate(TURNS) for c in range(2)]
RINGS = [
    [((y * 2 + (low ^ z)) * 2 + c) * 8 + z * 4 + x for c, z, x in RING]
    for y in range(4)
    for low in range(2)
]


def one_hot(rows):
    out = np.zeros((len(rows), len(rows)), np.float32)
    out[np.arange(len(rows)), rows] = 1.0
    return out


def in_order(outer, size):
    natural = np.arange(outer * 16 * size).reshape(outer, 2, 8, size)
    return np.stack([natural[:, c, z * 4 + x] for c, z, x in RING])


QKV_ORDER = one_hot(np.arange(768).reshape(8, 2, 8, 6).transpose(1, 2, 0, 3).reshape(768))
ROW_ORDER = one_hot(in_order(8, 6).reshape(768))
UNIT_ORDER = one_hot(in_order(2, 24).reshape(768))


def regroup_matrix():
    out = np.zeros((480, 512), np.float32)
    for j in range(8):
        for r in range(24):
            out[j * 24 + r, j * 64 + r] = 1.0
        for r in range(6):
            for k in range(4):
                out[192 + k * 48 + j * 6 + r, j * 64 + 30 + k * 6 + r] = 1.0
            out[384 + j * 6 + r, j * 64 + 24 + r] = 1.0
            out[432 + j * 6 + r, j * 64 + 54 + r] = 1.0
    return out


REGROUP = regroup_matrix()
NT = (((1,), (1,)), ((), ()))
NN = (((1,), (0,)), ((), ()))
TN = (((0,), (0,)), ((), ()))


def dot(left, right, dims=NN):
    return lax.dot_general(left, right, dims, preferred_element_type=F32)


def about(us):
    return pl.CostEstimate(flops=int(us * 1.1e9), bytes_accessed=0, transcendentals=0)


def call(kernel, outs, ins, us, scratch=(), **kwargs):
    return pl.pallas_call(
        kernel,
        out_shape=outs,
        scratch_shapes=list(scratch),
        cost_estimate=about(us),
        compiler_params=pltpu.CompilerParams(vmem_limit_bytes=VMEM_LIMIT),
        **kwargs,
    )(*ins)


def shape(dims, dtype):
    return jax.ShapeDtypeStruct(dims, dtype)


def normalize(values):
    center = jnp.mean(values, axis=-1, keepdims=True)
    shifted = values - center
    spread = jnp.mean(shifted * shifted, axis=-1, keepdims=True)
    scale = lax.rsqrt(spread + EPSILON)
    return shifted * scale, scale


def regroup_kernel(slots_ref, order_ref, rest_ref, qkv_ref):
    rows = dot(order_ref[...], slots_ref[...].reshape(512, 768)).astype(BF)
    rest_ref[...] = rows[0:432]
    for g in range(8):
        qkv_ref[g] = rows[432:480]


def project_kernel(
    core_ref, own_ref, mine_ref, other_ref, order_ref,
    normed_ref, wt_ref, gains_ref, qkv_ref, w_scr, t_scr,
):
    core = core_ref[0]
    mine = pl.ds(pl.multiple_of(core * 384, 384), 384)
    theirs = pl.ds(pl.multiple_of(384 - core * 384, 384), 384)
    w_scr[mine, :] = mine_ref[...].reshape(384, 768)[:, :640]
    w_scr[theirs, :] = other_ref[...].reshape(384, 768)[:, :640]
    t_scr[...] = dot(w_scr[...].T, order_ref[...])
    wt_ref[...] = t_scr[0:576].astype(BF)
    gains = t_scr[576:584]
    gains_ref[...] = gains
    gain, bias = gains[0:1], gains[1:2]
    for j in range(8):
        hat, _ = normalize(own_ref[j].astype(F32))
        normed_ref[j * 128 : (j + 1) * 128, :] = (hat * gain + bias).astype(BF)
    for j in range(4):
        qkv_ref[:, j * 256 : (j + 1) * 256] = dot(
            wt_ref[...], normed_ref[j * 256 : (j + 1) * 256, :], NT
        ).astype(BF)


def tile_mask(first_key, first_query, core, length):
    row = lax.broadcasted_iota(jnp.int32, (256, 256), 0)
    lane = lax.broadcasted_iota(jnp.int32, (256, 256), 1)
    key = first_key + jnp.where(row < 128, row + 128 * core, row - 128 * core)
    query = first_query + 128 * core + jnp.where(lane < 128, lane, lane + 128)
    return (key <= query) & (key < length)


def fill_keys(own_ref, other_ref, k_scr, base):
    for u in range(3):
        for j in range(8):
            rows, lanes = pl.ds(base + u * 64, 64), pl.ds(j * 128, 128)
            k_scr[u, j * 256 : j * 256 + 128, :] = own_ref[rows, lanes].T
            k_scr[u, j * 256 + 128 : j * 256 + 256, :] = other_ref[rows, lanes].T


def fill_lanes(own_ref, other_ref, scr, base):
    for j in range(8):
        scr[:, j * 256 : j * 256 + 128] = own_ref[base : base + 192, j * 128 : j * 128 + 128]
        scr[:, j * 256 + 128 : j * 256 + 256] = other_ref[
            base : base + 192, j * 128 : j * 128 + 128
        ]


def loop_bounds(m, length):
    full = jnp.minimum(2 * m, length // 256)
    every = jnp.minimum(2 * m + 2, (length + 255) // 256)
    return full, every


def forward_kernel(info_ref, q_ref, own_ref, other_ref, o_ref, low_ref, lse_ref, k_scr, v_scr):
    length, core = info_ref[0], info_ref[1]
    fill_keys(own_ref, other_ref, k_scr, 0)
    fill_lanes(own_ref, other_ref, v_scr, 192)
    for m in range(4):
        lanes = slice(m * 256, (m + 1) * 256)
        queries = [q_ref[u * 64 : (u + 1) * 64, lanes] * BF(0.125) for u in range(3)]

        def step(jk, carry, masked, queries=queries, m=m):
            start = pl.multiple_of(jk * 256, 256)
            if masked:
                allowed = tile_mask(start, m * 512, core, length)
            out = []
            for u in range(3):
                top, total, accum = carry[u]
                s = dot(k_scr[u, pl.ds(start, 256), :], queries[u])
                t = s * s + 1.0
                r = lax.rsqrt(t)
                a = t * r
                g = s * r
                if masked:
                    a = jnp.where(allowed, a, -1e30)
                fresh = jnp.maximum(top, jnp.max(a, axis=0, keepdims=True))
                e = jnp.exp(a - fresh)
                rescale = jnp.exp(top - fresh)
                total = total * rescale + jnp.sum(e, axis=0, keepdims=True)
                w = (g * e).astype(BF)
                accum = accum * rescale + dot(
                    v_scr[u * 64 : (u + 1) * 64, pl.ds(start, 256)], w
                )
                out.append((fresh, total, accum))
            return tuple(out)

        zero = (jnp.zeros((1, 256), F32), jnp.zeros((1, 256), F32), jnp.zeros((64, 256), F32))
        full, every = loop_bounds(m, length)
        carry = lax.fori_loop(0, full, functools.partial(step, masked=False), (zero,) * 3)
        carry = lax.fori_loop(full, every, functools.partial(step, masked=True), carry)
        for u in range(3):
            top, total, accum = carry[u]
            o = accum / total
            o_ref[u * 64 : (u + 1) * 64, lanes] = o
            for half in range(2):
                low_ref[2 * m + half, u * 64 : (u + 1) * 64, :] = o[
                    :, half * 128 : half * 128 + 128
                ].astype(BF)
            lse_ref[u : u + 1, lanes] = top + jnp.log(total)


def backward_kernel(
    info_ref, q_ref, own_ref, other_ref, o_ref, lse_ref, da_ref,
    dq_ref, down_ref, dother_ref,
    k_scr, kt_scr, v_scr, dk_scr, dv_scr,
):
    length, core = info_ref[0], info_ref[1]
    fill_keys(own_ref, other_ref, k_scr, 0)
    fill_lanes(own_ref, other_ref, kt_scr, 0)
    fill_keys(own_ref, other_ref, v_scr, 192)
    dk_scr[...] = jnp.zeros_like(dk_scr)
    dv_scr[...] = jnp.zeros_like(dv_scr)
    for m in range(4):
        lanes = slice(m * 256, (m + 1) * 256)
        sets = []
        for u in range(3):
            rows = slice(u * 64, (u + 1) * 64)
            qt = q_ref[rows, lanes] * BF(0.125)
            dat = jnp.concatenate([da_ref[2 * m, rows, :], da_ref[2 * m + 1, rows, :]], axis=1)
            delta = jnp.sum(dat.astype(F32) * o_ref[rows, lanes], axis=0, keepdims=True)
            sets.append((qt, qt.T, dat, dat.T, delta, lse_ref[u : u + 1, lanes]))

        def step(jk, carry, masked, sets=sets, m=m):
            start = pl.multiple_of(jk * 256, 256)
            tile = pl.ds(start, 256)
            if masked:
                allowed = tile_mask(start, m * 512, core, length)
            out = []
            for u in range(3):
                qt, q, dat, da, delta, lse = sets[u]
                s = dot(k_scr[u, tile, :], qt)
                dp = dot(v_scr[u, tile, :], dat)
                t = s * s + 1.0
                r = lax.rsqrt(t)
                g = s * r
                p = jnp.exp(t * r - lse)
                if masked:
                    p = jnp.where(allowed, p, 0.0)
                w = (g * p).astype(BF)
                ds = (p * (dp * (r * r * (r - 1.0) + 1.0) - g * delta)).astype(BF)
                dv_scr[u, tile, :] += dot(w, da)
                dk_scr[u, tile, :] += dot(ds, q)
                out.append(carry[u] + dot(kt_scr[u * 64 : (u + 1) * 64, tile], ds))
            return tuple(out)

        full, every = loop_bounds(m, length)
        carry = (jnp.zeros((64, 256), F32),) * 3
        carry = lax.fori_loop(0, full, functools.partial(step, masked=False), carry)
        carry = lax.fori_loop(full, every, functools.partial(step, masked=True), carry)
        for u in range(3):
            dq_ref[u * 64 : (u + 1) * 64, lanes] = (carry[u] * 0.125).astype(BF)
    for scr, base in ((dk_scr, 0), (dv_scr, 192)):
        for u in range(3):
            for j in range(8):
                rows, lanes = pl.ds(base + u * 64, 64), pl.ds(j * 128, 128)
                down_ref[rows, lanes] = scr[u, j * 256 : j * 256 + 128, :].T
                dother_ref[rows, lanes] = scr[u, j * 256 + 128 : j * 256 + 256, :].T.astype(BF)


GELU_SCALE = math.sqrt(2.0 / math.pi)


def feed_kernel(
    x_ref, dy_ref, att_ref, gains_ref, order_ref, order_t_ref, down_ref, up_ref, out_ref,
    y_ref, dfirst_ref, datt_ref, dgain_ref, grads_ref,
    hat_scr, scale_scr, n2_scr, n2t_scr, acc_scr, dn_scr, attt_scr, gdown, gup, gout, sems,
):
    k = pl.program_id(0)
    gain, bias = gains_ref[2:3], gains_ref[3:4]

    @pl.when(k == 0)
    def _():
        for b in range(2):
            natural = att_ref[b * 4 : b * 4 + 4].reshape(768, 128)
            attt_scr[:, b * 128 : (b + 1) * 128] = dot(order_ref[...], natural).astype(BF)
        first = x_ref[...].astype(F32) + dot(attt_scr[...].T, out_ref[...].reshape(768, 768))
        hat, scale = normalize(first)
        hat_scr[...] = hat
        scale_scr[...] = scale
        n2 = dot((hat * gain + bias).astype(BF), order_ref[...], NT).astype(BF)
        n2_scr[...] = n2
        n2t_scr[...] = n2.T
        acc_scr[...] = first
        dn_scr[...] = jnp.zeros_like(dn_scr)

    up = up_ref[...].reshape(768, 768)
    down = down_ref[...].reshape(768, 768)
    dy = dy_ref[...]
    hidden = dot(n2_scr[...], up)
    d_active = dot(dy, down, NT)
    square = hidden * hidden
    tanh = jnp.tanh(GELU_SCALE * hidden * (1.0 + 0.044715 * square))
    share = 0.5 + 0.5 * tanh
    active = (hidden * share).astype(BF)
    slope = share + 0.5 * hidden * (1.0 - tanh * tanh) * (
        GELU_SCALE * (1.0 + (3 * 0.044715) * square)
    )
    d_hidden = (slope * d_active).astype(BF)
    acc_scr[...] += dot(active, down)
    dn_scr[...] += dot(d_hidden, up, NT)
    gdown[k] = dot(active.T, dy).astype(BF).reshape(16, 48, 768)
    gup[k] = dot(n2t_scr[...], d_hidden).astype(BF).reshape(16, 48, 768)

    def copy(source, block, sem):
        return pltpu.make_async_copy(
            source, grads_ref.at[:, pl.ds(48 * block, 48), :], sems.at[sem]
        )

    for i in range(4):

        @pl.when(k == i)
        def _(i=i):
            copy(gdown.at[i], i, i).start()
            copy(gup.at[i], 4 + i, 4 + i).start()

    @pl.when(k == 3)
    def _():
        y_ref[...] = acc_scr[...].astype(BF)
        dn = dn_scr[...]
        high = dn.astype(BF)
        low = (dn - high.astype(F32)).astype(BF)
        dn = dot(high, order_ref[...]) + dot(low, order_ref[...])
        hat = hat_scr[...]
        dgain_ref[0:1, :] = jnp.sum(dn * hat, axis=0, keepdims=True)
        dgain_ref[1:2, :] = jnp.sum(dn, axis=0, keepdims=True)
        dgain_ref[2:8, :] = jnp.zeros((6, 768), F32)
        t = dn * gain
        part = t - jnp.mean(t, -1, keepdims=True) - hat * jnp.mean(t * hat, -1, keepdims=True)
        d_first = dy.astype(F32) + part * scale_scr[...]
        dfirst_ref[...] = d_first
        low = d_first.astype(BF)
        gout[...] = dot(attt_scr[...], low).astype(BF).reshape(16, 48, 768)
        copy(gout, 8, 8).start()
        d_att = dot(out_ref[...].reshape(768, 768), low, NT).astype(BF)
        d_att = dot(order_t_ref[...], d_att).astype(BF)
        for b in range(2):
            datt_ref[b * 4 : b * 4 + 4] = d_att[:, b * 128 : (b + 1) * 128].reshape(4, 192, 128)
        for i in range(4):
            copy(gdown.at[i], i, i).wait()
            copy(gup.at[i], 4 + i, 4 + i).wait()
        copy(gout, 8, 8).wait()


def whole(*dims):
    return pl.BlockSpec(dims, lambda i: (0,) * len(dims))


def feed(x, dy, att, gains, order, order_t, weights):
    return pl.pallas_call(
        feed_kernel,
        grid=(4,),
        in_specs=[
            whole(256, 768), whole(256, 768), whole(8, 192, 128), whole(8, 768),
            whole(768, 768), whole(768, 768),
            pl.BlockSpec((16, 48, 768), lambda k: (0, k, 0)),
            pl.BlockSpec((16, 48, 768), lambda k: (0, 4 + k, 0)),
            pl.BlockSpec((16, 48, 768), lambda k: (0, 8, 0)),
        ],
        out_specs=[
            whole(256, 768), whole(256, 768), whole(8, 192, 128), whole(8, 768),
            pl.BlockSpec(memory_space=pl.ANY),
        ],
        out_shape=[
            shape((256, 768), BF), shape((256, 768), F32), shape((8, 192, 128), BF),
            shape((8, 768), F32), shape((16, 432, 768), BF),
        ],
        scratch_shapes=[
            pltpu.VMEM((256, 768), F32), pltpu.VMEM((256, 1), F32),
            pltpu.VMEM((256, 768), BF), pltpu.VMEM((768, 256), BF), pltpu.VMEM((256, 768), F32),
            pltpu.VMEM((256, 768), F32), pltpu.VMEM((768, 256), BF),
            pltpu.VMEM((4, 16, 48, 768), BF), pltpu.VMEM((4, 16, 48, 768), BF),
            pltpu.VMEM((16, 48, 768), BF), pltpu.SemaphoreType.DMA((9,)),
        ],
        cost_estimate=about(18),
        compiler_params=pltpu.CompilerParams(vmem_limit_bytes=VMEM_LIMIT),
    )(x, dy, att, gains, order, order_t, weights, weights, weights)


def unproject_kernel(
    core_ref, own_ref, dq_ref, dkv_ref, partner_ref, normed_ref, wt_ref, dgain_ref, order_ref,
    part_ref, mine_ref, theirs_ref, dt_scr, dw_scr, p_scr,
):
    core = core_ref[0]
    dt_scr[0:192, :] = dq_ref[...]
    dt_scr[192:576, :] = (dkv_ref[...] + partner_ref[...].astype(F32)).astype(BF)
    dw_scr[0:576, :] = dot(dt_scr[...], normed_ref[...])
    bias_sum = jnp.zeros((1, 768), F32)
    gain_sum = jnp.zeros((1, 768), F32)
    for j in range(8):
        d_normed = dot(dt_scr[:, j * 128 : (j + 1) * 128].T, wt_ref[...])
        part_ref[j] = d_normed.astype(BF)
        hat, _ = normalize(own_ref[j].astype(F32))
        gain_sum += jnp.sum(d_normed * hat, axis=0, keepdims=True)
        bias_sum += jnp.sum(d_normed, axis=0, keepdims=True)
    dw_scr[576:577, :] = gain_sum
    dw_scr[577:578, :] = bias_sum
    dw_scr[578:580, :] = dgain_ref[0:2, :]
    dw_scr[580:640, :] = jnp.zeros((60, 768), F32)
    p_scr[...] = dot(order_ref[...], dw_scr[...].astype(BF), NT).astype(BF)
    blank = jnp.zeros((8, 48, 128), BF)
    for ref, first in ((mine_ref, core * 384), (theirs_ref, 384 - core * 384)):
        rows = pl.ds(pl.multiple_of(first, 384), 384)
        ref[:, :, 0:640] = p_scr[rows, :].reshape(8, 48, 640)
        ref[:, :, 640:768] = blank


def slots_kernel(rest_ref, qkv_ref, order_ref, out_ref, r_scr):
    r_scr[0:432, :] = rest_ref[...]
    total = jnp.zeros((48, 768), F32)
    for g in range(8):
        total += qkv_ref[g].astype(F32)
    r_scr[432:480, :] = total.astype(BF)
    out_ref[...] = dot(order_ref[...], r_scr[...], TN).astype(BF).reshape(8, 64, 768)


def finish_kernel(x_ref, dfirst_ref, gains_ref, got_ref, dtok_ref):
    gain = gains_ref[0:1]
    for b in range(2):
        rows = slice(b * 128, (b + 1) * 128)
        dn = jnp.zeros((128, 768), F32)
        for e in range(4):
            dn += got_ref[4 * b + e].astype(F32)
        hat, scale = normalize(x_ref[rows, :].astype(F32))
        t = dn * gain
        part = t - jnp.mean(t, -1, keepdims=True) - hat * jnp.mean(t * hat, -1, keepdims=True)
        dtok_ref[rows, :] = (dfirst_ref[rows, :] + part * scale).astype(BF)


def sums_kernel(got_ref, units_ref, sum_ref, up_ref, dw_ref):
    total = jnp.zeros((64, 768), F32)
    for e in range(4):
        both = got_ref[e].astype(F32) + got_ref[4 + e].astype(F32)
        dw_ref[e] = both
        total += both
    sum_ref[...] = total
    up_ref[...] = lax.dot_general(
        total, units_ref[...], NN, precision=lax.Precision.HIGHEST, preferred_element_type=F32
    )


def scalars(count):
    return dict(
        in_specs=[pl.BlockSpec(memory_space=pltpu.SMEM)]
        + [pl.BlockSpec(memory_space=pltpu.VMEM)] * (count - 1)
    )


def body(tokens, lengths, gain_one, bias_one, w_qkv, w_out, gain_two, bias_two, w_up, w_down, d_out):
    place = lax.axis_index("seq")
    core = lax.rem(place, 2)
    length = lengths[place // 8]
    info = jnp.stack([length, core]).astype(jnp.int32)
    core_info = core.reshape(1).astype(jnp.int32)
    order = jnp.asarray(ROW_ORDER, BF)
    order_t = jnp.asarray(ROW_ORDER.T, BF)
    qkv_order = jnp.asarray(QKV_ORDER, BF)
    regroup = jnp.asarray(REGROUP, BF)
    exchange = functools.partial(
        lax.all_to_all, axis_name="seq", split_axis=0, concat_axis=0, tiled=True,
        axis_index_groups=SAME_CORE,
    )

    qkv = w_qkv.reshape(6, 3, 4, 192).transpose(2, 0, 1, 3).reshape(4, 6, 576)
    norms = jnp.stack([gain_one, bias_one, gain_two, bias_two], axis=1)
    qkv = jnp.concatenate(
        [qkv, jnp.broadcast_to(norms[None], (4, 6, 4)), jnp.zeros((4, 6, 188), BF)], axis=2
    )
    up = w_up.reshape(6, 4, 768).transpose(1, 0, 2).reshape(24, 768)
    up = dot(up, jnp.asarray(UNIT_ORDER.T, BF)).astype(BF)
    shared = jnp.concatenate([w_down, w_out, up], axis=0)
    slot = jnp.concatenate(
        [jnp.broadcast_to(shared[None], (4, 54, 768)), qkv, jnp.zeros((4, 4, 768), BF)], axis=1
    )
    slots = exchange(jnp.broadcast_to(slot[None], (2, 4, 64, 768)).reshape(8, 64, 768))
    rest, qkv_rows = call(
        regroup_kernel,
        [shape((432, 768), BF), shape((8, 48, 768), BF)],
        (slots, regroup),
        2,
    )
    weights = lax.all_gather(rest, BOTH, axis=0, axis_index_groups=RINGS)
    qkv_mine = lax.all_to_all(qkv_rows, "batch", 0, 0, tiled=True)
    qkv_other = lax.ppermute(qkv_mine, "seq", SWAP_CORE)
    x = tokens.transpose(1, 0, 2)
    dy = d_out.transpose(1, 0, 2).reshape(256, 768)
    own = exchange(jnp.broadcast_to(x[:, None], (2, 4, 128, 768)).reshape(8, 128, 768))
    x = x.reshape(256, 768)

    normed, wt, gains, qkv_t = call(
        project_kernel,
        [shape((1024, 768), BF), shape((576, 768), BF), shape((8, 768), F32), shape((576, 1024), BF)],
        (core_info, own, qkv_mine, qkv_other, qkv_order),
        5,
        [pltpu.VMEM((768, 640), BF), pltpu.VMEM((640, 768), F32)],
        **scalars(5),
    )
    q_t, kv = qkv_t[:192], qkv_t[192:]
    kv_other = lax.ppermute(kv, "seq", SWAP_CORE)
    o, o_low, lse = call(
        forward_kernel,
        [shape((192, 1024), F32), shape((8, 192, 128), BF), shape((3, 1024), F32)],
        (info, q_t, kv, kv_other),
        13,
        [pltpu.VMEM((3, 2048, 64), BF), pltpu.VMEM((192, 2048), BF)],
        **scalars(4),
    )
    att = exchange(o_low)
    y, d_first, d_att, d_gain, grads = feed(x, dy, att, gains, order, order_t, weights)

    rest_sum = lax.psum_scatter(
        grads.reshape(16 * 432, 768), BOTH, scatter_dimension=0, tiled=True,
        axis_index_groups=RINGS,
    )
    d_att = exchange(d_att)
    dq, dkv, dkv_other = call(
        backward_kernel,
        [shape((192, 1024), BF), shape((384, 1024), F32), shape((384, 1024), BF)],
        (info, q_t, kv, kv_other, o, lse, d_att),
        17,
        [
            pltpu.VMEM((3, 2048, 64), BF),
            pltpu.VMEM((192, 2048), BF),
            pltpu.VMEM((3, 2048, 64), BF),
            pltpu.VMEM((3, 2048, 64), F32),
            pltpu.VMEM((3, 2048, 64), F32),
        ],
        **scalars(7),
    )
    partner = lax.ppermute(dkv_other, "seq", SWAP_CORE)
    part, mine, theirs = call(
        unproject_kernel,
        [shape((8, 128, 768), BF), shape((8, 48, 768), BF), shape((8, 48, 768), BF)],
        (core_info, own, dq, dkv, partner, normed, wt, d_gain, qkv_order),
        7,
        [pltpu.VMEM((576, 1024), BF), pltpu.VMEM((640, 768), F32), pltpu.VMEM((768, 640), BF)],
        **scalars(9),
    )
    theirs = lax.ppermute(theirs, "seq", SWAP_CORE)
    mine = (mine.astype(F32) + theirs.astype(F32)).astype(BF)
    qkv_sums = lax.all_to_all(mine, "batch", 0, 0, tiled=True)
    back = exchange(part)
    d_tokens = call(finish_kernel, shape((256, 768), BF), (x, d_first, gains, back), 3)
    slots = call(
        slots_kernel,
        shape((8, 64, 768), BF),
        (rest_sum, qkv_sums, regroup),
        2,
        [pltpu.VMEM((480, 768), BF)],
    )
    slots = exchange(slots)
    total, d_up, d_qkv = call(
        sums_kernel,
        [shape((64, 768), F32), shape((64, 768), F32), shape((4, 64, 768), F32)],
        (slots, jnp.asarray(UNIT_ORDER, F32)),
        2,
    )
    norms = total[54:60, 576:580]
    d_up = d_up[30:54].reshape(4, 6, 768).transpose(1, 0, 2).reshape(6, 3072)
    d_qkv = d_qkv[:, 54:60, :576].reshape(4, 6, 3, 192).transpose(1, 2, 0, 3).reshape(6, 2304)
    output = y.reshape(2, 128, 768).transpose(1, 0, 2)
    d_tokens = d_tokens.reshape(2, 128, 768).transpose(1, 0, 2)
    return (
        output, d_tokens, norms[:, 0], norms[:, 1], d_qkv, total[24:30], norms[:, 2], norms[:, 3],
        d_up, total[0:24],
    )


def solution(mesh):
    rows = P(("seq", "batch"))
    tokens = P("seq", "batch", None)
    return jax.shard_map(
        body,
        mesh=mesh,
        in_specs=(tokens, P("batch"), rows, rows, rows, rows, rows, rows, rows, rows, tokens),
        out_specs=(tokens, tokens, rows, rows, rows, rows, rows, rows, rows, rows),
        check_vma=False,
    )
```

```python
import functools
import math

import jax
import jax.numpy as jnp
import numpy as np
from jax import lax
from jax.experimental import pallas as pl
from jax.experimental.pallas import tpu as pltpu
from jax.sharding import PartitionSpec as P

H = 12
HD = 64
EPSILON = 1e-05
BF = jnp.bfloat16
F32 = jnp.float32
VMEM_LIMIT = 50 * 1024 * 1024
BOTH = ("seq", "batch")
SAME_CORE = [[2 * k + c for k in range(8)] for c in range(2)]
SWAP_CORE = [(i, i ^ 1) for i in range(16)]
TURNS = [(0, 0), (0, 1), (0, 2), (0, 3), (1, 3), (1, 2), (1, 1), (1, 0)]
RING = [(c, z, x) for z, x in TURNS for c in range(2)]
RINGS = [
    [((y * 2 + (low ^ z)) * 2 + c) * 8 + z * 4 + x for c, z, x in RING]
    for y in range(4)
    for low in range(2)
]


SWAP_Z = [(b, b ^ 4) for b in range(8)]


def along_x(step):
    return [(b, b // 4 * 4 + (b + step) % 4) for b in range(8)]


def one_hot(rows):
    out = np.zeros((len(rows), len(rows)), np.float32)
    out[np.arange(len(rows)), rows] = 1.0
    return out


def in_order(outer, size):
    natural = np.arange(outer * 16 * size).reshape(outer, 2, 8, size)
    return np.stack([natural[:, c, z * 4 + x] for c, z, x in RING])


QKV_ORDER = one_hot(np.arange(768).reshape(8, 2, 8, 6).transpose(1, 2, 0, 3).reshape(768))
ROW_ORDER = one_hot(in_order(8, 6).reshape(768))
UNIT_ORDER = one_hot(in_order(2, 24).reshape(768))


def regroup_matrix():
    out = np.zeros((480, 512), np.float32)
    for j in range(8):
        for r in range(24):
            out[j * 24 + r, j * 64 + r] = 1.0
        for r in range(6):
            for k in range(4):
                out[192 + k * 48 + j * 6 + r, j * 64 + 30 + k * 6 + r] = 1.0
            out[384 + j * 6 + r, j * 64 + 24 + r] = 1.0
            out[432 + j * 6 + r, j * 64 + 54 + r] = 1.0
    return out


REGROUP = regroup_matrix()
NT = (((1,), (1,)), ((), ()))
NN = (((1,), (0,)), ((), ()))
TN = (((0,), (0,)), ((), ()))


def dot(left, right, dims=NN):
    return lax.dot_general(left, right, dims, preferred_element_type=F32)


def about(us):
    return pl.CostEstimate(flops=int(us * 1.1e9), bytes_accessed=0, transcendentals=0)


def call(kernel, outs, ins, us, scratch=(), **kwargs):
    return pl.pallas_call(
        kernel,
        out_shape=outs,
        scratch_shapes=list(scratch),
        cost_estimate=about(us),
        compiler_params=pltpu.CompilerParams(vmem_limit_bytes=VMEM_LIMIT),
        **kwargs,
    )(*ins)


def shape(dims, dtype):
    return jax.ShapeDtypeStruct(dims, dtype)


def normalize(values):
    center = jnp.mean(values, axis=-1, keepdims=True)
    shifted = values - center
    spread = jnp.mean(shifted * shifted, axis=-1, keepdims=True)
    scale = lax.rsqrt(spread + EPSILON)
    return shifted * scale, scale


def pack_kernel(down_ref, out_ref, up_ref, qkv_ref, norms_ref, units_ref, slot_ref, scr):
    up = jnp.concatenate(
        [up_ref[:, k * 768 : (k + 1) * 768].astype(F32) for k in range(4)], axis=0
    ).astype(BF)
    scr[0:24, :] = down_ref[...].astype(F32)
    scr[24:30, :] = out_ref[...].astype(F32)
    scr[30:54, :] = dot(up, units_ref[...], NT)
    scr[60:64, :] = jnp.zeros((4, 768), F32)
    for e in range(4):
        parts = [qkv_ref[:, s * 768 + e * 192 : s * 768 + (e + 1) * 192] for s in range(3)]
        row = jnp.concatenate(parts + [norms_ref[:, 0:64], jnp.zeros((6, 128), BF)], axis=1)
        scr[54:60, :] = row.astype(F32)
        slot = scr[...].astype(BF)
        slot_ref[e] = slot
        slot_ref[4 + e] = slot


def regroup_kernel(slots_ref, order_ref, rest_ref, qkv_ref):
    rows = dot(order_ref[...], slots_ref[...].reshape(512, 768)).astype(BF)
    rest_ref[...] = rows[0:432]
    qkv_ref[...] = rows[432:480, 0:640]


def rows_at(info_ref, dc, dz, dx):
    c = lax.rem(info_ref[1] + dc, 2)
    z = lax.rem(info_ref[2] + dz, 2)
    x = lax.rem(info_ref[3] + dx, 4)
    return pl.ds(pl.multiple_of((c * 8 + z * 4 + x) * 48, 48), 48)


def project_kernel(
    info_ref, own_ref, near_ref, far_ref, near_other_ref, far_other_ref, order_ref,
    normed_ref, wt_ref, gains_ref, qkv_ref, w_scr, t_scr,
):
    for i, ref in enumerate((near_ref, far_ref, near_other_ref, far_other_ref)):
        for dx in range(4):
            w_scr[rows_at(info_ref, i // 2, i % 2, dx), :] = ref[dx]
    t_scr[...] = dot(w_scr[...].T, order_ref[...])
    wt_ref[...] = t_scr[0:576].astype(BF)
    gains = t_scr[576:584]
    gains_ref[...] = gains
    gain, bias = gains[0:1], gains[1:2]
    for j in range(8):
        hat, _ = normalize(own_ref[j].astype(F32))
        normed_ref[j * 128 : (j + 1) * 128, :] = (hat * gain + bias).astype(BF)
    for j in range(4):
        qkv_ref[:, j * 256 : (j + 1) * 256] = dot(
            wt_ref[...], normed_ref[j * 256 : (j + 1) * 256, :], NT
        ).astype(BF)


def tile_mask(first_key, first_query, core, length):
    row = lax.broadcasted_iota(jnp.int32, (256, 256), 0)
    lane = lax.broadcasted_iota(jnp.int32, (256, 256), 1)
    key = first_key + jnp.where(row < 128, row + 128 * core, row - 128 * core)
    query = first_query + 128 * core + jnp.where(lane < 128, lane, lane + 128)
    return (key <= query) & (key < length)


def fill_keys(own_ref, other_ref, k_scr, base):
    for u in range(3):
        for j in range(8):
            rows, lanes = pl.ds(base + u * 64, 64), pl.ds(j * 128, 128)
            k_scr[u, j * 256 : j * 256 + 128, :] = own_ref[rows, lanes].T
            k_scr[u, j * 256 + 128 : j * 256 + 256, :] = other_ref[rows, lanes].T


def fill_lanes(own_ref, other_ref, scr, base):
    for j in range(8):
        scr[:, j * 256 : j * 256 + 128] = own_ref[base : base + 192, j * 128 : j * 128 + 128]
        scr[:, j * 256 + 128 : j * 256 + 256] = other_ref[
            base : base + 192, j * 128 : j * 128 + 128
        ]


def loop_bounds(m, length):
    full = jnp.minimum(2 * m, length // 256)
    every = jnp.minimum(2 * m + 2, (length + 255) // 256)
    return full, every


def forward_kernel(info_ref, q_ref, own_ref, other_ref, o_ref, low_ref, lse_ref, k_scr, v_scr):
    length, core = info_ref[0], info_ref[1]
    fill_keys(own_ref, other_ref, k_scr, 0)
    fill_lanes(own_ref, other_ref, v_scr, 192)
    for m in range(4):
        lanes = slice(m * 256, (m + 1) * 256)
        queries = [q_ref[u * 64 : (u + 1) * 64, lanes] * BF(0.125) for u in range(3)]

        def step(jk, carry, masked, queries=queries, m=m):
            start = pl.multiple_of(jk * 256, 256)
            if masked:
                allowed = tile_mask(start, m * 512, core, length)
            out = []
            for u in range(3):
                top, total, accum = carry[u]
                s = dot(k_scr[u, pl.ds(start, 256), :], queries[u])
                t = s * s + 1.0
                r = lax.rsqrt(t)
                a = t * r
                g = s * r
                if masked:
                    a = jnp.where(allowed, a, -1e30)
                fresh = jnp.maximum(top, jnp.max(a, axis=0, keepdims=True))
                e = jnp.exp(a - fresh)
                rescale = jnp.exp(top - fresh)
                total = total * rescale + jnp.sum(e, axis=0, keepdims=True)
                w = (g * e).astype(BF)
                accum = accum * rescale + dot(
                    v_scr[u * 64 : (u + 1) * 64, pl.ds(start, 256)], w
                )
                out.append((fresh, total, accum))
            return tuple(out)

        zero = (jnp.zeros((1, 256), F32), jnp.zeros((1, 256), F32), jnp.zeros((64, 256), F32))
        full, every = loop_bounds(m, length)
        carry = lax.fori_loop(0, full, functools.partial(step, masked=False), (zero,) * 3)
        carry = lax.fori_loop(full, every, functools.partial(step, masked=True), carry)
        for u in range(3):
            top, total, accum = carry[u]
            o = accum / total
            o_ref[u * 64 : (u + 1) * 64, lanes] = o
            for half in range(2):
                low_ref[2 * m + half, u * 64 : (u + 1) * 64, :] = o[
                    :, half * 128 : half * 128 + 128
                ].astype(BF)
            lse_ref[u : u + 1, lanes] = top + jnp.log(total)


def backward_kernel(
    info_ref, q_ref, own_ref, other_ref, o_ref, lse_ref, da_ref,
    dq_ref, down_ref, dother_ref,
    k_scr, kt_scr, v_scr, dk_scr, dv_scr,
):
    length, core = info_ref[0], info_ref[1]
    fill_keys(own_ref, other_ref, k_scr, 0)
    fill_lanes(own_ref, other_ref, kt_scr, 0)
    fill_keys(own_ref, other_ref, v_scr, 192)
    dk_scr[...] = jnp.zeros_like(dk_scr)
    dv_scr[...] = jnp.zeros_like(dv_scr)
    for m in range(4):
        lanes = slice(m * 256, (m + 1) * 256)
        sets = []
        for u in range(3):
            rows = slice(u * 64, (u + 1) * 64)
            qt = q_ref[rows, lanes] * BF(0.125)
            dat = jnp.concatenate([da_ref[2 * m, rows, :], da_ref[2 * m + 1, rows, :]], axis=1)
            delta = jnp.sum(dat.astype(F32) * o_ref[rows, lanes], axis=0, keepdims=True)
            sets.append((qt, qt.T, dat, dat.T, delta, lse_ref[u : u + 1, lanes]))

        def step(jk, carry, masked, sets=sets, m=m):
            start = pl.multiple_of(jk * 256, 256)
            tile = pl.ds(start, 256)
            if masked:
                allowed = tile_mask(start, m * 512, core, length)
            out = []
            for u in range(3):
                qt, q, dat, da, delta, lse = sets[u]
                s = dot(k_scr[u, tile, :], qt)
                dp = dot(v_scr[u, tile, :], dat)
                t = s * s + 1.0
                r = lax.rsqrt(t)
                g = s * r
                p = jnp.exp(t * r - lse)
                if masked:
                    p = jnp.where(allowed, p, 0.0)
                w = (g * p).astype(BF)
                ds = (p * (dp * (r * r * (r - 1.0) + 1.0) - g * delta)).astype(BF)
                dv_scr[u, tile, :] += dot(w, da)
                dk_scr[u, tile, :] += dot(ds, q)
                out.append(carry[u] + dot(kt_scr[u * 64 : (u + 1) * 64, tile], ds))
            return tuple(out)

        full, every = loop_bounds(m, length)
        carry = (jnp.zeros((64, 256), F32),) * 3
        carry = lax.fori_loop(0, full, functools.partial(step, masked=False), carry)
        carry = lax.fori_loop(full, every, functools.partial(step, masked=True), carry)
        for u in range(3):
            dq_ref[u * 64 : (u + 1) * 64, lanes] = (carry[u] * 0.125).astype(BF)
    for scr, base in ((dk_scr, 0), (dv_scr, 192)):
        for u in range(3):
            for j in range(8):
                rows, lanes = pl.ds(base + u * 64, 64), pl.ds(j * 128, 128)
                down_ref[rows, lanes] = scr[u, j * 256 : j * 256 + 128, :].T
                dother_ref[rows, lanes] = scr[u, j * 256 + 128 : j * 256 + 256, :].T.astype(BF)


GELU_SCALE = math.sqrt(2.0 / math.pi)


def feed_kernel(
    x_ref, dy_ref, att_ref, gains_ref, order_ref, order_t_ref, down_ref, up_ref, out_ref,
    y_ref, dfirst_ref, datt_ref, dgain_ref, grads_ref,
    hat_scr, scale_scr, n2_scr, n2t_scr, acc_scr, dn_scr, attt_scr, gdown, gup, gout, sems,
):
    k = pl.program_id(0)
    gain, bias = gains_ref[2:3], gains_ref[3:4]

    @pl.when(k == 0)
    def _():
        for b in range(2):
            natural = att_ref[b * 4 : b * 4 + 4].reshape(768, 128)
            attt_scr[:, b * 128 : (b + 1) * 128] = dot(order_ref[...], natural).astype(BF)
        first = x_ref[...].astype(F32) + dot(attt_scr[...].T, out_ref[...].reshape(768, 768))
        hat, scale = normalize(first)
        hat_scr[...] = hat
        scale_scr[...] = scale
        n2 = dot((hat * gain + bias).astype(BF), order_ref[...], NT).astype(BF)
        n2_scr[...] = n2
        n2t_scr[...] = n2.T
        acc_scr[...] = first
        dn_scr[...] = jnp.zeros_like(dn_scr)

    up = up_ref[...].reshape(768, 768)
    down = down_ref[...].reshape(768, 768)
    dy = dy_ref[...]
    hidden = dot(n2_scr[...], up)
    d_active = dot(dy, down, NT)
    square = hidden * hidden
    tanh = jnp.tanh(GELU_SCALE * hidden * (1.0 + 0.044715 * square))
    share = 0.5 + 0.5 * tanh
    active = (hidden * share).astype(BF)
    slope = share + 0.5 * hidden * (1.0 - tanh * tanh) * (
        GELU_SCALE * (1.0 + (3 * 0.044715) * square)
    )
    d_hidden = (slope * d_active).astype(BF)
    acc_scr[...] += dot(active, down)
    dn_scr[...] += dot(d_hidden, up, NT)
    gdown[k] = dot(active.T, dy).astype(BF).reshape(16, 48, 768)
    gup[k] = dot(n2t_scr[...], d_hidden).astype(BF).reshape(16, 48, 768)

    def copy(source, block, sem):
        return pltpu.make_async_copy(
            source, grads_ref.at[:, pl.ds(48 * block, 48), :], sems.at[sem]
        )

    for i in range(4):

        @pl.when(k == i)
        def _(i=i):
            copy(gdown.at[i], i, i).start()
            copy(gup.at[i], 4 + i, 4 + i).start()

    @pl.when(k == 3)
    def _():
        y_ref[...] = acc_scr[...].astype(BF)
        dn = dn_scr[...]
        high = dn.astype(BF)
        low = (dn - high.astype(F32)).astype(BF)
        dn = dot(high, order_ref[...]) + dot(low, order_ref[...])
        hat = hat_scr[...]
        dgain_ref[0:1, :] = jnp.sum(dn * hat, axis=0, keepdims=True)
        dgain_ref[1:2, :] = jnp.sum(dn, axis=0, keepdims=True)
        dgain_ref[2:8, :] = jnp.zeros((6, 768), F32)
        t = dn * gain
        part = t - jnp.mean(t, -1, keepdims=True) - hat * jnp.mean(t * hat, -1, keepdims=True)
        d_first = dy.astype(F32) + part * scale_scr[...]
        dfirst_ref[...] = d_first
        low = d_first.astype(BF)
        gout[...] = dot(attt_scr[...], low).astype(BF).reshape(16, 48, 768)
        copy(gout, 8, 8).start()
        d_att = dot(out_ref[...].reshape(768, 768), low, NT).astype(BF)
        d_att = dot(order_t_ref[...], d_att).astype(BF)
        for b in range(2):
            datt_ref[b * 4 : b * 4 + 4] = d_att[:, b * 128 : (b + 1) * 128].reshape(4, 192, 128)
        for i in range(4):
            copy(gdown.at[i], i, i).wait()
            copy(gup.at[i], 4 + i, 4 + i).wait()
        copy(gout, 8, 8).wait()


def whole(*dims):
    return pl.BlockSpec(dims, lambda i: (0,) * len(dims))


def feed(x, dy, att, gains, order, order_t, weights):
    return pl.pallas_call(
        feed_kernel,
        grid=(4,),
        in_specs=[
            whole(256, 768), whole(256, 768), whole(8, 192, 128), whole(8, 768),
            whole(768, 768), whole(768, 768),
            pl.BlockSpec((16, 48, 768), lambda k: (0, k, 0)),
            pl.BlockSpec((16, 48, 768), lambda k: (0, 4 + k, 0)),
            pl.BlockSpec((16, 48, 768), lambda k: (0, 8, 0)),
        ],
        out_specs=[
            whole(256, 768), whole(256, 768), whole(8, 192, 128), whole(8, 768),
            pl.BlockSpec(memory_space=pl.ANY),
        ],
        out_shape=[
            shape((256, 768), BF), shape((256, 768), F32), shape((8, 192, 128), BF),
            shape((8, 768), F32), shape((16, 432, 768), BF),
        ],
        scratch_shapes=[
            pltpu.VMEM((256, 768), F32), pltpu.VMEM((256, 1), F32),
            pltpu.VMEM((256, 768), BF), pltpu.VMEM((768, 256), BF), pltpu.VMEM((256, 768), F32),
            pltpu.VMEM((256, 768), F32), pltpu.VMEM((768, 256), BF),
            pltpu.VMEM((4, 16, 48, 768), BF), pltpu.VMEM((4, 16, 48, 768), BF),
            pltpu.VMEM((16, 48, 768), BF), pltpu.SemaphoreType.DMA((9,)),
        ],
        cost_estimate=about(18),
        compiler_params=pltpu.CompilerParams(vmem_limit_bytes=VMEM_LIMIT),
    )(x, dy, att, gains, order, order_t, weights, weights, weights)


def unproject_kernel(
    info_ref, own_ref, dq_ref, dkv_ref, partner_ref, normed_ref, wt_ref, dgain_ref, order_ref,
    part_ref, mine_ref, theirs_ref, dt_scr, dw_scr, p_scr,
):
    dt_scr[0:192, :] = dq_ref[...]
    dt_scr[192:576, :] = (dkv_ref[...] + partner_ref[...].astype(F32)).astype(BF)
    dw_scr[0:576, :] = dot(dt_scr[...], normed_ref[...])
    bias_sum = jnp.zeros((1, 768), F32)
    gain_sum = jnp.zeros((1, 768), F32)
    for j in range(8):
        d_normed = dot(dt_scr[:, j * 128 : (j + 1) * 128].T, wt_ref[...])
        part_ref[j] = d_normed.astype(BF)
        hat, _ = normalize(own_ref[j].astype(F32))
        gain_sum += jnp.sum(d_normed * hat, axis=0, keepdims=True)
        bias_sum += jnp.sum(d_normed, axis=0, keepdims=True)
    dw_scr[576:577, :] = gain_sum
    dw_scr[577:578, :] = bias_sum
    dw_scr[578:580, :] = dgain_ref[0:2, :]
    dw_scr[580:640, :] = jnp.zeros((60, 768), F32)
    p_scr[...] = dot(order_ref[...], dw_scr[...].astype(BF), NT).astype(BF)
    for dc, ref in enumerate((mine_ref, theirs_ref)):
        for dx in range(4):
            for dz in range(2):
                ref[dx, dz] = p_scr[rows_at(info_ref, dc, dz, dx), :]


def slots_kernel(rest_ref, qkv_ref, order_ref, out_ref, r_scr):
    r_scr[0:432, :] = rest_ref[...]
    r_scr[432:480, 0:640] = qkv_ref[...]
    r_scr[432:480, 640:768] = jnp.zeros((48, 128), BF)
    out_ref[...] = dot(order_ref[...], r_scr[...], TN).astype(BF).reshape(8, 64, 768)


def finish_kernel(x_ref, dfirst_ref, gains_ref, got_ref, dtok_ref):
    gain = gains_ref[0:1]
    for b in range(2):
        rows = slice(b * 128, (b + 1) * 128)
        dn = jnp.zeros((128, 768), F32)
        for e in range(4):
            dn += got_ref[4 * b + e].astype(F32)
        hat, scale = normalize(x_ref[rows, :].astype(F32))
        t = dn * gain
        part = t - jnp.mean(t, -1, keepdims=True) - hat * jnp.mean(t * hat, -1, keepdims=True)
        dtok_ref[rows, :] = (dfirst_ref[rows, :] + part * scale).astype(BF)


def sums_kernel(got_ref, units_ref, down_ref, out_ref, up_ref, qkv_ref, g1_ref, b1_ref, g2_ref, b2_ref):
    total = jnp.zeros((64, 768), F32)
    chunks = []
    for e in range(4):
        both = got_ref[e].astype(F32) + got_ref[4 + e].astype(F32)
        chunks.append(both[54:60])
        total += both
    down_ref[...] = total[0:24]
    out_ref[...] = total[24:30]
    left, up = total[30:54], jnp.zeros((24, 768), F32)
    for _ in range(3):
        piece = left.astype(BF)
        left = left - piece.astype(F32)
        up += dot(piece, units_ref[...])
    for k in range(4):
        up_ref[:, k * 768 : (k + 1) * 768] = up[k * 6 : k * 6 + 6]
    for s in range(3):
        qkv_ref[:, s * 768 : (s + 1) * 768] = jnp.concatenate(
            [chunks[e][:, s * 192 : (s + 1) * 192] for e in range(4)], axis=1
        )
    norms = total[:, 512:640].T
    for i, ref in enumerate((g1_ref, b1_ref, g2_ref, b2_ref)):
        ref[...] = norms[64 + i : 65 + i, 54:60]


def scalars(count):
    return dict(
        in_specs=[pl.BlockSpec(memory_space=pltpu.SMEM)]
        + [pl.BlockSpec(memory_space=pltpu.VMEM)] * (count - 1)
    )


def body(tokens, lengths, gain_one, bias_one, w_qkv, w_out, gain_two, bias_two, w_up, w_down, d_out):
    place = lax.axis_index("seq")
    core = lax.rem(place, 2)
    length = lengths[place // 8]
    row = lax.axis_index("batch")
    info = jnp.stack([length, core, row // 4, lax.rem(row, 4)]).astype(jnp.int32)
    order = jnp.asarray(ROW_ORDER, BF)
    order_t = jnp.asarray(ROW_ORDER.T, BF)
    qkv_order = jnp.asarray(QKV_ORDER, BF)
    regroup = jnp.asarray(REGROUP, BF)
    exchange = functools.partial(
        lax.all_to_all, axis_name="seq", split_axis=0, concat_axis=0, tiled=True,
        axis_index_groups=SAME_CORE,
    )

    norms = jnp.stack([gain_one, bias_one, gain_two, bias_two], axis=1)
    norms = jnp.pad(norms, ((0, 0), (0, 124)))
    units = jnp.asarray(UNIT_ORDER, BF)
    slots = call(
        pack_kernel,
        shape((8, 64, 768), BF),
        (w_down, w_out, w_up, w_qkv, norms, units),
        2,
        [pltpu.VMEM((64, 768), F32)],
    )
    slots = exchange(slots)
    rest, qkv_rows = call(
        regroup_kernel,
        [shape((432, 768), BF), shape((48, 640), BF)],
        (slots, regroup),
        2,
    )
    weights = lax.all_gather(rest, BOTH, axis=0, axis_index_groups=RINGS)
    near = jnp.stack(
        [qkv_rows] + [lax.ppermute(qkv_rows, "batch", along_x(step)) for step in (-1, 2, 1)]
    )
    far = lax.ppermute(near, "batch", SWAP_Z)
    near_other = lax.ppermute(near, "seq", SWAP_CORE)
    far_other = lax.ppermute(far, "seq", SWAP_CORE)
    x = tokens.transpose(1, 0, 2)
    dy = d_out.transpose(1, 0, 2).reshape(256, 768)
    own = exchange(jnp.broadcast_to(x[:, None], (2, 4, 128, 768)).reshape(8, 128, 768))
    x = x.reshape(256, 768)

    normed, wt, gains, qkv_t = call(
        project_kernel,
        [shape((1024, 768), BF), shape((576, 768), BF), shape((8, 768), F32), shape((576, 1024), BF)],
        (info, own, near, far, near_other, far_other, qkv_order),
        5,
        [pltpu.VMEM((768, 640), BF), pltpu.VMEM((640, 768), F32)],
        **scalars(7),
    )
    q_t, kv = qkv_t[:192], qkv_t[192:]
    kv_other = lax.ppermute(kv, "seq", SWAP_CORE)
    o, o_low, lse = call(
        forward_kernel,
        [shape((192, 1024), F32), shape((8, 192, 128), BF), shape((3, 1024), F32)],
        (info, q_t, kv, kv_other),
        13,
        [pltpu.VMEM((3, 2048, 64), BF), pltpu.VMEM((192, 2048), BF)],
        **scalars(4),
    )
    att = exchange(o_low)
    y, d_first, d_att, d_gain, grads = feed(x, dy, att, gains, order, order_t, weights)

    rest_sum = lax.psum_scatter(
        grads.reshape(16 * 432, 768), BOTH, scatter_dimension=0, tiled=True,
        axis_index_groups=RINGS,
    )
    d_att = exchange(d_att)
    dq, dkv, dkv_other = call(
        backward_kernel,
        [shape((192, 1024), BF), shape((384, 1024), F32), shape((384, 1024), BF)],
        (info, q_t, kv, kv_other, o, lse, d_att),
        17,
        [
            pltpu.VMEM((3, 2048, 64), BF),
            pltpu.VMEM((192, 2048), BF),
            pltpu.VMEM((3, 2048, 64), BF),
            pltpu.VMEM((3, 2048, 64), F32),
            pltpu.VMEM((3, 2048, 64), F32),
        ],
        **scalars(7),
    )
    partner = lax.ppermute(dkv_other, "seq", SWAP_CORE)
    part, mine, theirs = call(
        unproject_kernel,
        [shape((8, 128, 768), BF), shape((4, 2, 48, 640), BF), shape((4, 2, 48, 640), BF)],
        (info, own, dq, dkv, partner, normed, wt, d_gain, qkv_order),
        7,
        [pltpu.VMEM((576, 1024), BF), pltpu.VMEM((640, 768), F32), pltpu.VMEM((768, 640), BF)],
        **scalars(9),
    )
    add = lambda *parts: sum(p.astype(F32) for p in parts).astype(BF)
    line = add(mine, lax.ppermute(theirs, "seq", SWAP_CORE))
    line = add(
        line[0],
        lax.ppermute(line[1], "batch", along_x(1)),
        lax.ppermute(line[2], "batch", along_x(2)),
        lax.ppermute(line[3], "batch", along_x(-1)),
    )
    qkv_sum = add(line[0], lax.ppermute(line[1], "batch", SWAP_Z))
    back = exchange(part)
    d_tokens = call(finish_kernel, shape((256, 768), BF), (x, d_first, gains, back), 3)
    slots = call(
        slots_kernel,
        shape((8, 64, 768), BF),
        (rest_sum, qkv_sum, regroup),
        2,
        [pltpu.VMEM((480, 768), BF)],
    )
    slots = exchange(slots)
    vector = shape((1, 6), F32)
    d_down, d_out_w, d_up, d_qkv, *norms = call(
        sums_kernel,
        [shape((24, 768), F32), shape((6, 768), F32), shape((6, 3072), F32), shape((6, 2304), F32)]
        + [vector] * 4,
        (slots, units),
        2,
    )
    norms = [v.reshape(6) for v in norms]
    output = y.reshape(2, 128, 768).transpose(1, 0, 2)
    d_tokens = d_tokens.reshape(2, 128, 768).transpose(1, 0, 2)
    return (
        output, d_tokens, norms[0], norms[1], d_qkv, d_out_w, norms[2], norms[3], d_up, d_down,
    )


def solution(mesh):
    rows = P(("seq", "batch"))
    tokens = P("seq", "batch", None)
    return jax.shard_map(
        body,
        mesh=mesh,
        in_specs=(tokens, P("batch"), rows, rows, rows, rows, rows, rows, rows, rows, tokens),
        out_specs=(tokens, tokens, rows, rows, rows, rows, rows, rows, rows, rows),
        check_vma=False,
    )
```

```python
import functools
import math

import jax
import jax.numpy as jnp
import numpy as np
from jax import lax
from jax.experimental import pallas as pl
from jax.experimental.pallas import tpu as pltpu
from jax.sharding import PartitionSpec as P

H = 12
HD = 64
EPSILON = 1e-05
BF = jnp.bfloat16
F32 = jnp.float32
BOTH = ("seq", "batch")
SAME_CORE = [[2 * k + c for k in range(8)] for c in range(2)]
SWAP_CORE = [(i, i ^ 1) for i in range(16)]
TURNS = [(0, 0), (0, 1), (0, 2), (0, 3), (1, 3), (1, 2), (1, 1), (1, 0)]
RING = [(c, z, x) for z, x in TURNS for c in range(2)]


RINGS = [
    [((y * 2 + (low ^ z)) * 2 + c) * 8 + z * 4 + x for c, z, x in RING]
    for y in range(4)
    for low in range(2)
]
SWAP_Z = [(b, b ^ 4) for b in range(8)]


def along_x(step):
    return [(b, b // 4 * 4 + (b + step) % 4) for b in range(8)]


def in_order(outer, size):
    natural = np.arange(outer * 16 * size, dtype=np.int32).reshape(outer, 2, 8, size)
    return np.stack([natural[:, c, z * 4 + x] for c, z, x in RING]).reshape(1, -1)


QKV_ORDER = (
    np.arange(768, dtype=np.int32).reshape(8, 2, 8, 6).transpose(1, 2, 0, 3).reshape(1, 768)
)
ROW_ORDER = in_order(8, 6)
UNIT_ORDER = in_order(2, 24)


def regroup_order():
    slot = np.arange(512, dtype=np.int32).reshape(8, 64)
    parts = [slot[:, 0:24]] + [slot[:, f : f + 6] for f in (30, 36, 42, 48, 24, 54)]
    return np.concatenate([p.reshape(-1) for p in parts] + [np.full(32, -1, np.int32)])[None]


REGROUP = regroup_order()


def places(order_ref):
    order = order_ref[...]
    size = order.shape[1]
    rows = lax.broadcasted_iota(jnp.int32, (size, size), 0)
    return jnp.where(rows == order, 1.0, 0.0).astype(BF)


NT = (((1,), (1,)), ((), ()))
NN = (((1,), (0,)), ((), ()))
TN = (((0,), (0,)), ((), ()))


def dot(left, right, dims=NN):
    return lax.dot_general(left, right, dims, preferred_element_type=F32)


def about(us):
    return pl.CostEstimate(flops=int(us * 1.1e9), bytes_accessed=0, transcendentals=0)


PARAMS = pltpu.CompilerParams(vmem_limit_bytes=60 * 1024 * 1024)


def call(kernel, outs, ins, us, scratch=(), **kwargs):
    return pl.pallas_call(
        kernel,
        out_shape=outs,
        scratch_shapes=list(scratch),
        cost_estimate=about(us),
        compiler_params=PARAMS,
        **kwargs,
    )(*ins)


def shape(dims, dtype):
    return jax.ShapeDtypeStruct(dims, dtype)


def normalize(values):
    center = jnp.mean(values, axis=-1, keepdims=True)
    shifted = values - center
    spread = jnp.mean(shifted * shifted, axis=-1, keepdims=True)
    scale = lax.rsqrt(spread + EPSILON)
    return shifted * scale, scale


def pack_kernel(
    down_ref, out_ref, up_ref, qkv_ref, g1_ref, b1_ref, g2_ref, b2_ref, units_ref,
    slot_ref, scr, turn_scr,
):
    turn_scr[...] = jnp.zeros_like(turn_scr)
    for i, ref in enumerate((g1_ref, b1_ref, g2_ref, b2_ref)):
        turn_scr[64 + i : 65 + i, 0:6] = ref[...].astype(F32)
    norms = turn_scr[...].T[0:6, 64:128].astype(BF)
    up = jnp.concatenate(
        [up_ref[:, k * 768 : (k + 1) * 768].astype(F32) for k in range(4)], axis=0
    ).astype(BF)
    scr[0:24, :] = down_ref[...].astype(F32)
    scr[24:30, :] = out_ref[...].astype(F32)
    scr[30:54, :] = dot(up, places(units_ref))
    scr[60:64, :] = jnp.zeros((4, 768), F32)
    for e in range(4):
        parts = [qkv_ref[:, s * 768 + e * 192 : s * 768 + (e + 1) * 192] for s in range(3)]
        row = jnp.concatenate(parts + [norms, jnp.zeros((6, 128), BF)], axis=1)
        scr[54:60, :] = row.astype(F32)
        slot = scr[...].astype(BF)
        slot_ref[e] = slot
        slot_ref[4 + e] = slot


def regroup_kernel(slots_ref, order_ref, rest_ref, qkv_ref):
    rows = dot(places(order_ref), slots_ref[...].reshape(512, 768), TN).astype(BF)
    rest_ref[...] = rows[0:432]
    qkv_ref[...] = rows[432:480, 0:640]


def core_of():
    return lax.rem(lax.axis_index("seq"), 2)


def length_of(lengths_ref):
    return jnp.where(lax.axis_index("seq") < 8, lengths_ref[0], lengths_ref[1])


def rows_at(dc, dz, dx):
    row = lax.axis_index("batch")
    c = lax.rem(core_of() + dc, 2)
    z = lax.rem(row // 4 + dz, 2)
    x = lax.rem(row + dx, 4)
    return pl.ds(pl.multiple_of((c * 8 + z * 4 + x) * 48, 48), 48)


def project_kernel(
    own_ref, near_ref, far_ref, near_other_ref, far_other_ref, order_ref,
    normed_ref, wt_ref, gains_ref, q_ref, kv_ref, w_scr, t_scr,
):
    for i, ref in enumerate((near_ref, far_ref, near_other_ref, far_other_ref)):
        for dx in range(4):
            w_scr[rows_at(i // 2, i % 2, dx), :] = ref[dx]
    t_scr[...] = dot(w_scr[...].T, places(order_ref), NT)
    wt_ref[...] = t_scr[0:576].astype(BF)
    gains = t_scr[576:584]
    gains_ref[...] = gains
    gain, bias = gains[0:1], gains[1:2]
    for j in range(8):
        hat, _ = normalize(own_ref[j].astype(F32))
        normed_ref[j * 128 : (j + 1) * 128, :] = (hat * gain + bias).astype(BF)
    for j in range(4):
        lanes = slice(j * 256, (j + 1) * 256)
        qkv = dot(wt_ref[...], normed_ref[lanes, :], NT).astype(BF)
        q_ref[:, lanes] = qkv[0:192]
        kv_ref[:, lanes] = qkv[192:576]


def last_keys(m, core, length):
    lane = lax.broadcasted_iota(jnp.int32, (1, 256), 1)
    query = m * 512 + 128 * core + jnp.where(lane < 128, lane, lane + 128)
    return jnp.minimum(query, length - 1)


def allowed(start, first, last, core):
    offset = start + first + (128 * core if first < 128 else -128 * core)
    return lax.broadcasted_iota(jnp.int32, (64, 256), 0) <= last - offset


def fill_keys(own_ref, other_ref, k_scr, base):
    for u in range(3):
        for j in range(8):
            rows, lanes = pl.ds(base + u * 64, 64), pl.ds(j * 128, 128)
            k_scr[u, j * 256 : j * 256 + 128, :] = own_ref[rows, lanes].T
            k_scr[u, j * 256 + 128 : j * 256 + 256, :] = other_ref[rows, lanes].T


def fill_lanes(own_ref, other_ref, scr, base):
    for j in range(8):
        scr[:, j * 256 : j * 256 + 128] = own_ref[base : base + 192, j * 128 : j * 128 + 128]
        scr[:, j * 256 + 128 : j * 256 + 256] = other_ref[
            base : base + 192, j * 128 : j * 128 + 128
        ]


PAIRS = [(h, u) for h in range(2) for u in range(3)]
CHUNKS = [slice(i * 64, i * 64 + 64) for i in range(4)]


def steps(m, length):
    return jnp.minimum(m + 1, (length + 511) // 512)


def sweep(length, begin, score, step, finish):
    def one(_, place):
        m, jk = place
        more = jk + 1 < steps(m, length)
        next_m = jnp.where(more, m, jnp.minimum(m + 1, 3))
        next_jk = jnp.where(more, jk + 1, 0)

        @pl.when(jk == 0)
        def _():
            begin()

        edge = (jk == m) | (jk * 512 + 512 > length)

        @pl.when(edge)
        def _():
            step(m, jk, next_m, next_jk, True)

        @pl.when(jnp.logical_not(edge))
        def _():
            step(m, jk, next_m, next_jk, False)

        @pl.when(jnp.logical_not(more))
        def _():
            finish(m)

        return jnp.where(more, m, m + 1), next_jk

    for h, u in PAIRS:
        score(h, u, 0, 0)
    total = sum(steps(m, length) for m in range(4))
    lax.fori_loop(0, total, one, (jnp.int32(0), jnp.int32(0)))


def group(m):
    return pl.ds(pl.multiple_of(m * 256, 256), 256)


def key_tile(jk, h):
    return pl.ds(pl.multiple_of(jk * 512, 512) + h * 256, 256)


def forward_plain(q_scr, k_scr, v_scr, scratch, length, core, finish):
    s_scr, w_scr, acc_scr, sum_scr = scratch[0:6], scratch[6:12], scratch[12:15], scratch[15:18]

    def begin():
        for u in range(3):
            acc_scr[u][...] = jnp.zeros((64, 256), F32)
            sum_scr[u][...] = jnp.zeros((8, 256), F32)

    def score(h, u, m, jk):
        queries = q_scr[u * 64 : (u + 1) * 64, group(m)]
        s_scr[h * 3 + u][...] = dot(k_scr[u, key_tile(jk, h), :], queries)

    def step(m, jk, next_m, next_jk, masked):
        last = last_keys(m, core, length)
        for h, u in PAIRS:
            scores, weights = s_scr[h * 3 + u], w_scr[h * 3 + u]
            total = sum_scr[u][...]
            for rows in CHUNKS:
                s = scores[rows, :]
                t = s * s + 1.0
                r = lax.rsqrt(t)
                e = jnp.exp(t * r)
                if masked:
                    e = jnp.where(allowed(jk * 512 + h * 256, rows.start, last, core), e, 0.0)
                total = total + jnp.sum(e.reshape(8, 8, 256), axis=0)
                weights[rows, :] = (s * r * e).astype(BF)
            sum_scr[u][...] = total
            score(h, u, next_m, next_jk)
            acc_scr[u][...] += dot(v_scr[u * 64 : (u + 1) * 64, key_tile(jk, h)], weights[...])

    def close(m):
        for u in range(3):
            total = jnp.sum(sum_scr[u][...], axis=0, keepdims=True)
            finish(m, u, acc_scr[u][...], total, jnp.zeros((1, 256), F32))

    sweep(length, begin, score, step, close)


def forward_any(q_scr, k_scr, v_scr, length, core, finish):
    def one(m, _):
        last = last_keys(m, core, length)

        def step(jk, carry):
            start = pl.multiple_of(jk * 256, 256)
            mask = jnp.concatenate([allowed(start, r.start, last, core) for r in CHUNKS], axis=0)
            out = []
            for u in range(3):
                top, total, accum = carry[u]
                s = dot(k_scr[u, pl.ds(start, 256), :], q_scr[u * 64 : (u + 1) * 64, group(m)])
                t = s * s + 1.0
                r = lax.rsqrt(t)
                a = jnp.where(mask, t * r, -1e30)
                fresh = jnp.maximum(top, jnp.max(a, axis=0, keepdims=True))
                e = jnp.exp(a - fresh)
                rescale = jnp.exp(top - fresh)
                total = total * rescale + jnp.sum(e, axis=0, keepdims=True)
                accum = accum * rescale + dot(
                    v_scr[u * 64 : (u + 1) * 64, pl.ds(start, 256)], (s * r * e).astype(BF)
                )
                out.append((fresh, total, accum))
            return tuple(out)

        zero = (jnp.zeros((1, 256), F32), jnp.zeros((1, 256), F32), jnp.zeros((64, 256), F32))
        carry = lax.fori_loop(0, 2 * steps(m, length), step, (zero,) * 3)
        for u in range(3):
            finish(m, u, carry[u][2], carry[u][1], carry[u][0])
        return 0

    lax.fori_loop(0, 4, one, 0)


def forward_kernel(
    lengths_ref, q_ref, own_ref, other_ref, o_ref, low_ref, lse_ref, q_scr, k_scr, v_scr, *scratch
):
    length, core = length_of(lengths_ref), core_of()
    fill_keys(own_ref, other_ref, k_scr, 0)
    fill_lanes(own_ref, other_ref, v_scr, 192)
    q_scr[...] = q_ref[...] * BF(0.125)

    def finish(m, u, accum, total, top):
        lanes = group(m)
        o = accum / total
        o_ref[u * 64 : (u + 1) * 64, lanes] = o
        for half in range(2):
            low_ref[2 * m + half, u * 64 : (u + 1) * 64, :] = o[
                :, half * 128 : half * 128 + 128
            ].astype(BF)
        lse_ref[u : u + 1, lanes] = top + jnp.log(total)

    def largest(ref):
        values = ref[0:192, :].astype(F32)
        return jnp.max(jnp.sum((values * values).reshape(3, 64, 1024), axis=1))

    bound = largest(q_ref) * jnp.maximum(largest(own_ref), largest(other_ref)) * (1.0 / 64.0)
    small = bound < 3600.0

    @pl.when(small)
    def _():
        forward_plain(q_scr, k_scr, v_scr, scratch, length, core, finish)

    @pl.when(jnp.logical_not(small))
    def _():
        forward_any(q_scr, k_scr, v_scr, length, core, finish)


def backward_kernel(
    lengths_ref, q_ref, own_ref, other_ref, o_ref, lse_ref, da_ref,
    dq_ref, down_ref, dother_ref,
    q_scr, k_scr, kt_scr, v_scr, da_scr, dk_scr, dv_scr, delta_scr, *scratch,
):
    s_scr, dp_scr, w_scr, ds_scr, dq_scr = (scratch[i : i + 6] for i in (0, 6, 12, 18, 24))
    length, core = length_of(lengths_ref), core_of()
    fill_keys(own_ref, other_ref, k_scr, 0)
    fill_lanes(own_ref, other_ref, kt_scr, 0)
    fill_keys(own_ref, other_ref, v_scr, 192)
    q_scr[...] = q_ref[...] * BF(0.125)
    for j in range(8):
        lanes = slice(j * 128, (j + 1) * 128)
        da_scr[:, lanes] = da_ref[j]
        for u in range(3):
            rows = slice(u * 64, (u + 1) * 64)
            delta_scr[u : u + 1, lanes] = jnp.sum(
                da_ref[j, rows, :].astype(F32) * o_ref[rows, lanes], axis=0, keepdims=True
            )
    dk_scr[...] = jnp.zeros_like(dk_scr)
    dv_scr[...] = jnp.zeros_like(dv_scr)

    def begin():
        for u in range(3):
            dq_scr[u][...] = jnp.zeros((64, 256), F32)

    def score(h, u, m, jk):
        rows, tile = slice(u * 64, (u + 1) * 64), key_tile(jk, h)
        s_scr[h * 3 + u][...] = dot(k_scr[u, tile, :], q_scr[rows, group(m)])
        dp_scr[h * 3 + u][...] = dot(v_scr[u, tile, :], da_scr[rows, group(m)])

    def step(m, jk, next_m, next_jk, masked):
        last = last_keys(m, core, length)
        for h, u in PAIRS:
            tile = key_tile(jk, h)
            heads = slice(u * 64, (u + 1) * 64)
            delta, lse = delta_scr[u : u + 1, group(m)], lse_ref[u : u + 1, group(m)]
            place = h * 3 + u
            for rows in CHUNKS:
                s = s_scr[place][rows, :]
                t = s * s + 1.0
                r = lax.rsqrt(t)
                p = jnp.exp(t * r - lse)
                if masked:
                    p = jnp.where(allowed(jk * 512 + h * 256, rows.start, last, core), p, 0.0)
                g = s * r
                w_scr[place][rows, :] = (g * p).astype(BF)
                ds = p * (dp_scr[place][rows, :] * (r * r * (r - 1.0) + 1.0) - g * delta)
                ds_scr[place][rows, :] = ds.astype(BF)
            score(h, u, next_m, next_jk)
            dv_scr[u, :, tile] += dot(da_scr[heads, group(m)], w_scr[place][...], NT)
            dk_scr[u, :, tile] += dot(q_scr[heads, group(m)], ds_scr[place][...], NT)
            dq_scr[u][...] += dot(kt_scr[heads, tile], ds_scr[place][...])

    def close(m):
        for u in range(3):
            dq_ref[u * 64 : (u + 1) * 64, group(m)] = (dq_scr[u][...] * 0.125).astype(BF)

    sweep(length, begin, score, step, close)
    for scr, base in ((dk_scr, 0), (dv_scr, 192)):
        for u in range(3):
            rows = pl.ds(base + u * 64, 64)
            for j in range(8):
                lanes = pl.ds(j * 128, 128)
                down_ref[rows, lanes] = scr[u, :, j * 256 : j * 256 + 128].astype(BF)
                dother_ref[rows, lanes] = scr[u, :, j * 256 + 128 : j * 256 + 256].astype(BF)


GELU_SCALE = math.sqrt(2.0 / math.pi)


def prepare_kernel(att_ref, order_ref, place_ref, attended_ref, attended_t_ref):
    place_ref[...] = places(order_ref)
    natural = [att_ref[b * 4 : b * 4 + 4].reshape(768, 128).T for b in range(2)]
    attended = dot(jnp.concatenate(natural, axis=0), place_ref[...]).astype(BF)
    attended_ref[...] = attended
    attended_t_ref[...] = attended.T


def feed_kernel(
    x_hbm, dy_hbm, att_hbm, att_t_hbm, gains_hbm, place_hbm, weights_hbm,
    y_hbm, dfirst_hbm, datt_hbm, dgain_hbm, grads_hbm,
    x_ref, dy_ref, att_ref, att_t_ref, gains_ref, place_ref, down_ref, up_ref, out_ref,
    y_ref, dfirst_ref, datt_ref, dgain_ref, gdown, gup, gout, acc_scr, dn_scr, loads, stores,
):
    def block(ref, number):
        return ref.at[:, pl.ds(48 * number, 48), :]

    arrivals = [(att_hbm, att_ref), (block(weights_hbm, 8), out_ref), (x_hbm, x_ref)]
    arrivals += [(gains_hbm, gains_ref), (place_hbm, place_ref)]
    for k in range(4):
        arrivals.append((block(weights_hbm, 4 + k), up_ref.at[k]))
        if k == 0:
            arrivals.append((dy_hbm, dy_ref))
        arrivals.append((block(weights_hbm, k), down_ref.at[k]))
    arrivals.append((att_t_hbm, att_t_ref))
    arrivals = [pltpu.make_async_copy(*pair, loads.at[i]) for i, pair in enumerate(arrivals)]
    for copy in arrivals:
        copy.start()
    departures = []

    def send(source, target):
        copy = pltpu.make_async_copy(source, target, stores.at[len(departures)])
        copy.start()
        departures.append(copy)

    for copy in arrivals[0:4]:
        copy.wait()
    gain, bias = gains_ref[2:3], gains_ref[3:4]
    w_out = out_ref[...].reshape(768, 768)
    first = x_ref[...].astype(F32) + dot(att_ref[...], w_out)
    hat, scale = normalize(first)
    acc_scr[...] = first
    arrivals[4].wait()
    n2 = dot((hat * gain + bias).astype(BF), place_ref[...]).astype(BF)
    n2t = n2.T
    waiting = arrivals[5:]
    for k in range(4):
        waiting.pop(0).wait()
        up = up_ref[k].reshape(768, 768)
        hidden = dot(n2, up)
        if k == 0:
            waiting.pop(0).wait()
        waiting.pop(0).wait()
        down = down_ref[k].reshape(768, 768)
        dy = dy_ref[...]
        d_active = dot(dy, down, NT)
        square = hidden * hidden
        tanh = jnp.tanh(GELU_SCALE * hidden * (1.0 + 0.044715 * square))
        share = 0.5 + 0.5 * tanh
        active = (hidden * share).astype(BF)
        slope = share + 0.5 * hidden * (1.0 - tanh * tanh) * (
            GELU_SCALE * (1.0 + (3 * 0.044715) * square)
        )
        d_hidden = (slope * d_active).astype(BF)
        gdown[k] = dot(active.T, dy).astype(BF).reshape(16, 48, 768)
        send(gdown.at[k], block(grads_hbm, k))
        gup[k] = dot(n2t, d_hidden).astype(BF).reshape(16, 48, 768)
        send(gup.at[k], block(grads_hbm, 4 + k))
        acc_scr[...] += dot(active, down)
        if k == 0:
            dn_scr[...] = dot(d_hidden, up, NT)
        else:
            dn_scr[...] += dot(d_hidden, up, NT)
    y_ref[...] = acc_scr[...].astype(BF)
    send(y_ref, y_hbm)
    dn = dot(dn_scr[...].astype(BF), place_ref[...], NT)
    t = dn * gain
    part = t - jnp.mean(t, -1, keepdims=True) - hat * jnp.mean(t * hat, -1, keepdims=True)
    d_first = dy_ref[...].astype(F32) + part * scale
    low = d_first.astype(BF)
    waiting.pop(0).wait()
    gout[...] = dot(att_t_ref[...], low).astype(BF).reshape(16, 48, 768)
    send(gout, block(grads_hbm, 8))
    d_att = dot(w_out, low, NT).astype(BF)
    d_att = dot(place_ref[...], d_att).astype(BF)
    for b in range(2):
        datt_ref[b * 4 : b * 4 + 4] = d_att[:, b * 128 : (b + 1) * 128].reshape(4, 192, 128)
    send(datt_ref, datt_hbm)
    dfirst_ref[...] = d_first
    send(dfirst_ref, dfirst_hbm)
    dgain_ref[0:1, :] = jnp.sum(dn * hat, axis=0, keepdims=True)
    dgain_ref[1:2, :] = jnp.sum(dn, axis=0, keepdims=True)
    dgain_ref[2:8, :] = jnp.zeros((6, 768), F32)
    send(dgain_ref, dgain_hbm)
    for copy in departures:
        copy.wait()


def whole(*dims):
    return pl.BlockSpec(dims, lambda *_: (0,) * len(dims))


def feed(*arrays):
    outs = [
        shape((256, 768), BF), shape((256, 768), F32), shape((8, 192, 128), BF),
        shape((8, 768), F32), shape((16, 432, 768), BF),
    ]
    blocks = pltpu.VMEM((4, 16, 48, 768), BF)
    held = [pltpu.VMEM(a.shape, a.dtype) for a in arrays[:-1]]
    held += [blocks, blocks, pltpu.VMEM((16, 48, 768), BF)]
    held += [pltpu.VMEM(o.shape, o.dtype) for o in outs[:-1]]
    held += [blocks, blocks, pltpu.VMEM((16, 48, 768), BF)]
    held += [pltpu.VMEM((256, 768), F32)] * 2
    held += [pltpu.SemaphoreType.DMA((15,)), pltpu.SemaphoreType.DMA((13,))]
    return call(
        feed_kernel,
        outs,
        arrays,
        17,
        held,
        in_specs=[pl.BlockSpec(memory_space=pl.ANY)] * len(arrays),
        out_specs=[pl.BlockSpec(memory_space=pl.ANY)] * len(outs),
    )


def unproject_kernel(
    own_ref, dq_ref, dkv_ref, partner_ref, normed_ref, wt_ref, dgain_ref, order_ref,
    part_ref, mine_ref, theirs_ref, dt_scr, dw_scr, p_scr,
):
    dt_scr[0:192, :] = dq_ref[...]
    dt_scr[192:576, :] = (dkv_ref[...].astype(F32) + partner_ref[...].astype(F32)).astype(BF)
    bias_sum = jnp.zeros((1, 768), F32)
    gain_sum = jnp.zeros((1, 768), F32)
    for j in range(4):
        d_normed = dot(dt_scr[:, j * 256 : (j + 1) * 256].T, wt_ref[...])
        part_ref[2 * j : 2 * j + 2] = d_normed.astype(BF).reshape(2, 128, 768)
        hat, _ = normalize(own_ref[2 * j : 2 * j + 2].reshape(256, 768).astype(F32))
        gain_sum += jnp.sum(d_normed * hat, axis=0, keepdims=True)
        bias_sum += jnp.sum(d_normed, axis=0, keepdims=True)
    dw_scr[0:576, :] = dot(dt_scr[...], normed_ref[...])
    dw_scr[576:577, :] = gain_sum
    dw_scr[577:578, :] = bias_sum
    dw_scr[578:580, :] = dgain_ref[0:2, :]
    dw_scr[580:640, :] = jnp.zeros((60, 768), F32)
    p_scr[...] = dot(dw_scr[...].astype(BF), places(order_ref)).T.astype(BF)
    for dc, ref in enumerate((mine_ref, theirs_ref)):
        for dx in range(4):
            for dz in range(2):
                ref[dx, dz] = p_scr[rows_at(dc, dz, dx), :]


def slots_kernel(rest_ref, qkv_ref, order_ref, out_ref, r_scr):
    r_scr[0:432, :] = rest_ref[...]
    r_scr[432:480, 0:640] = qkv_ref[...]
    r_scr[432:480, 640:768] = jnp.zeros((48, 128), BF)
    r_scr[480:512, :] = jnp.zeros((32, 768), BF)
    out_ref[...] = dot(places(order_ref), r_scr[...]).astype(BF).reshape(8, 64, 768)


def finish_kernel(x_ref, dfirst_ref, gains_ref, got_ref, dtok_ref):
    gain = gains_ref[0:1]
    for b in range(2):
        rows = slice(b * 128, (b + 1) * 128)
        dn = jnp.zeros((128, 768), F32)
        for e in range(4):
            dn += got_ref[4 * b + e].astype(F32)
        hat, scale = normalize(x_ref[rows, :].astype(F32))
        t = dn * gain
        part = t - jnp.mean(t, -1, keepdims=True) - hat * jnp.mean(t * hat, -1, keepdims=True)
        dtok_ref[rows, :] = (dfirst_ref[rows, :] + part * scale).astype(BF)


def sums_kernel(got_ref, units_ref, down_ref, out_ref, up_ref, qkv_ref, g1_ref, b1_ref, g2_ref, b2_ref):
    total = jnp.zeros((64, 768), F32)
    chunks = []
    for e in range(4):
        both = got_ref[e].astype(F32) + got_ref[4 + e].astype(F32)
        chunks.append(both[54:60])
        total += both
    down_ref[...] = total[0:24]
    out_ref[...] = total[24:30]
    left, up, units = total[30:54], jnp.zeros((24, 768), F32), places(units_ref)
    for _ in range(3):
        piece = left.astype(BF)
        left = left - piece.astype(F32)
        up += dot(piece, units, NT)
    for k in range(4):
        up_ref[:, k * 768 : (k + 1) * 768] = up[k * 6 : k * 6 + 6]
    for s in range(3):
        qkv_ref[:, s * 768 : (s + 1) * 768] = jnp.concatenate(
            [chunks[e][:, s * 192 : (s + 1) * 192] for e in range(4)], axis=1
        )
    norms = total[:, 512:640].T
    for i, ref in enumerate((g1_ref, b1_ref, g2_ref, b2_ref)):
        ref[...] = norms[64 + i : 65 + i, 54:60]


def scalars(count):
    return dict(
        in_specs=[pl.BlockSpec(memory_space=pltpu.SMEM)]
        + [pl.BlockSpec(memory_space=pltpu.VMEM)] * (count - 1)
    )


def body(tokens, lengths, gain_one, bias_one, w_qkv, w_out, gain_two, bias_two, w_up, w_down, d_out):
    order, units, regroup, qkv_order = (
        jnp.asarray(v) for v in (ROW_ORDER, UNIT_ORDER, REGROUP, QKV_ORDER)
    )
    exchange = functools.partial(
        lax.all_to_all, axis_name="seq", split_axis=0, concat_axis=0, tiled=True,
        axis_index_groups=SAME_CORE,
    )

    vectors = [v.reshape(1, 6) for v in (gain_one, bias_one, gain_two, bias_two)]
    slots = pl.pallas_call(
        pack_kernel,
        grid=(1,),
        in_specs=[whole(24, 768), whole(6, 768), whole(6, 3072), whole(6, 2304)]
        + [whole(1, 6)] * 4
        + [whole(1, 768)],
        out_specs=whole(8, 64, 768),
        out_shape=shape((8, 64, 768), BF),
        scratch_shapes=[pltpu.VMEM((64, 768), F32), pltpu.VMEM((128, 128), F32)],
        cost_estimate=about(2),
        compiler_params=PARAMS,
    )(w_down, w_out, w_up, w_qkv, *vectors, units)
    slots = exchange(slots)
    rest, qkv_rows = call(
        regroup_kernel,
        [shape((432, 768), BF), shape((48, 640), BF)],
        (slots, regroup),
        2,
    )
    weights = lax.all_gather(rest, BOTH, axis=0, axis_index_groups=RINGS)
    near = jnp.stack(
        [qkv_rows] + [lax.ppermute(qkv_rows, "batch", along_x(step)) for step in (-1, 2, 1)]
    )
    far = lax.ppermute(near, "batch", SWAP_Z)
    near_other = lax.ppermute(near, "seq", SWAP_CORE)
    far_other = lax.ppermute(far, "seq", SWAP_CORE)
    x = tokens.transpose(1, 0, 2)
    dy = d_out.transpose(1, 0, 2).reshape(256, 768)
    own = exchange(jnp.broadcast_to(x[:, None], (2, 4, 128, 768)).reshape(8, 128, 768))
    x = x.reshape(256, 768)

    normed, wt, gains, q_t, kv = call(
        project_kernel,
        [
            shape((1024, 768), BF), shape((576, 768), BF), shape((8, 768), F32),
            shape((192, 1024), BF), shape((384, 1024), BF),
        ],
        (own, near, far, near_other, far_other, qkv_order),
        5,
        [pltpu.VMEM((768, 640), BF), pltpu.VMEM((640, 768), F32)],
    )
    kv_other = lax.ppermute(kv, "seq", SWAP_CORE)
    o, o_low, lse = call(
        forward_kernel,
        [shape((192, 1024), F32), shape((8, 192, 128), BF), shape((3, 1024), F32)],
        (lengths, q_t, kv, kv_other),
        12,
        [
            pltpu.VMEM((192, 1024), BF), pltpu.VMEM((3, 2048, 64), BF),
            pltpu.VMEM((192, 2048), BF),
        ]
        + [pltpu.VMEM((256, 256), F32)] * 6
        + [pltpu.VMEM((256, 256), BF)] * 6
        + [pltpu.VMEM((64, 256), F32)] * 3
        + [pltpu.VMEM((8, 256), F32)] * 3,
        **scalars(4),
    )
    att = exchange(o_low)
    place, attended, attended_t = call(
        prepare_kernel,
        [shape((768, 768), BF), shape((256, 768), BF), shape((768, 256), BF)],
        (att, order),
        2,
    )
    y, d_first, d_att, d_gain, grads = feed(x, dy, attended, attended_t, gains, place, weights)

    rest_sum = lax.psum_scatter(
        grads.reshape(16 * 432, 768), BOTH, scatter_dimension=0, tiled=True,
        axis_index_groups=RINGS,
    )
    d_att = exchange(d_att)
    dq, dkv, dkv_other = call(
        backward_kernel,
        [shape((192, 1024), BF), shape((384, 1024), BF), shape((384, 1024), BF)],
        (lengths, q_t, kv, kv_other, o, lse, d_att),
        20,
        [
            pltpu.VMEM((192, 1024), BF),
            pltpu.VMEM((3, 2048, 64), BF),
            pltpu.VMEM((192, 2048), BF),
            pltpu.VMEM((3, 2048, 64), BF),
            pltpu.VMEM((192, 1024), BF),
            pltpu.VMEM((3, 64, 2048), F32),
            pltpu.VMEM((3, 64, 2048), F32),
            pltpu.VMEM((3, 1024), F32),
        ]
        + [pltpu.VMEM((256, 256), F32)] * 12
        + [pltpu.VMEM((256, 256), BF)] * 12
        + [pltpu.VMEM((64, 256), F32)] * 3,
        **scalars(7),
    )
    partner = lax.ppermute(dkv_other, "seq", SWAP_CORE)
    part, mine, theirs = call(
        unproject_kernel,
        [shape((8, 128, 768), BF), shape((4, 2, 48, 640), BF), shape((4, 2, 48, 640), BF)],
        (own, dq, dkv, partner, normed, wt, d_gain, qkv_order),
        7,
        [pltpu.VMEM((576, 1024), BF), pltpu.VMEM((640, 768), F32), pltpu.VMEM((768, 640), BF)],
    )
    add = lambda *parts: sum(p.astype(F32) for p in parts).astype(BF)
    line = add(mine, lax.ppermute(theirs, "seq", SWAP_CORE))
    line = add(
        line[0],
        lax.ppermute(line[1], "batch", along_x(1)),
        lax.ppermute(line[2], "batch", along_x(2)),
        lax.ppermute(line[3], "batch", along_x(-1)),
    )
    qkv_sum = add(line[0], lax.ppermute(line[1], "batch", SWAP_Z))
    back = exchange(part)
    d_tokens = call(finish_kernel, shape((256, 768), BF), (x, d_first, gains, back), 3)
    slots = call(
        slots_kernel,
        shape((8, 64, 768), BF),
        (rest_sum, qkv_sum, regroup),
        2,
        [pltpu.VMEM((512, 768), BF)],
    )
    slots = exchange(slots)
    vector = shape((1, 6), F32)
    d_down, d_out_w, d_up, d_qkv, *norms = call(
        sums_kernel,
        [shape((24, 768), F32), shape((6, 768), F32), shape((6, 3072), F32), shape((6, 2304), F32)]
        + [vector] * 4,
        (slots, units),
        2,
    )
    norms = [v.reshape(6) for v in norms]
    output = y.reshape(2, 128, 768).transpose(1, 0, 2)
    d_tokens = d_tokens.reshape(2, 128, 768).transpose(1, 0, 2)
    return (
        output, d_tokens, norms[0], norms[1], d_qkv, d_out_w, norms[2], norms[3], d_up, d_down,
    )


def solution(mesh):
    rows = P(("seq", "batch"))
    tokens = P("seq", "batch", None)
    return jax.shard_map(
        body,
        mesh=mesh,
        in_specs=(tokens, P("batch"), rows, rows, rows, rows, rows, rows, rows, rows, tokens),
        out_specs=(tokens, tokens, rows, rows, rows, rows, rows, rows, rows, rows),
        check_vma=False,
    )
```

```python
import functools
import math

import jax
import jax.numpy as jnp
import numpy as np
from jax import lax
from jax.experimental import pallas as pl
from jax.experimental.pallas import tpu as pltpu
from jax.sharding import PartitionSpec as P

H = 12
HD = 64
EPSILON = 1e-05
BF = jnp.bfloat16
F32 = jnp.float32
BOTH = ("seq", "batch")
SAME_CORE = [[2 * k + c for k in range(8)] for c in range(2)]
SWAP_CORE = [(i, i ^ 1) for i in range(16)]
TURNS = [(0, 0), (0, 1), (0, 2), (0, 3), (1, 3), (1, 2), (1, 1), (1, 0)]
RING = [(c, z, x) for z, x in TURNS for c in range(2)]


RINGS = [
    [((y * 2 + (low ^ z)) * 2 + c) * 8 + z * 4 + x for c, z, x in RING]
    for y in range(4)
    for low in range(2)
]
SWAP_Z = [(b, b ^ 4) for b in range(8)]


def along_x(step):
    return [(b, b // 4 * 4 + (b + step) % 4) for b in range(8)]


def in_order(outer, size):
    natural = np.arange(outer * 16 * size, dtype=np.int32).reshape(outer, 2, 8, size)
    return np.stack([natural[:, c, z * 4 + x] for c, z, x in RING]).reshape(1, -1)


QKV_ORDER = (
    np.arange(768, dtype=np.int32).reshape(8, 2, 8, 6).transpose(1, 2, 0, 3).reshape(1, 768)
)
ROW_ORDER = in_order(8, 6)
UNIT_ORDER = in_order(2, 24)


def regroup_order():
    slot = np.arange(512, dtype=np.int32).reshape(8, 64)
    parts = [slot[:, 0:24]] + [slot[:, f : f + 6] for f in (30, 36, 42, 48, 24, 54)]
    return np.concatenate([p.reshape(-1) for p in parts] + [np.full(32, -1, np.int32)])[None]


REGROUP = regroup_order()


def places(order_ref):
    order = order_ref[...]
    size = order.shape[1]
    rows = lax.broadcasted_iota(jnp.int32, (size, size), 0)
    return jnp.where(rows == order, 1.0, 0.0).astype(BF)


NT = (((1,), (1,)), ((), ()))
NN = (((1,), (0,)), ((), ()))
TN = (((0,), (0,)), ((), ()))


def dot(left, right, dims=NN):
    return lax.dot_general(left, right, dims, preferred_element_type=F32)


def about(us):
    return pl.CostEstimate(flops=int(us * 1.1e9), bytes_accessed=0, transcendentals=0)


def call(kernel, outs, ins, us, scratch=(), mib=60, **kwargs):
    return pl.pallas_call(
        kernel,
        out_shape=outs,
        scratch_shapes=list(scratch),
        cost_estimate=about(us),
        compiler_params=pltpu.CompilerParams(vmem_limit_bytes=mib * 1024 * 1024),
        **kwargs,
    )(*ins)


def shape(dims, dtype):
    return jax.ShapeDtypeStruct(dims, dtype)


def normalize(values):
    center = jnp.mean(values, axis=-1, keepdims=True)
    shifted = values - center
    spread = jnp.mean(shifted * shifted, axis=-1, keepdims=True)
    scale = lax.rsqrt(spread + EPSILON)
    return shifted * scale, scale


def pack_kernel(
    down_ref, out_ref, up_ref, qkv_ref, g1_ref, b1_ref, g2_ref, b2_ref, units_ref,
    slot_ref, scr, turn_scr,
):
    turn_scr[...] = jnp.zeros_like(turn_scr)
    for i, ref in enumerate((g1_ref, b1_ref, g2_ref, b2_ref)):
        turn_scr[64 + i : 65 + i, 0:6] = ref[...].astype(F32)
    norms = turn_scr[...].T[0:6, 64:128].astype(BF)
    up = jnp.concatenate(
        [up_ref[:, k * 768 : (k + 1) * 768].astype(F32) for k in range(4)], axis=0
    ).astype(BF)
    scr[0:24, :] = down_ref[...].astype(F32)
    scr[24:30, :] = out_ref[...].astype(F32)
    scr[30:54, :] = dot(up, places(units_ref))
    scr[60:64, :] = jnp.zeros((4, 768), F32)
    for e in range(4):
        parts = [qkv_ref[:, s * 768 + e * 192 : s * 768 + (e + 1) * 192] for s in range(3)]
        row = jnp.concatenate(parts + [norms, jnp.zeros((6, 128), BF)], axis=1)
        scr[54:60, :] = row.astype(F32)
        slot = scr[...].astype(BF)
        slot_ref[e] = slot
        slot_ref[4 + e] = slot


def regroup_kernel(slots_ref, order_ref, rest_ref, qkv_ref):
    rows = dot(places(order_ref), slots_ref[...].reshape(512, 768), TN).astype(BF)
    rest_ref[...] = rows[0:432]
    qkv_ref[...] = rows[432:480, 0:640]


def core_of():
    return lax.rem(lax.axis_index("seq"), 2)


def length_of(lengths_ref):
    return jnp.where(lax.axis_index("seq") < 8, lengths_ref[0], lengths_ref[1])


def rows_at(dc, dz, dx):
    row = lax.axis_index("batch")
    c = lax.rem(core_of() + dc, 2)
    z = lax.rem(row // 4 + dz, 2)
    x = lax.rem(row + dx, 4)
    return pl.ds(pl.multiple_of((c * 8 + z * 4 + x) * 48, 48), 48)


def project_kernel(
    own_ref, near_ref, far_ref, near_other_ref, far_other_ref, order_ref,
    normed_ref, wt_ref, gains_ref, q_ref, kv_ref, w_scr, t_scr,
):
    for i, ref in enumerate((near_ref, far_ref, near_other_ref, far_other_ref)):
        for dx in range(4):
            w_scr[rows_at(i // 2, i % 2, dx), :] = ref[dx]
    t_scr[...] = dot(w_scr[...].T, places(order_ref), NT)
    wt_ref[...] = t_scr[0:576].astype(BF)
    gains = t_scr[576:584]
    gains_ref[...] = gains
    gain, bias = gains[0:1], gains[1:2]
    for j in range(8):
        hat, _ = normalize(own_ref[j].astype(F32))
        normed_ref[j * 128 : (j + 1) * 128, :] = (hat * gain + bias).astype(BF)
    for j in range(4):
        lanes = slice(j * 256, (j + 1) * 256)
        qkv = dot(wt_ref[...], normed_ref[lanes, :], NT).astype(BF)
        q_ref[:, lanes] = qkv[0:192]
        kv_ref[:, lanes] = qkv[192:576]


def last_keys(m, core, length):
    lane = lax.broadcasted_iota(jnp.int32, (1, 256), 1)
    query = m * 512 + 128 * core + jnp.where(lane < 128, lane, lane + 128)
    return jnp.minimum(query, length - 1)


def allowed(start, first, last, core):
    offset = start + first + (128 * core if first < 128 else -128 * core)
    return lax.broadcasted_iota(jnp.int32, (64, 256), 0) <= last - offset


def fill_keys(own_ref, other_ref, k_scr, base):
    for u in range(3):
        for j in range(8):
            rows, lanes = pl.ds(base + u * 64, 64), pl.ds(j * 128, 128)
            k_scr[u, j * 256 : j * 256 + 128, :] = own_ref[rows, lanes].T
            k_scr[u, j * 256 + 128 : j * 256 + 256, :] = other_ref[rows, lanes].T


def fill_lanes(own_ref, other_ref, scr, base):
    for j in range(8):
        scr[:, j * 256 : j * 256 + 128] = own_ref[base : base + 192, j * 128 : j * 128 + 128]
        scr[:, j * 256 + 128 : j * 256 + 256] = other_ref[
            base : base + 192, j * 128 : j * 128 + 128
        ]


PAIRS = [(h, u) for h in range(2) for u in range(3)]
CHUNKS = [slice(i * 64, i * 64 + 64) for i in range(4)]


def steps(m, length):
    return jnp.minimum(m + 1, (length + 511) // 512)


def sweep(length, begin, score, step, finish):
    def one(_, place):
        m, jk = place
        more = jk + 1 < steps(m, length)
        next_m = jnp.where(more, m, jnp.minimum(m + 1, 3))
        next_jk = jnp.where(more, jk + 1, 0)

        @pl.when(jk == 0)
        def _():
            begin()

        edge = (jk == m) | (jk * 512 + 512 > length)

        @pl.when(edge)
        def _():
            step(m, jk, next_m, next_jk, True)

        @pl.when(jnp.logical_not(edge))
        def _():
            step(m, jk, next_m, next_jk, False)

        @pl.when(jnp.logical_not(more))
        def _():
            finish(m)

        return jnp.where(more, m, m + 1), next_jk

    for h, u in PAIRS:
        score(h, u, 0, 0)
    total = sum(steps(m, length) for m in range(4))
    lax.fori_loop(0, total, one, (jnp.int32(0), jnp.int32(0)))


def group(m):
    return pl.ds(pl.multiple_of(m * 256, 256), 256)


def key_tile(jk, h):
    return pl.ds(pl.multiple_of(jk * 512, 512) + h * 256, 256)


def forward_plain(q_scr, k_scr, v_scr, scratch, length, core, finish):
    s_scr, w_scr, acc_scr, sum_scr = scratch[0:6], scratch[6:12], scratch[12:15], scratch[15:18]

    def begin():
        for u in range(3):
            acc_scr[u][...] = jnp.zeros((64, 256), F32)
            sum_scr[u][...] = jnp.zeros((8, 256), F32)

    def score(h, u, m, jk):
        queries = q_scr[u * 64 : (u + 1) * 64, group(m)]
        s_scr[h * 3 + u][...] = dot(k_scr[u, key_tile(jk, h), :], queries)

    def step(m, jk, next_m, next_jk, masked):
        last = last_keys(m, core, length)
        for h, u in PAIRS:
            scores, weights = s_scr[h * 3 + u], w_scr[h * 3 + u]
            total = sum_scr[u][...]
            for rows in CHUNKS:
                s = scores[rows, :]
                t = s * s + 1.0
                r = lax.rsqrt(t)
                e = jnp.exp(t * r)
                if masked:
                    e = jnp.where(allowed(jk * 512 + h * 256, rows.start, last, core), e, 0.0)
                total = total + jnp.sum(e.reshape(8, 8, 256), axis=0)
                weights[rows, :] = (s * r * e).astype(BF)
            sum_scr[u][...] = total
            score(h, u, next_m, next_jk)
            acc_scr[u][...] += dot(v_scr[u * 64 : (u + 1) * 64, key_tile(jk, h)], weights[...])

    def close(m):
        for u in range(3):
            total = jnp.sum(sum_scr[u][...], axis=0, keepdims=True)
            finish(m, u, acc_scr[u][...], total, jnp.zeros((1, 256), F32))

    sweep(length, begin, score, step, close)


def forward_any(q_scr, k_scr, v_scr, length, core, finish):
    def one(m, _):
        last = last_keys(m, core, length)

        def step(jk, carry):
            start = pl.multiple_of(jk * 256, 256)
            mask = jnp.concatenate([allowed(start, r.start, last, core) for r in CHUNKS], axis=0)
            out = []
            for u in range(3):
                top, total, accum = carry[u]
                s = dot(k_scr[u, pl.ds(start, 256), :], q_scr[u * 64 : (u + 1) * 64, group(m)])
                t = s * s + 1.0
                r = lax.rsqrt(t)
                a = jnp.where(mask, t * r, -1e30)
                fresh = jnp.maximum(top, jnp.max(a, axis=0, keepdims=True))
                e = jnp.exp(a - fresh)
                rescale = jnp.exp(top - fresh)
                total = total * rescale + jnp.sum(e, axis=0, keepdims=True)
                accum = accum * rescale + dot(
                    v_scr[u * 64 : (u + 1) * 64, pl.ds(start, 256)], (s * r * e).astype(BF)
                )
                out.append((fresh, total, accum))
            return tuple(out)

        zero = (jnp.zeros((1, 256), F32), jnp.zeros((1, 256), F32), jnp.zeros((64, 256), F32))
        carry = lax.fori_loop(0, 2 * steps(m, length), step, (zero,) * 3)
        for u in range(3):
            finish(m, u, carry[u][2], carry[u][1], carry[u][0])
        return 0

    lax.fori_loop(0, 4, one, 0)


def forward_kernel(
    lengths_ref, q_ref, own_ref, other_ref, o_ref, low_ref, lse_ref, q_scr, k_scr, v_scr, *scratch
):
    length, core = length_of(lengths_ref), core_of()
    fill_keys(own_ref, other_ref, k_scr, 0)
    fill_lanes(own_ref, other_ref, v_scr, 192)
    q_scr[...] = q_ref[...] * BF(0.125)

    def finish(m, u, accum, total, top):
        lanes = group(m)
        o = accum / total
        o_ref[u * 64 : (u + 1) * 64, lanes] = o
        for half in range(2):
            low_ref[2 * m + half, u * 64 : (u + 1) * 64, :] = o[
                :, half * 128 : half * 128 + 128
            ].astype(BF)
        lse_ref[u : u + 1, lanes] = top + jnp.log(total)

    def largest(ref):
        values = ref[0:192, :].astype(F32)
        return jnp.max(jnp.sum((values * values).reshape(3, 64, 1024), axis=1))

    bound = largest(q_ref) * jnp.maximum(largest(own_ref), largest(other_ref)) * (1.0 / 64.0)
    small = bound < 3600.0

    @pl.when(small)
    def _():
        forward_plain(q_scr, k_scr, v_scr, scratch, length, core, finish)

    @pl.when(jnp.logical_not(small))
    def _():
        forward_any(q_scr, k_scr, v_scr, length, core, finish)


def backward_kernel(
    lengths_ref, q_ref, own_ref, other_ref, o_ref, lse_ref, da_ref,
    dq_ref, down_ref, dother_ref,
    q_scr, k_scr, kt_scr, v_scr, da_scr, dk_scr, dv_scr, delta_scr, *scratch,
):
    s_scr, dp_scr, w_scr, ds_scr, dq_scr = (scratch[i : i + 6] for i in (0, 6, 12, 18, 24))
    length, core = length_of(lengths_ref), core_of()
    fill_keys(own_ref, other_ref, k_scr, 0)
    fill_lanes(own_ref, other_ref, kt_scr, 0)
    fill_keys(own_ref, other_ref, v_scr, 192)
    q_scr[...] = q_ref[...] * BF(0.125)
    for j in range(8):
        lanes = slice(j * 128, (j + 1) * 128)
        da_scr[:, lanes] = da_ref[j]
        for u in range(3):
            rows = slice(u * 64, (u + 1) * 64)
            delta_scr[u : u + 1, lanes] = jnp.sum(
                da_ref[j, rows, :].astype(F32) * o_ref[rows, lanes], axis=0, keepdims=True
            )
    dk_scr[...] = jnp.zeros_like(dk_scr)
    dv_scr[...] = jnp.zeros_like(dv_scr)

    def begin():
        for u in range(3):
            dq_scr[u][...] = jnp.zeros((64, 256), F32)

    def score(h, u, m, jk):
        rows, tile = slice(u * 64, (u + 1) * 64), key_tile(jk, h)
        s_scr[h * 3 + u][...] = dot(k_scr[u, tile, :], q_scr[rows, group(m)])
        dp_scr[h * 3 + u][...] = dot(v_scr[u, tile, :], da_scr[rows, group(m)])

    def step(m, jk, next_m, next_jk, masked):
        last = last_keys(m, core, length)
        for h, u in PAIRS:
            tile = key_tile(jk, h)
            heads = slice(u * 64, (u + 1) * 64)
            delta, lse = delta_scr[u : u + 1, group(m)], lse_ref[u : u + 1, group(m)]
            place = h * 3 + u
            for rows in CHUNKS:
                s = s_scr[place][rows, :]
                t = s * s + 1.0
                r = lax.rsqrt(t)
                p = jnp.exp(t * r - lse)
                if masked:
                    p = jnp.where(allowed(jk * 512 + h * 256, rows.start, last, core), p, 0.0)
                g = s * r
                w_scr[place][rows, :] = (g * p).astype(BF)
                ds = p * (dp_scr[place][rows, :] * (r * r * (r - 1.0) + 1.0) - g * delta)
                ds_scr[place][rows, :] = ds.astype(BF)
            score(h, u, next_m, next_jk)
            dv_scr[u, :, tile] += dot(da_scr[heads, group(m)], w_scr[place][...], NT)
            dk_scr[u, :, tile] += dot(q_scr[heads, group(m)], ds_scr[place][...], NT)
            dq_scr[u][...] += dot(kt_scr[heads, tile], ds_scr[place][...])

    def close(m):
        for u in range(3):
            dq_ref[u * 64 : (u + 1) * 64, group(m)] = (dq_scr[u][...] * 0.125).astype(BF)

    sweep(length, begin, score, step, close)
    for scr, base in ((dk_scr, 0), (dv_scr, 192)):
        for u in range(3):
            rows = pl.ds(base + u * 64, 64)
            for j in range(8):
                lanes = pl.ds(j * 128, 128)
                down_ref[rows, lanes] = scr[u, :, j * 256 : j * 256 + 128].astype(BF)
                dother_ref[rows, lanes] = scr[u, :, j * 256 + 128 : j * 256 + 256].astype(BF)


GELU_SCALE = math.sqrt(2.0 / math.pi)


def prepare_kernel(att_ref, order_ref, place_ref, attended_ref, attended_t_ref):
    place_ref[...] = places(order_ref)
    natural = [att_ref[b * 4 : b * 4 + 4].reshape(768, 128).T for b in range(2)]
    attended = dot(jnp.concatenate(natural, axis=0), place_ref[...]).astype(BF)
    attended_ref[...] = attended
    attended_t_ref[...] = attended.T


def feed_kernel(
    x_hbm, dy_hbm, att_hbm, att_t_hbm, gains_hbm, place_hbm, weights_hbm,
    y_hbm, dfirst_hbm, datt_hbm, dgain_hbm, grads_hbm,
    x_ref, dy_ref, att_ref, att_t_ref, gains_ref, place_ref, down_ref, up_ref, out_ref,
    y_ref, dfirst_ref, datt_ref, dgain_ref, gdown, gup, gout, acc_scr, dn_scr, loads, stores,
):
    def block(ref, number):
        return ref.at[:, pl.ds(48 * number, 48), :]

    arrivals = [(att_hbm, att_ref), (block(weights_hbm, 8), out_ref), (x_hbm, x_ref)]
    arrivals += [(gains_hbm, gains_ref), (place_hbm, place_ref)]
    for k in range(4):
        arrivals.append((block(weights_hbm, 4 + k), up_ref.at[k]))
        if k == 0:
            arrivals.append((dy_hbm, dy_ref))
        arrivals.append((block(weights_hbm, k), down_ref.at[k]))
    arrivals.append((att_t_hbm, att_t_ref))
    arrivals = [pltpu.make_async_copy(*pair, loads.at[i]) for i, pair in enumerate(arrivals)]
    for copy in arrivals:
        copy.start()
    departures = []

    def send(source, target):
        copy = pltpu.make_async_copy(source, target, stores.at[len(departures)])
        copy.start()
        departures.append(copy)

    for copy in arrivals[0:4]:
        copy.wait()
    gain, bias = gains_ref[2:3], gains_ref[3:4]
    w_out = out_ref[...].reshape(768, 768)
    first = x_ref[...].astype(F32) + dot(att_ref[...], w_out)
    hat, scale = normalize(first)
    acc_scr[...] = first
    arrivals[4].wait()
    n2 = dot((hat * gain + bias).astype(BF), place_ref[...]).astype(BF)
    n2t = n2.T
    waiting = arrivals[5:]
    for k in range(4):
        waiting.pop(0).wait()
        up = up_ref[k].reshape(768, 768)
        hidden = dot(n2, up)
        if k == 0:
            waiting.pop(0).wait()
        waiting.pop(0).wait()
        down = down_ref[k].reshape(768, 768)
        dy = dy_ref[...]
        d_active = dot(dy, down, NT)
        square = hidden * hidden
        tanh = jnp.tanh(GELU_SCALE * hidden * (1.0 + 0.044715 * square))
        share = 0.5 + 0.5 * tanh
        active = (hidden * share).astype(BF)
        slope = share + 0.5 * hidden * (1.0 - tanh * tanh) * (
            GELU_SCALE * (1.0 + (3 * 0.044715) * square)
        )
        d_hidden = (slope * d_active).astype(BF)
        gdown[k] = dot(active.T, dy).astype(BF).reshape(16, 48, 768)
        send(gdown.at[k], block(grads_hbm, k))
        gup[k] = dot(n2t, d_hidden).astype(BF).reshape(16, 48, 768)
        send(gup.at[k], block(grads_hbm, 4 + k))
        acc_scr[...] += dot(active, down)
        if k == 0:
            dn_scr[...] = dot(d_hidden, up, NT)
        else:
            dn_scr[...] += dot(d_hidden, up, NT)
    y_ref[...] = acc_scr[...].astype(BF)
    send(y_ref, y_hbm)
    dn = dot(dn_scr[...].astype(BF), place_ref[...], NT)
    t = dn * gain
    part = t - jnp.mean(t, -1, keepdims=True) - hat * jnp.mean(t * hat, -1, keepdims=True)
    d_first = dy_ref[...].astype(F32) + part * scale
    low = d_first.astype(BF)
    waiting.pop(0).wait()
    gout[...] = dot(att_t_ref[...], low).astype(BF).reshape(16, 48, 768)
    send(gout, block(grads_hbm, 8))
    d_att = dot(w_out, low, NT).astype(BF)
    d_att = dot(place_ref[...], d_att).astype(BF)
    for b in range(2):
        datt_ref[b * 4 : b * 4 + 4] = d_att[:, b * 128 : (b + 1) * 128].reshape(4, 192, 128)
    send(datt_ref, datt_hbm)
    dfirst_ref[...] = d_first
    send(dfirst_ref, dfirst_hbm)
    dgain_ref[0:1, :] = jnp.sum(dn * hat, axis=0, keepdims=True)
    dgain_ref[1:2, :] = jnp.sum(dn, axis=0, keepdims=True)
    dgain_ref[2:8, :] = jnp.zeros((6, 768), F32)
    send(dgain_ref, dgain_hbm)
    for copy in departures:
        copy.wait()


def whole(*dims):
    return pl.BlockSpec(dims, lambda *_: (0,) * len(dims))


def feed(*arrays):
    outs = [
        shape((256, 768), BF), shape((256, 768), F32), shape((8, 192, 128), BF),
        shape((8, 768), F32), shape((16, 432, 768), BF),
    ]
    blocks = pltpu.VMEM((4, 16, 48, 768), BF)
    held = [pltpu.VMEM(a.shape, a.dtype) for a in arrays[:-1]]
    held += [blocks, blocks, pltpu.VMEM((16, 48, 768), BF)]
    held += [pltpu.VMEM(o.shape, o.dtype) for o in outs[:-1]]
    held += [blocks, blocks, pltpu.VMEM((16, 48, 768), BF)]
    held += [pltpu.VMEM((256, 768), F32)] * 2
    held += [pltpu.SemaphoreType.DMA((15,)), pltpu.SemaphoreType.DMA((13,))]
    return call(
        feed_kernel,
        outs,
        arrays,
        17,
        held,
        in_specs=[pl.BlockSpec(memory_space=pl.ANY)] * len(arrays),
        out_specs=[pl.BlockSpec(memory_space=pl.ANY)] * len(outs),
    )


def unproject_kernel(
    own_ref, dq_ref, dkv_ref, partner_ref, normed_ref, wt_ref, dgain_ref, order_ref,
    part_ref, mine_ref, theirs_ref, dt_scr, dw_scr, p_scr,
):
    dt_scr[0:192, :] = dq_ref[...]
    dt_scr[192:576, :] = (dkv_ref[...].astype(F32) + partner_ref[...].astype(F32)).astype(BF)
    bias_sum = jnp.zeros((1, 768), F32)
    gain_sum = jnp.zeros((1, 768), F32)
    for j in range(4):
        d_normed = dot(dt_scr[:, j * 256 : (j + 1) * 256].T, wt_ref[...])
        part_ref[2 * j : 2 * j + 2] = d_normed.astype(BF).reshape(2, 128, 768)
        hat, _ = normalize(own_ref[2 * j : 2 * j + 2].reshape(256, 768).astype(F32))
        gain_sum += jnp.sum(d_normed * hat, axis=0, keepdims=True)
        bias_sum += jnp.sum(d_normed, axis=0, keepdims=True)
    dw_scr[0:576, :] = dot(dt_scr[...], normed_ref[...])
    dw_scr[576:577, :] = gain_sum
    dw_scr[577:578, :] = bias_sum
    dw_scr[578:580, :] = dgain_ref[0:2, :]
    dw_scr[580:640, :] = jnp.zeros((60, 768), F32)
    p_scr[...] = dot(dw_scr[...].astype(BF), places(order_ref)).T.astype(BF)
    for dc, ref in enumerate((mine_ref, theirs_ref)):
        for dx in range(4):
            for dz in range(2):
                ref[dx, dz] = p_scr[rows_at(dc, dz, dx), :]


def slots_kernel(rest_ref, qkv_ref, order_ref, out_ref, r_scr):
    r_scr[0:432, :] = rest_ref[...]
    r_scr[432:480, 0:640] = qkv_ref[...]
    r_scr[432:480, 640:768] = jnp.zeros((48, 128), BF)
    r_scr[480:512, :] = jnp.zeros((32, 768), BF)
    out_ref[...] = dot(places(order_ref), r_scr[...]).astype(BF).reshape(8, 64, 768)


def finish_kernel(x_ref, dfirst_ref, gains_ref, got_ref, dtok_ref):
    gain = gains_ref[0:1]
    for b in range(2):
        rows = slice(b * 128, (b + 1) * 128)
        dn = jnp.zeros((128, 768), F32)
        for e in range(4):
            dn += got_ref[4 * b + e].astype(F32)
        hat, scale = normalize(x_ref[rows, :].astype(F32))
        t = dn * gain
        part = t - jnp.mean(t, -1, keepdims=True) - hat * jnp.mean(t * hat, -1, keepdims=True)
        dtok_ref[rows, :] = (dfirst_ref[rows, :] + part * scale).astype(BF)


def sums_kernel(got_ref, units_ref, down_ref, out_ref, up_ref, qkv_ref, g1_ref, b1_ref, g2_ref, b2_ref):
    total = jnp.zeros((64, 768), F32)
    chunks = []
    for e in range(4):
        both = got_ref[e].astype(F32) + got_ref[4 + e].astype(F32)
        chunks.append(both[54:60])
        total += both
    down_ref[...] = total[0:24]
    out_ref[...] = total[24:30]
    left, up, units = total[30:54], jnp.zeros((24, 768), F32), places(units_ref)
    for _ in range(3):
        piece = left.astype(BF)
        left = left - piece.astype(F32)
        up += dot(piece, units, NT)
    for k in range(4):
        up_ref[:, k * 768 : (k + 1) * 768] = up[k * 6 : k * 6 + 6]
    for s in range(3):
        qkv_ref[:, s * 768 : (s + 1) * 768] = jnp.concatenate(
            [chunks[e][:, s * 192 : (s + 1) * 192] for e in range(4)], axis=1
        )
    norms = total[:, 512:640].T
    for i, ref in enumerate((g1_ref, b1_ref, g2_ref, b2_ref)):
        ref[...] = norms[64 + i : 65 + i, 54:60]


def scalars(count):
    return dict(
        in_specs=[pl.BlockSpec(memory_space=pltpu.SMEM)]
        + [pl.BlockSpec(memory_space=pltpu.VMEM)] * (count - 1)
    )


def body(tokens, lengths, gain_one, bias_one, w_qkv, w_out, gain_two, bias_two, w_up, w_down, d_out):
    order, units, regroup, qkv_order = (
        jnp.asarray(v) for v in (ROW_ORDER, UNIT_ORDER, REGROUP, QKV_ORDER)
    )
    exchange = functools.partial(
        lax.all_to_all, axis_name="seq", split_axis=0, concat_axis=0, tiled=True,
        axis_index_groups=SAME_CORE,
    )

    vectors = [v.reshape(1, 6) for v in (gain_one, bias_one, gain_two, bias_two)]
    slots = pl.pallas_call(
        pack_kernel,
        grid=(1,),
        in_specs=[whole(24, 768), whole(6, 768), whole(6, 3072), whole(6, 2304)]
        + [whole(1, 6)] * 4
        + [whole(1, 768)],
        out_specs=whole(8, 64, 768),
        out_shape=shape((8, 64, 768), BF),
        scratch_shapes=[pltpu.VMEM((64, 768), F32), pltpu.VMEM((128, 128), F32)],
        cost_estimate=about(2),
        compiler_params=pltpu.CompilerParams(vmem_limit_bytes=60 * 1024 * 1024),
    )(w_down, w_out, w_up, w_qkv, *vectors, units)
    slots = exchange(slots)
    rest, qkv_rows = call(
        regroup_kernel,
        [shape((432, 768), BF), shape((48, 640), BF)],
        (slots, regroup),
        2,
        mib=12,
    )
    weights = lax.all_gather(rest, BOTH, axis=0, axis_index_groups=RINGS)
    near = jnp.stack(
        [qkv_rows] + [lax.ppermute(qkv_rows, "batch", along_x(step)) for step in (-1, 2, 1)]
    )
    far = lax.ppermute(near, "batch", SWAP_Z)
    near_other = lax.ppermute(near, "seq", SWAP_CORE)
    far_other = lax.ppermute(far, "seq", SWAP_CORE)
    x = tokens.transpose(1, 0, 2)
    dy = d_out.transpose(1, 0, 2).reshape(256, 768)
    own = exchange(jnp.broadcast_to(x[:, None], (2, 4, 128, 768)).reshape(8, 128, 768))
    x = x.reshape(256, 768)

    normed, wt, gains, q_t, kv = call(
        project_kernel,
        [
            shape((1024, 768), BF), shape((576, 768), BF), shape((8, 768), F32),
            shape((192, 1024), BF), shape((384, 1024), BF),
        ],
        (own, near, far, near_other, far_other, qkv_order),
        5,
        [pltpu.VMEM((768, 640), BF), pltpu.VMEM((640, 768), F32)],
        mib=30,
    )
    kv_other = lax.ppermute(kv, "seq", SWAP_CORE)
    o, o_low, lse = call(
        forward_kernel,
        [shape((192, 1024), F32), shape((8, 192, 128), BF), shape((3, 1024), F32)],
        (lengths, q_t, kv, kv_other),
        12,
        [
            pltpu.VMEM((192, 1024), BF), pltpu.VMEM((3, 2048, 64), BF),
            pltpu.VMEM((192, 2048), BF),
        ]
        + [pltpu.VMEM((256, 256), F32)] * 6
        + [pltpu.VMEM((256, 256), BF)] * 6
        + [pltpu.VMEM((64, 256), F32)] * 3
        + [pltpu.VMEM((8, 256), F32)] * 3,
        mib=30,
        **scalars(4),
    )
    att = exchange(o_low)
    place, attended, attended_t = call(
        prepare_kernel,
        [shape((768, 768), BF), shape((256, 768), BF), shape((768, 256), BF)],
        (att, order),
        2,
        mib=16,
    )
    y, d_first, d_att, d_gain, grads = feed(x, dy, attended, attended_t, gains, place, weights)

    rest_sum = lax.psum_scatter(
        grads.reshape(16 * 432, 768), BOTH, scatter_dimension=0, tiled=True,
        axis_index_groups=RINGS,
    )
    d_att = exchange(d_att)
    dq, dkv, dkv_other = call(
        backward_kernel,
        [shape((192, 1024), BF), shape((384, 1024), BF), shape((384, 1024), BF)],
        (lengths, q_t, kv, kv_other, o, lse, d_att),
        20,
        [
            pltpu.VMEM((192, 1024), BF),
            pltpu.VMEM((3, 2048, 64), BF),
            pltpu.VMEM((192, 2048), BF),
            pltpu.VMEM((3, 2048, 64), BF),
            pltpu.VMEM((192, 1024), BF),
            pltpu.VMEM((3, 64, 2048), F32),
            pltpu.VMEM((3, 64, 2048), F32),
            pltpu.VMEM((3, 1024), F32),
        ]
        + [pltpu.VMEM((256, 256), F32)] * 12
        + [pltpu.VMEM((256, 256), BF)] * 12
        + [pltpu.VMEM((64, 256), F32)] * 3,
        mib=36,
        **scalars(7),
    )
    partner = lax.ppermute(dkv_other, "seq", SWAP_CORE)
    part, mine, theirs = call(
        unproject_kernel,
        [shape((8, 128, 768), BF), shape((4, 2, 48, 640), BF), shape((4, 2, 48, 640), BF)],
        (own, dq, dkv, partner, normed, wt, d_gain, qkv_order),
        7,
        [pltpu.VMEM((576, 1024), BF), pltpu.VMEM((640, 768), F32), pltpu.VMEM((768, 640), BF)],
        mib=30,
    )
    add = lambda *parts: sum(p.astype(F32) for p in parts).astype(BF)
    line = add(mine, lax.ppermute(theirs, "seq", SWAP_CORE))
    line = add(
        line[0],
        lax.ppermute(line[1], "batch", along_x(1)),
        lax.ppermute(line[2], "batch", along_x(2)),
        lax.ppermute(line[3], "batch", along_x(-1)),
    )
    qkv_sum = add(line[0], lax.ppermute(line[1], "batch", SWAP_Z))
    back = exchange(part)
    d_tokens = call(finish_kernel, shape((256, 768), BF), (x, d_first, gains, back), 3, mib=16)
    slots = call(
        slots_kernel,
        shape((8, 64, 768), BF),
        (rest_sum, qkv_sum, regroup),
        2,
        [pltpu.VMEM((512, 768), BF)],
        mib=12,
    )
    slots = exchange(slots)
    vector = shape((1, 6), F32)
    d_down, d_out_w, d_up, d_qkv, *norms = call(
        sums_kernel,
        [shape((24, 768), F32), shape((6, 768), F32), shape((6, 3072), F32), shape((6, 2304), F32)]
        + [vector] * 4,
        (slots, units),
        2,
        mib=12,
    )
    norms = [v.reshape(6) for v in norms]
    output = y.reshape(2, 128, 768).transpose(1, 0, 2)
    d_tokens = d_tokens.reshape(2, 128, 768).transpose(1, 0, 2)
    return (
        output, d_tokens, norms[0], norms[1], d_qkv, d_out_w, norms[2], norms[3], d_up, d_down,
    )


def solution(mesh):
    rows = P(("seq", "batch"))
    tokens = P("seq", "batch", None)
    return jax.shard_map(
        body,
        mesh=mesh,
        in_specs=(tokens, P("batch"), rows, rows, rows, rows, rows, rows, rows, rows, tokens),
        out_specs=(tokens, tokens, rows, rows, rows, rows, rows, rows, rows, rows),
        check_vma=False,
    )
```

```python
import functools
import math

import jax
import jax.numpy as jnp
import numpy as np
from jax import lax
from jax.experimental import pallas as pl
from jax.experimental.pallas import tpu as pltpu
from jax.sharding import PartitionSpec as P

H = 12
HD = 64
EPSILON = 1e-05
BF = jnp.bfloat16
F32 = jnp.float32
BOTH = ("seq", "batch")
SAME_CORE = [[2 * k + c for k in range(8)] for c in range(2)]
SWAP_CORE = [(i, i ^ 1) for i in range(16)]
TURNS = [(0, 0), (0, 1), (0, 2), (0, 3), (1, 3), (1, 2), (1, 1), (1, 0)]
RING = [(c, z, x) for z, x in TURNS for c in range(2)]


RINGS = [
    [((y * 2 + (low ^ z)) * 2 + c) * 8 + z * 4 + x for c, z, x in RING]
    for y in range(4)
    for low in range(2)
]
SWAP_HALF = [(s * 8 + b, (s ^ 2) * 8 + (b ^ 4)) for s in range(16) for b in range(8)]


def along_x(step):
    return [(b, b // 4 * 4 + (b + step) % 4) for b in range(8)]


def in_order(outer, size):
    natural = np.arange(outer * 16 * size, dtype=np.int32).reshape(outer, 2, 8, size)
    return np.stack([natural[:, c, z * 4 + x] for c, z, x in RING]).reshape(1, -1)


QKV_ORDER = (
    np.arange(768, dtype=np.int32).reshape(8, 2, 8, 6).transpose(1, 2, 0, 3).reshape(1, 768)
)
ROW_ORDER = in_order(8, 6)
UNIT_ORDER = in_order(2, 24)


def regroup_order():
    slot = np.arange(512, dtype=np.int32).reshape(8, 64)
    parts = [slot[:, 0:24]] + [slot[:, f : f + 6] for f in (30, 36, 42, 48, 24, 54)]
    return np.concatenate([p.reshape(-1) for p in parts] + [np.full(32, -1, np.int32)])[None]


REGROUP = regroup_order()
SPREAD = np.concatenate(
    [np.arange(96, dtype=np.int32).reshape(16, 6), np.full((16, 2), -1, np.int32)], axis=1
).reshape(128, 1)


def places(order_ref):
    order = order_ref[...]
    size = order.shape[1]
    rows = lax.broadcasted_iota(jnp.int32, (size, size), 0)
    return jnp.where(rows == order, 1.0, 0.0).astype(BF)


NT = (((1,), (1,)), ((), ()))
NN = (((1,), (0,)), ((), ()))
TN = (((0,), (0,)), ((), ()))


def dot(left, right, dims=NN):
    return lax.dot_general(left, right, dims, preferred_element_type=F32)


def about(us):
    return pl.CostEstimate(flops=int(us * 1.1e9), bytes_accessed=0, transcendentals=0)


def call(kernel, outs, ins, us, scratch=(), mib=60, **kwargs):
    return pl.pallas_call(
        kernel,
        out_shape=outs,
        scratch_shapes=list(scratch),
        cost_estimate=about(us),
        compiler_params=pltpu.CompilerParams(vmem_limit_bytes=mib * 1024 * 1024),
        **kwargs,
    )(*ins)


def shape(dims, dtype):
    return jax.ShapeDtypeStruct(dims, dtype)


def normalize(values):
    center = jnp.mean(values, axis=-1, keepdims=True)
    shifted = values - center
    spread = jnp.mean(shifted * shifted, axis=-1, keepdims=True)
    scale = lax.rsqrt(spread + EPSILON)
    return shifted * scale, scale


def pack_kernel(
    down_ref, out_ref, up_ref, qkv_ref, g1_ref, b1_ref, g2_ref, b2_ref, units_ref,
    slot_ref, scr, turn_scr,
):
    turn_scr[...] = jnp.zeros_like(turn_scr)
    for i, ref in enumerate((g1_ref, b1_ref, g2_ref, b2_ref)):
        turn_scr[64 + i : 65 + i, 0:6] = ref[...].astype(F32)
    norms = turn_scr[...].T[0:6, 64:128].astype(BF)
    up = jnp.concatenate(
        [up_ref[:, k * 768 : (k + 1) * 768].astype(F32) for k in range(4)], axis=0
    ).astype(BF)
    scr[0:24, :] = down_ref[...].astype(F32)
    scr[24:30, :] = out_ref[...].astype(F32)
    scr[30:54, :] = dot(up, places(units_ref))
    scr[60:64, :] = jnp.zeros((4, 768), F32)
    for e in range(4):
        parts = [qkv_ref[:, s * 768 + e * 192 : s * 768 + (e + 1) * 192] for s in range(3)]
        row = jnp.concatenate(parts + [norms, jnp.zeros((6, 128), BF)], axis=1)
        scr[54:60, :] = row.astype(F32)
        slot = scr[...].astype(BF)
        slot_ref[2 * e] = slot
        slot_ref[2 * e + 1] = slot


def regroup_kernel(slots_ref, order_ref, rest_ref, qkv_ref):
    rows = dot(places(order_ref), slots_ref[...].reshape(512, 768), TN).astype(BF)
    rest_ref[...] = rows[0:432]
    qkv_ref[...] = rows[432:480, 0:640]


def core_of():
    return lax.rem(lax.axis_index("seq"), 2)


def length_of(lengths_ref):
    return jnp.where(lax.rem(lax.axis_index("seq") // 2, 2) == 0, lengths_ref[0], lengths_ref[1])


def rows_at(dc, dz, dx, size=48):
    row = lax.axis_index("batch")
    c = lax.rem(core_of() + dc, 2)
    z = lax.rem(row // 4 + dz, 2)
    x = lax.rem(row + dx, 4)
    return pl.ds(pl.multiple_of((c * 8 + z * 4 + x) * size, size), size)


def project_kernel(
    own_ref, near_ref, far_ref, near_other_ref, far_other_ref, order_ref,
    normed_ref, wt_ref, gains_ref, q_ref, kv_ref, w_scr, t_scr,
):
    for i, ref in enumerate((near_ref, far_ref, near_other_ref, far_other_ref)):
        for dx in range(4):
            w_scr[rows_at(i // 2, i % 2, dx), :] = ref[dx]
    t_scr[...] = dot(w_scr[...].T, places(order_ref), NT)
    wt_ref[...] = t_scr[0:576].astype(BF)
    gains = t_scr[576:584]
    gains_ref[...] = gains
    gain, bias = gains[0:1], gains[1:2]
    for j in range(8):
        hat, _ = normalize(own_ref[j].astype(F32))
        normed_ref[j * 128 : (j + 1) * 128, :] = (hat * gain + bias).astype(BF)
    for j in range(4):
        lanes = slice(j * 256, (j + 1) * 256)
        qkv = dot(wt_ref[...], normed_ref[lanes, :], NT).astype(BF)
        q_ref[:, lanes] = qkv[0:192]
        kv_ref[:, lanes] = qkv[192:576]


def last_keys(m, core, length):
    lane = lax.broadcasted_iota(jnp.int32, (1, 256), 1)
    query = m * 512 + 128 * core + jnp.where(lane < 128, lane, lane + 128)
    return jnp.minimum(query, length - 1)


def allowed(start, first, last, core):
    offset = start + first + (128 * core if first < 128 else -128 * core)
    return lax.broadcasted_iota(jnp.int32, (64, 256), 0) <= last - offset


def fill_keys(own_ref, other_ref, k_scr, base):
    for u in range(3):
        for j in range(8):
            rows, lanes = pl.ds(base + u * 64, 64), pl.ds(j * 128, 128)
            k_scr[u, j * 256 : j * 256 + 128, :] = own_ref[rows, lanes].T
            k_scr[u, j * 256 + 128 : j * 256 + 256, :] = other_ref[rows, lanes].T


def fill_lanes(own_ref, other_ref, scr, base):
    for j in range(8):
        scr[:, j * 256 : j * 256 + 128] = own_ref[base : base + 192, j * 128 : j * 128 + 128]
        scr[:, j * 256 + 128 : j * 256 + 256] = other_ref[
            base : base + 192, j * 128 : j * 128 + 128
        ]


PAIRS = [(h, u) for h in range(2) for u in range(3)]
CHUNKS = [slice(i * 64, i * 64 + 64) for i in range(4)]


def steps(m, length):
    return jnp.minimum(m + 1, (length + 511) // 512)


def sweep(length, begin, score, step, finish):
    def one(_, place):
        m, jk = place
        more = jk + 1 < steps(m, length)
        next_m = jnp.where(more, m, jnp.minimum(m + 1, 3))
        next_jk = jnp.where(more, jk + 1, 0)

        @pl.when(jk == 0)
        def _():
            begin()

        edge = (jk == m) | (jk * 512 + 512 > length)

        @pl.when(edge)
        def _():
            step(m, jk, next_m, next_jk, True)

        @pl.when(jnp.logical_not(edge))
        def _():
            step(m, jk, next_m, next_jk, False)

        @pl.when(jnp.logical_not(more))
        def _():
            finish(m)

        return jnp.where(more, m, m + 1), next_jk

    for h, u in PAIRS:
        score(h, u, 0, 0)
    total = sum(steps(m, length) for m in range(4))
    lax.fori_loop(0, total, one, (jnp.int32(0), jnp.int32(0)))


def group(m):
    return pl.ds(pl.multiple_of(m * 256, 256), 256)


def key_tile(jk, h):
    return pl.ds(pl.multiple_of(jk * 512, 512) + h * 256, 256)


def forward_plain(q_scr, k_scr, v_scr, scratch, length, core, finish):
    s_scr, w_scr, acc_scr, sum_scr = scratch[0:6], scratch[6:12], scratch[12:15], scratch[15:18]

    def begin():
        for u in range(3):
            acc_scr[u][...] = jnp.zeros((64, 256), F32)
            sum_scr[u][...] = jnp.zeros((8, 256), F32)

    def score(h, u, m, jk):
        queries = q_scr[u * 64 : (u + 1) * 64, group(m)]
        s_scr[h * 3 + u][...] = dot(k_scr[u, key_tile(jk, h), :], queries)

    def step(m, jk, next_m, next_jk, masked):
        last = last_keys(m, core, length)
        for h, u in PAIRS:
            scores, weights = s_scr[h * 3 + u], w_scr[h * 3 + u]
            total = sum_scr[u][...]
            for rows in CHUNKS:
                s = scores[rows, :]
                t = s * s + 1.0
                r = lax.rsqrt(t)
                e = jnp.exp(t * r)
                if masked:
                    e = jnp.where(allowed(jk * 512 + h * 256, rows.start, last, core), e, 0.0)
                total = total + jnp.sum(e.reshape(8, 8, 256), axis=0)
                weights[rows, :] = (s * r * e).astype(BF)
            sum_scr[u][...] = total
            score(h, u, next_m, next_jk)
            acc_scr[u][...] += dot(v_scr[u * 64 : (u + 1) * 64, key_tile(jk, h)], weights[...])

    def close(m):
        for u in range(3):
            total = jnp.sum(sum_scr[u][...], axis=0, keepdims=True)
            finish(m, u, acc_scr[u][...], total, jnp.zeros((1, 256), F32))

    sweep(length, begin, score, step, close)


def forward_any(q_scr, k_scr, v_scr, length, core, finish):
    def one(m, _):
        last = last_keys(m, core, length)

        def step(jk, carry):
            start = pl.multiple_of(jk * 256, 256)
            mask = jnp.concatenate([allowed(start, r.start, last, core) for r in CHUNKS], axis=0)
            out = []
            for u in range(3):
                top, total, accum = carry[u]
                s = dot(k_scr[u, pl.ds(start, 256), :], q_scr[u * 64 : (u + 1) * 64, group(m)])
                t = s * s + 1.0
                r = lax.rsqrt(t)
                a = jnp.where(mask, t * r, -1e30)
                fresh = jnp.maximum(top, jnp.max(a, axis=0, keepdims=True))
                e = jnp.exp(a - fresh)
                rescale = jnp.exp(top - fresh)
                total = total * rescale + jnp.sum(e, axis=0, keepdims=True)
                accum = accum * rescale + dot(
                    v_scr[u * 64 : (u + 1) * 64, pl.ds(start, 256)], (s * r * e).astype(BF)
                )
                out.append((fresh, total, accum))
            return tuple(out)

        zero = (jnp.zeros((1, 256), F32), jnp.zeros((1, 256), F32), jnp.zeros((64, 256), F32))
        carry = lax.fori_loop(0, 2 * steps(m, length), step, (zero,) * 3)
        for u in range(3):
            finish(m, u, carry[u][2], carry[u][1], carry[u][0])
        return 0

    lax.fori_loop(0, 4, one, 0)


def forward_kernel(
    lengths_ref, q_ref, own_ref, other_ref, o_ref, low_ref, lse_ref, q_scr, k_scr, v_scr, *scratch
):
    length, core = length_of(lengths_ref), core_of()
    fill_keys(own_ref, other_ref, k_scr, 0)
    fill_lanes(own_ref, other_ref, v_scr, 192)
    q_scr[...] = q_ref[...] * BF(0.125)

    def finish(m, u, accum, total, top):
        lanes = group(m)
        o = accum / total
        o_ref[u * 64 : (u + 1) * 64, lanes] = o
        for half in range(2):
            low_ref[2 * m + half, u * 64 : (u + 1) * 64, :] = o[
                :, half * 128 : half * 128 + 128
            ].astype(BF)
        lse_ref[u : u + 1, lanes] = top + jnp.log(total)

    def largest(ref):
        values = ref[0:192, :].astype(F32)
        return jnp.max(jnp.sum((values * values).reshape(3, 64, 1024), axis=1))

    bound = largest(q_ref) * jnp.maximum(largest(own_ref), largest(other_ref)) * (1.0 / 64.0)
    small = bound < 3600.0

    @pl.when(small)
    def _():
        forward_plain(q_scr, k_scr, v_scr, scratch, length, core, finish)

    @pl.when(jnp.logical_not(small))
    def _():
        forward_any(q_scr, k_scr, v_scr, length, core, finish)


def backward_kernel(
    lengths_ref, q_ref, own_ref, other_ref, o_ref, lse_ref, da_ref,
    dq_ref, down_ref, dother_ref,
    q_scr, k_scr, kt_scr, v_scr, da_scr, dk_scr, dv_scr, delta_scr, *scratch,
):
    s_scr, dp_scr, w_scr, ds_scr, dq_scr = (scratch[i : i + 6] for i in (0, 6, 12, 18, 24))
    length, core = length_of(lengths_ref), core_of()
    fill_keys(own_ref, other_ref, k_scr, 0)
    fill_lanes(own_ref, other_ref, kt_scr, 0)
    fill_keys(own_ref, other_ref, v_scr, 192)
    q_scr[...] = q_ref[...] * BF(0.125)
    for j in range(8):
        lanes = slice(j * 128, (j + 1) * 128)
        da_scr[:, lanes] = da_ref[j]
        for u in range(3):
            rows = slice(u * 64, (u + 1) * 64)
            delta_scr[u : u + 1, lanes] = jnp.sum(
                da_ref[j, rows, :].astype(F32) * o_ref[rows, lanes], axis=0, keepdims=True
            )
    dk_scr[...] = jnp.zeros_like(dk_scr)
    dv_scr[...] = jnp.zeros_like(dv_scr)

    def begin():
        for u in range(3):
            dq_scr[u][...] = jnp.zeros((64, 256), F32)

    def score(h, u, m, jk):
        rows, tile = slice(u * 64, (u + 1) * 64), key_tile(jk, h)
        s_scr[h * 3 + u][...] = dot(k_scr[u, tile, :], q_scr[rows, group(m)])
        dp_scr[h * 3 + u][...] = dot(v_scr[u, tile, :], da_scr[rows, group(m)])

    def step(m, jk, next_m, next_jk, masked):
        last = last_keys(m, core, length)
        for h, u in PAIRS:
            tile = key_tile(jk, h)
            heads = slice(u * 64, (u + 1) * 64)
            delta, lse = delta_scr[u : u + 1, group(m)], lse_ref[u : u + 1, group(m)]
            place = h * 3 + u
            for rows in CHUNKS:
                s = s_scr[place][rows, :]
                t = s * s + 1.0
                r = lax.rsqrt(t)
                p = jnp.exp(t * r - lse)
                if masked:
                    p = jnp.where(allowed(jk * 512 + h * 256, rows.start, last, core), p, 0.0)
                g = s * r
                w_scr[place][rows, :] = (g * p).astype(BF)
                ds = p * (dp_scr[place][rows, :] * (r * r * (r - 1.0) + 1.0) - g * delta)
                ds_scr[place][rows, :] = ds.astype(BF)
            score(h, u, next_m, next_jk)
            dv_scr[u, :, tile] += dot(da_scr[heads, group(m)], w_scr[place][...], NT)
            dk_scr[u, :, tile] += dot(q_scr[heads, group(m)], ds_scr[place][...], NT)
            dq_scr[u][...] += dot(kt_scr[heads, tile], ds_scr[place][...])

    def close(m):
        for u in range(3):
            dq_ref[u * 64 : (u + 1) * 64, group(m)] = (dq_scr[u][...] * 0.125).astype(BF)

    sweep(length, begin, score, step, close)
    for scr, base in ((dk_scr, 0), (dv_scr, 192)):
        for u in range(3):
            rows = pl.ds(base + u * 64, 64)
            for j in range(8):
                lanes = pl.ds(j * 128, 128)
                down_ref[rows, lanes] = scr[u, :, j * 256 : j * 256 + 128].astype(BF)
                dother_ref[rows, lanes] = scr[u, :, j * 256 + 128 : j * 256 + 256].astype(BF)


GELU_SCALE = math.sqrt(2.0 / math.pi)


def prepare_kernel(att_ref, order_ref, place_ref, attended_ref, attended_t_ref):
    place_ref[...] = places(order_ref)
    for b in range(2):
        for e in range(4):
            attended_t_ref[e * 192 : (e + 1) * 192, b * 128 : (b + 1) * 128] = att_ref[2 * e + b]
    attended_ref[...] = dot(attended_t_ref[...].T, place_ref[...]).astype(BF)


def feed_kernel(
    x_hbm, dy_hbm, att_hbm, gains_hbm, place_hbm, weights_hbm,
    y_hbm, dfirst_hbm, low_hbm, datt_hbm, dgain_hbm, grads_hbm,
    x_ref, dy_ref, att_ref, gains_ref, place_ref, down_ref, up_ref, out_ref,
    y_ref, dfirst_ref, low_ref, datt_ref, dgain_ref, gdown, gup, acc_scr, dn_scr, loads, stores,
):
    def block(ref, number):
        return ref.at[:, pl.ds(48 * number, 48), :]

    arrivals = [(att_hbm, att_ref), (block(weights_hbm, 8), out_ref), (x_hbm, x_ref)]
    arrivals += [(gains_hbm, gains_ref), (place_hbm, place_ref)]
    for k in range(4):
        arrivals.append((block(weights_hbm, 4 + k), up_ref.at[k]))
        if k == 0:
            arrivals.append((dy_hbm, dy_ref))
        arrivals.append((block(weights_hbm, k), down_ref.at[k]))
    arrivals = [pltpu.make_async_copy(*pair, loads.at[i]) for i, pair in enumerate(arrivals)]
    for copy in arrivals:
        copy.start()
    departures = []

    def send(source, target):
        copy = pltpu.make_async_copy(source, target, stores.at[len(departures)])
        copy.start()
        departures.append(copy)

    for copy in arrivals[0:4]:
        copy.wait()
    gain, bias = gains_ref[2:3], gains_ref[3:4]
    w_out = out_ref[...].reshape(768, 768)
    first = x_ref[...].astype(F32) + dot(att_ref[...], w_out)
    hat, scale = normalize(first)
    acc_scr[...] = first
    arrivals[4].wait()
    n2 = dot((hat * gain + bias).astype(BF), place_ref[...]).astype(BF)
    n2t = n2.T
    waiting = arrivals[5:]
    for k in range(4):
        waiting.pop(0).wait()
        up = up_ref[k].reshape(768, 768)
        hidden = dot(n2, up)
        if k == 0:
            waiting.pop(0).wait()
        waiting.pop(0).wait()
        down = down_ref[k].reshape(768, 768)
        dy = dy_ref[...]
        d_active = dot(dy, down, NT)
        square = hidden * hidden
        tanh = jnp.tanh(GELU_SCALE * hidden * (1.0 + 0.044715 * square))
        share = 0.5 + 0.5 * tanh
        active = (hidden * share).astype(BF)
        slope = share + 0.5 * hidden * (1.0 - tanh * tanh) * (
            GELU_SCALE * (1.0 + (3 * 0.044715) * square)
        )
        d_hidden = (slope * d_active).astype(BF)
        gdown[k] = dot(active.T, dy).astype(BF).reshape(16, 48, 768)
        send(gdown.at[k], block(grads_hbm, k))
        gup[k] = dot(n2t, d_hidden).astype(BF).reshape(16, 48, 768)
        send(gup.at[k], block(grads_hbm, 4 + k))
        acc_scr[...] += dot(active, down)
        d_n2 = dot(d_hidden, up, NT)
        dn_scr[...] = d_n2 if k == 0 else dn_scr[...] + d_n2
    y_ref[...] = acc_scr[...].astype(BF)
    send(y_ref, y_hbm)
    dn = dot(dn_scr[...].astype(BF), place_ref[...], NT)
    t = dn * gain
    part = t - jnp.mean(t, -1, keepdims=True) - hat * jnp.mean(t * hat, -1, keepdims=True)
    d_first = dy_ref[...].astype(F32) + part * scale
    low = d_first.astype(BF)
    low_ref[...] = low
    send(low_ref, low_hbm)
    dfirst_ref[...] = d_first
    send(dfirst_ref, dfirst_hbm)
    d_att = dot(w_out, low, NT).astype(BF)
    d_att = dot(place_ref[...], d_att).astype(BF)
    for b in range(2):
        for e in range(4):
            datt_ref[2 * e + b] = d_att[e * 192 : (e + 1) * 192, b * 128 : (b + 1) * 128]
    send(datt_ref, datt_hbm)
    dgain_ref[0:1, :] = jnp.sum(dn * hat, axis=0, keepdims=True)
    dgain_ref[1:2, :] = jnp.sum(dn, axis=0, keepdims=True)
    dgain_ref[2:8, :] = jnp.zeros((6, 768), F32)
    send(dgain_ref, dgain_hbm)
    for copy in departures:
        copy.wait()


def out_kernel(attended_t_ref, low_ref, grad_ref):
    grad = dot(attended_t_ref[...], low_ref[...]).reshape(8, 2, 2, 24, 768)
    half = lax.axis_index("batch") // 4
    for j in range(8):
        rows = [
            jnp.where(half == z, grad[j, c, z], grad[j ^ 1, c, z]) for c in range(2) for z in range(2)
        ]
        grad_ref[j] = jnp.concatenate(rows, axis=0).astype(BF)


def whole(*dims):
    return pl.BlockSpec(dims, lambda *_: (0,) * len(dims))


def feed(*arrays):
    outs = [
        shape((256, 768), BF), shape((256, 768), F32), shape((256, 768), BF),
        shape((8, 192, 128), BF), shape((8, 768), F32), shape((16, 384, 768), BF),
    ]
    blocks = pltpu.VMEM((4, 16, 48, 768), BF)
    held = [pltpu.VMEM(a.shape, a.dtype) for a in arrays[:-1]]
    held += [blocks, blocks, pltpu.VMEM((16, 48, 768), BF)]
    held += [pltpu.VMEM(o.shape, o.dtype) for o in outs[:-1]]
    held += [blocks, blocks] + [pltpu.VMEM((256, 768), F32)] * 2
    held += [pltpu.SemaphoreType.DMA((14,)), pltpu.SemaphoreType.DMA((13,))]
    return call(
        feed_kernel,
        outs,
        arrays,
        15,
        held,
        in_specs=[pl.BlockSpec(memory_space=pl.ANY)] * len(arrays),
        out_specs=[pl.BlockSpec(memory_space=pl.ANY)] * len(outs),
    )


def unproject_kernel(
    own_ref, dq_ref, dkv_ref, partner_ref, normed_ref, wt_ref, dgain_ref, order_ref,
    out_ref, spread_ref,
    part_ref, mine_ref, theirs_ref, dt_scr, dw_scr, p_scr, o_scr,
):
    dt_scr[0:192, :] = dq_ref[...]
    dt_scr[192:576, :] = (dkv_ref[...].astype(F32) + partner_ref[...].astype(F32)).astype(BF)
    bias_sum = jnp.zeros((1, 768), F32)
    gain_sum = jnp.zeros((1, 768), F32)
    for j in range(4):
        d_normed = dot(dt_scr[:, j * 256 : (j + 1) * 256].T, wt_ref[...])
        part_ref[2 * j : 2 * j + 2] = d_normed.astype(BF).reshape(2, 128, 768)
        hat, _ = normalize(own_ref[2 * j : 2 * j + 2].reshape(256, 768).astype(F32))
        gain_sum += jnp.sum(d_normed * hat, axis=0, keepdims=True)
        bias_sum += jnp.sum(d_normed, axis=0, keepdims=True)
    dw_scr[0:576, :] = dot(dt_scr[...], normed_ref[...])
    dw_scr[576:577, :] = gain_sum
    dw_scr[577:578, :] = bias_sum
    dw_scr[578:580, :] = dgain_ref[0:2, :]
    dw_scr[580:640, :] = jnp.zeros((60, 768), F32)
    p_scr[...] = dot(dw_scr[...].astype(BF), places(order_ref)).T.astype(BF)
    out = jnp.zeros((96, 768), F32)
    for j in range(8):
        out += out_ref[j].astype(F32)
    lanes = lax.broadcasted_iota(jnp.int32, (128, 96), 1)
    spread = jnp.where(lanes == spread_ref[...], 1.0, 0.0).astype(BF)
    o_scr[...] = dot(spread, out.astype(BF))
    for dc, ref in enumerate((mine_ref, theirs_ref)):
        for dx in range(4):
            for dz in range(2):
                ref[dx, dz, :, 0:640] = p_scr[rows_at(dc, dz, dx), :]
                few = o_scr[rows_at(dc, dz, dx, 8), :]
                ref[dx, dz, :, 640:768] = jnp.concatenate(
                    [few[:, q * 128 : (q + 1) * 128] for q in range(6)], axis=0
                ).astype(BF)


def slots_kernel(rest_ref, qkv_ref, order_ref, out_ref, r_scr):
    r_scr[0:384, :] = rest_ref[...]
    r_scr[384:432, :] = jnp.zeros((48, 768), BF)
    r_scr[432:480, 0:640] = qkv_ref[:, 0:640]
    r_scr[432:480, 640:768] = jnp.zeros((48, 128), BF)
    r_scr[480:512, :] = jnp.zeros((32, 768), BF)
    out_ref[...] = dot(places(order_ref), r_scr[...]).astype(BF).reshape(8, 64, 768)


def finish_kernel(x_ref, dfirst_ref, gains_ref, got_ref, qkv_ref, dtok_ref, out_ref):
    for q in range(6):
        out_ref[:, q * 128 : (q + 1) * 128] = qkv_ref[q * 8 : q * 8 + 8, 640:768].astype(F32)[0:6]
    gain = gains_ref[0:1]
    for b in range(2):
        rows = slice(b * 128, (b + 1) * 128)
        dn = jnp.zeros((128, 768), F32)
        for e in range(4):
            dn += got_ref[2 * e + b].astype(F32)
        hat, scale = normalize(x_ref[rows, :].astype(F32))
        t = dn * gain
        part = t - jnp.mean(t, -1, keepdims=True) - hat * jnp.mean(t * hat, -1, keepdims=True)
        dtok_ref[rows, :] = (dfirst_ref[rows, :] + part * scale).astype(BF)


def sums_kernel(got_ref, units_ref, down_ref, up_ref, qkv_ref, g1_ref, b1_ref, g2_ref, b2_ref):
    total = jnp.zeros((64, 768), F32)
    chunks = []
    for e in range(4):
        both = got_ref[2 * e].astype(F32) + got_ref[2 * e + 1].astype(F32)
        chunks.append(both[54:60])
        total += both
    down_ref[...] = total[0:24]
    left, up, units = total[30:54], jnp.zeros((24, 768), F32), places(units_ref)
    for _ in range(3):
        piece = left.astype(BF)
        left = left - piece.astype(F32)
        up += dot(piece, units, NT)
    for k in range(4):
        up_ref[:, k * 768 : (k + 1) * 768] = up[k * 6 : k * 6 + 6]
    for s in range(3):
        qkv_ref[:, s * 768 : (s + 1) * 768] = jnp.concatenate(
            [chunks[e][:, s * 192 : (s + 1) * 192] for e in range(4)], axis=1
        )
    norms = total[:, 512:640].T
    for i, ref in enumerate((g1_ref, b1_ref, g2_ref, b2_ref)):
        ref[...] = norms[64 + i : 65 + i, 54:60]


def scalars(count):
    return dict(
        in_specs=[pl.BlockSpec(memory_space=pltpu.SMEM)]
        + [pl.BlockSpec(memory_space=pltpu.VMEM)] * (count - 1)
    )


def body(tokens, lengths, gain_one, bias_one, w_qkv, w_out, gain_two, bias_two, w_up, w_down, d_out):
    order, units, regroup, qkv_order = (
        jnp.asarray(v) for v in (ROW_ORDER, UNIT_ORDER, REGROUP, QKV_ORDER)
    )
    exchange = functools.partial(
        lax.all_to_all, axis_name="seq", split_axis=0, concat_axis=0, tiled=True,
        axis_index_groups=SAME_CORE,
    )

    vectors = [v.reshape(1, 6) for v in (gain_one, bias_one, gain_two, bias_two)]
    slots = pl.pallas_call(
        pack_kernel,
        grid=(1,),
        in_specs=[whole(24, 768), whole(6, 768), whole(6, 3072), whole(6, 2304)]
        + [whole(1, 6)] * 4
        + [whole(1, 768)],
        out_specs=whole(8, 64, 768),
        out_shape=shape((8, 64, 768), BF),
        scratch_shapes=[pltpu.VMEM((64, 768), F32), pltpu.VMEM((128, 128), F32)],
        cost_estimate=about(2),
        compiler_params=pltpu.CompilerParams(vmem_limit_bytes=60 * 1024 * 1024),
    )(w_down, w_out, w_up, w_qkv, *vectors, units)
    slots = exchange(slots)
    rest, qkv_rows = call(
        regroup_kernel,
        [shape((432, 768), BF), shape((48, 640), BF)],
        (slots, regroup),
        2,
        mib=12,
    )
    weights = lax.all_gather(rest, BOTH, axis=0, axis_index_groups=RINGS)
    near = jnp.stack(
        [qkv_rows] + [lax.ppermute(qkv_rows, "batch", along_x(step)) for step in (-1, 2, 1)]
    )
    far = lax.ppermute(near, BOTH, SWAP_HALF)
    near_other = lax.ppermute(near, "seq", SWAP_CORE)
    far_other = lax.ppermute(far, "seq", SWAP_CORE)
    x = tokens.transpose(1, 0, 2)
    dy = d_out.transpose(1, 0, 2).reshape(256, 768)
    own = exchange(jnp.broadcast_to(x[None], (4, 2, 128, 768)).reshape(8, 128, 768))
    x = x.reshape(256, 768)

    normed, wt, gains, q_t, kv = call(
        project_kernel,
        [
            shape((1024, 768), BF), shape((576, 768), BF), shape((8, 768), F32),
            shape((192, 1024), BF), shape((384, 1024), BF),
        ],
        (own, near, far, near_other, far_other, qkv_order),
        5,
        [pltpu.VMEM((768, 640), BF), pltpu.VMEM((640, 768), F32)],
        mib=30,
    )
    kv_other = lax.ppermute(kv, "seq", SWAP_CORE)
    o, o_low, lse = call(
        forward_kernel,
        [shape((192, 1024), F32), shape((8, 192, 128), BF), shape((3, 1024), F32)],
        (lengths, q_t, kv, kv_other),
        12,
        [
            pltpu.VMEM((192, 1024), BF), pltpu.VMEM((3, 2048, 64), BF),
            pltpu.VMEM((192, 2048), BF),
        ]
        + [pltpu.VMEM((256, 256), F32)] * 6
        + [pltpu.VMEM((256, 256), BF)] * 6
        + [pltpu.VMEM((64, 256), F32)] * 3
        + [pltpu.VMEM((8, 256), F32)] * 3,
        mib=30,
        **scalars(4),
    )
    att = exchange(o_low)
    place, attended, attended_t = call(
        prepare_kernel,
        [shape((768, 768), BF), shape((256, 768), BF), shape((768, 256), BF)],
        (att, order),
        2,
        mib=16,
    )
    y, d_first, low, d_att, d_gain, grads = feed(x, dy, attended, gains, place, weights)
    rest_sum = lax.psum_scatter(
        grads.reshape(16 * 384, 768), BOTH, scatter_dimension=0, tiled=True,
        axis_index_groups=RINGS,
    )
    d_att = exchange(d_att)
    out_grad = exchange(call(out_kernel, shape((8, 96, 768), BF), (attended_t, low), 2))
    dq, dkv, dkv_other = call(
        backward_kernel,
        [shape((192, 1024), BF), shape((384, 1024), BF), shape((384, 1024), BF)],
        (lengths, q_t, kv, kv_other, o, lse, d_att),
        20,
        [
            pltpu.VMEM((192, 1024), BF),
            pltpu.VMEM((3, 2048, 64), BF),
            pltpu.VMEM((192, 2048), BF),
            pltpu.VMEM((3, 2048, 64), BF),
            pltpu.VMEM((192, 1024), BF),
            pltpu.VMEM((3, 64, 2048), F32),
            pltpu.VMEM((3, 64, 2048), F32),
            pltpu.VMEM((3, 1024), F32),
        ]
        + [pltpu.VMEM((256, 256), F32)] * 12
        + [pltpu.VMEM((256, 256), BF)] * 12
        + [pltpu.VMEM((64, 256), F32)] * 3,
        mib=60,
        **scalars(7),
    )
    partner = lax.ppermute(dkv_other, "seq", SWAP_CORE)
    part, mine, theirs = call(
        unproject_kernel,
        [shape((8, 128, 768), BF), shape((4, 2, 48, 768), BF), shape((4, 2, 48, 768), BF)],
        (own, dq, dkv, partner, normed, wt, d_gain, qkv_order, out_grad, jnp.asarray(SPREAD)),
        7,
        [
            pltpu.VMEM((576, 1024), BF), pltpu.VMEM((640, 768), F32),
            pltpu.VMEM((768, 640), BF), pltpu.VMEM((128, 768), F32),
        ],
        mib=60,
    )
    add = lambda *parts: sum(p.astype(F32) for p in parts).astype(BF)
    line = add(mine, lax.ppermute(theirs, "seq", SWAP_CORE))
    line = add(
        line[0],
        lax.ppermute(line[1], "batch", along_x(1)),
        lax.ppermute(line[2], "batch", along_x(2)),
        lax.ppermute(line[3], "batch", along_x(-1)),
    )
    qkv_sum = add(line[0], lax.ppermute(line[1], BOTH, SWAP_HALF))
    back = exchange(part)
    d_tokens, d_out_w = call(
        finish_kernel,
        [shape((256, 768), BF), shape((6, 768), F32)],
        (x, d_first, gains, back, qkv_sum),
        3,
        mib=16,
    )
    slots = call(
        slots_kernel,
        shape((8, 64, 768), BF),
        (rest_sum, qkv_sum, regroup),
        2,
        [pltpu.VMEM((512, 768), BF)],
        mib=12,
    )
    slots = exchange(slots)
    vector = shape((1, 6), F32)
    d_down, d_up, d_qkv, *norms = call(
        sums_kernel,
        [shape((24, 768), F32), shape((6, 3072), F32), shape((6, 2304), F32)]
        + [vector] * 4,
        (slots, units),
        2,
        mib=12,
    )
    norms = [v.reshape(6) for v in norms]
    output = y.reshape(2, 128, 768).transpose(1, 0, 2)
    d_tokens = d_tokens.reshape(2, 128, 768).transpose(1, 0, 2)
    return (
        output, d_tokens, norms[0], norms[1], d_qkv, d_out_w, norms[2], norms[3], d_up, d_down,
    )


def solution(mesh):
    rows = P(("seq", "batch"))
    tokens = P("seq", "batch", None)
    return jax.shard_map(
        body,
        mesh=mesh,
        in_specs=(tokens, P("batch"), rows, rows, rows, rows, rows, rows, rows, rows, tokens),
        out_specs=(tokens, tokens, rows, rows, rows, rows, rows, rows, rows, rows),
        check_vma=False,
    )
```

```python
import functools
import math

import jax
import jax.numpy as jnp
import numpy as np
from jax import lax
from jax.experimental import pallas as pl
from jax.experimental.pallas import tpu as pltpu
from jax.sharding import PartitionSpec as P

H = 12
HD = 64
EPSILON = 1e-05
BF = jnp.bfloat16
F32 = jnp.float32
BOTH = ("seq", "batch")
SAME_CORE = [[2 * k + c for k in range(8)] for c in range(2)]
SWAP_CORE = [(i, i ^ 1) for i in range(16)]
TURNS = [(0, 0), (0, 1), (0, 2), (0, 3), (1, 3), (1, 2), (1, 1), (1, 0)]
RING = [(c, z, x) for z, x in TURNS for c in range(2)]


RINGS = [
    [((y * 2 + (low ^ z)) * 2 + c) * 8 + z * 4 + x for c, z, x in RING]
    for y in range(4)
    for low in range(2)
]
SWAP_HALF = [(s * 8 + b, (s ^ 2) * 8 + (b ^ 4)) for s in range(16) for b in range(8)]


def along_x(step):
    return [(b, b // 4 * 4 + (b + step) % 4) for b in range(8)]


def in_order(outer, size):
    natural = np.arange(outer * 16 * size, dtype=np.int32).reshape(outer, 2, 8, size)
    return np.stack([natural[:, c, z * 4 + x] for c, z, x in RING]).reshape(1, -1)


QKV_ORDER = (
    np.arange(768, dtype=np.int32).reshape(8, 2, 8, 6).transpose(1, 2, 0, 3).reshape(1, 768)
)
ROW_ORDER = in_order(8, 6)
UNIT_ORDER = in_order(2, 24)


def regroup_order():
    slot = np.arange(512, dtype=np.int32).reshape(8, 64)
    parts = [slot[:, 0:24]] + [slot[:, f : f + 6] for f in (30, 36, 42, 48, 24, 54)]
    return np.concatenate([p.reshape(-1) for p in parts] + [np.full(32, -1, np.int32)])[None]


REGROUP = regroup_order()


def arrival_places():
    s, j, dz, dx, r = np.indices((2, 8, 2, 4, 6), dtype=np.int32).reshape(5, 768)
    return np.stack([j ^ dz, s, dz, dx, r] + [np.zeros_like(r)] * 3)


ARRIVAL = arrival_places()
SPREAD = np.concatenate(
    [np.arange(96, dtype=np.int32).reshape(16, 6), np.full((16, 2), -1, np.int32)], axis=1
).reshape(128, 1)


def places(order):
    size = order.shape[1]
    rows = lax.broadcasted_iota(jnp.int32, (size, size), 0)
    return jnp.where(rows == order, 1.0, 0.0).astype(BF)


NT = (((1,), (1,)), ((), ()))
NN = (((1,), (0,)), ((), ()))
TN = (((0,), (0,)), ((), ()))


def dot(left, right, dims=NN):
    return lax.dot_general(left, right, dims, preferred_element_type=F32)


def about(us):
    return pl.CostEstimate(flops=int(us * 1.1e9), bytes_accessed=0, transcendentals=0)


def call(kernel, outs, ins, us, scratch=(), mib=60, **kwargs):
    return pl.pallas_call(
        kernel,
        out_shape=outs,
        scratch_shapes=list(scratch),
        cost_estimate=about(us),
        compiler_params=pltpu.CompilerParams(vmem_limit_bytes=mib * 1024 * 1024),
        **kwargs,
    )(*ins)


def shape(dims, dtype):
    return jax.ShapeDtypeStruct(dims, dtype)


def normalize(values):
    center = jnp.mean(values, axis=-1, keepdims=True)
    shifted = values - center
    spread = jnp.mean(shifted * shifted, axis=-1, keepdims=True)
    scale = lax.rsqrt(spread + EPSILON)
    return shifted * scale, scale


def pack_kernel(
    down_ref, out_ref, up_ref, qkv_ref, g1_ref, b1_ref, g2_ref, b2_ref, units_ref,
    slot_ref, raw_ref, scr, turn_scr, raw_scr,
):
    turn_scr[...] = jnp.zeros_like(turn_scr)
    for i, ref in enumerate((g1_ref, b1_ref, g2_ref, b2_ref)):
        turn_scr[64 + i : 65 + i, 0:6] = ref[...].astype(F32)
    norms = turn_scr[...].T[0:6, 64:128].astype(BF)
    up = jnp.concatenate(
        [up_ref[:, k * 768 : (k + 1) * 768].astype(F32) for k in range(4)], axis=0
    ).astype(BF)
    scr[0:24, :] = down_ref[...].astype(F32)
    scr[24:30, :] = out_ref[...].astype(F32)
    scr[30:54, :] = dot(up, places(units_ref[...]))
    scr[54:64, :] = jnp.zeros((10, 768), F32)
    slot = scr[...].astype(BF)
    for j in range(8):
        slot_ref[j] = slot
    for e in range(4):
        parts = [qkv_ref[:, s * 768 + e * 192 : s * 768 + (e + 1) * 192] for s in range(3)]
        row = jnp.concatenate(parts + [norms], axis=1)
        raw_scr[e * 6 : e * 6 + 6, :] = row.astype(F32)
    raw_ref[...] = raw_scr[...].astype(BF)


def regroup_kernel(slots_ref, order_ref, far_ref, rest_ref):
    rows = dot(places(order_ref[...]), slots_ref[...].reshape(512, 768), TN).astype(BF)
    rest_ref[...] = rows[0:432]


def address_kernel(x_ref, near_ref, far_ref, out_ref, scr):
    for e in range(4):
        for dz, ref in enumerate((near_ref, far_ref)):
            for dx in range(4):
                first = (dz * 4 + dx) * 6
                scr[e, first : first + 6, :] = ref[dx].astype(F32)[e * 6 : e * 6 + 6]
        for b in range(2):
            out_ref[2 * e + b, 0:128, :] = x_ref[b]
            out_ref[2 * e + b, 128:176, 0:640] = scr[e].astype(BF)
            out_ref[2 * e + b, 128:176, 640:768] = jnp.zeros((48, 128), BF)


def core_of():
    return lax.rem(lax.axis_index("seq"), 2)


def length_of(lengths_ref):
    return jnp.where(lax.rem(lax.axis_index("seq") // 2, 2) == 0, lengths_ref[0], lengths_ref[1])


def rows_at(dc, dz, dx, size=48):
    row = lax.axis_index("batch")
    c = lax.rem(core_of() + dc, 2)
    z = lax.rem(row // 4 + dz, 2)
    x = lax.rem(row + dx, 4)
    return pl.ds(pl.multiple_of((c * 8 + z * 4 + x) * size, size), size)


def project_kernel(
    own_ref, other_ref, arrival_ref,
    normed_ref, wt_ref, gains_ref, q_ref, kv_ref, w_scr, t_scr,
):
    for j in range(8):
        w_scr[j * 48 : j * 48 + 48, :] = own_ref[j, 128:176, 0:640]
        w_scr[384 + j * 48 : 432 + j * 48, :] = other_ref[j]
    core, row = core_of(), lax.axis_index("batch")
    half, column = row // 4, lax.rem(row, 4)
    table = [arrival_ref[i : i + 1, :] for i in range(5)]
    c = jnp.where(table[1] == 0, core, 1 - core)
    z = jnp.where(table[2] == 0, half, 1 - half)
    x = jnp.bitwise_and(table[3] + column, 3)
    order = ((table[0] * 2 + c) * 8 + z * 4 + x) * 6 + table[4]
    t_scr[...] = dot(w_scr[...].T, places(order), NT)
    wt_ref[...] = t_scr[0:576].astype(BF)
    gains = t_scr[576:584]
    gains_ref[...] = gains
    gain, bias = gains[0:1], gains[1:2]
    for j in range(8):
        hat, _ = normalize(own_ref[j, 0:128, :].astype(F32))
        normed_ref[j * 128 : (j + 1) * 128, :] = (hat * gain + bias).astype(BF)
    for j in range(4):
        lanes = slice(j * 256, (j + 1) * 256)
        qkv = dot(wt_ref[...], normed_ref[lanes, :], NT).astype(BF)
        q_ref[:, lanes] = qkv[0:192]
        kv_ref[:, lanes] = qkv[192:576]


def last_keys(m, core, length):
    lane = lax.broadcasted_iota(jnp.int32, (1, 256), 1)
    query = m * 512 + 128 * core + jnp.where(lane < 128, lane, lane + 128)
    return jnp.minimum(query, length - 1)


def allowed(start, first, last, core):
    offset = start + first + (128 * core if first < 128 else -128 * core)
    return lax.broadcasted_iota(jnp.int32, (64, 256), 0) <= last - offset


def fill_keys(own_ref, other_ref, k_scr, base):
    for u in range(3):
        for j in range(8):
            rows, lanes = pl.ds(base + u * 64, 64), pl.ds(j * 128, 128)
            k_scr[u, j * 256 : j * 256 + 128, :] = own_ref[rows, lanes].T
            k_scr[u, j * 256 + 128 : j * 256 + 256, :] = other_ref[rows, lanes].T


def fill_lanes(own_ref, other_ref, scr, base):
    for j in range(8):
        scr[:, j * 256 : j * 256 + 128] = own_ref[base : base + 192, j * 128 : j * 128 + 128]
        scr[:, j * 256 + 128 : j * 256 + 256] = other_ref[
            base : base + 192, j * 128 : j * 128 + 128
        ]


PAIRS = [(h, u) for h in range(2) for u in range(3)]
CHUNKS = [slice(i * 64, i * 64 + 64) for i in range(4)]


def steps(m, length):
    return jnp.minimum(m + 1, (length + 511) // 512)


def sweep(length, begin, score, step, finish):
    def one(_, place):
        m, jk = place
        more = jk + 1 < steps(m, length)
        next_m = jnp.where(more, m, jnp.minimum(m + 1, 3))
        next_jk = jnp.where(more, jk + 1, 0)

        @pl.when(jk == 0)
        def _():
            begin()

        edge = (jk == m) | (jk * 512 + 512 > length)

        @pl.when(edge)
        def _():
            step(m, jk, next_m, next_jk, True)

        @pl.when(jnp.logical_not(edge))
        def _():
            step(m, jk, next_m, next_jk, False)

        @pl.when(jnp.logical_not(more))
        def _():
            finish(m)

        return jnp.where(more, m, m + 1), next_jk

    for h, u in PAIRS:
        score(h, u, 0, 0)
    total = sum(steps(m, length) for m in range(4))
    lax.fori_loop(0, total, one, (jnp.int32(0), jnp.int32(0)))


def group(m):
    return pl.ds(pl.multiple_of(m * 256, 256), 256)


def key_tile(jk, h):
    return pl.ds(pl.multiple_of(jk * 512, 512) + h * 256, 256)


def forward_plain(q_scr, k_scr, v_scr, scratch, length, core, finish):
    s_scr, w_scr, acc_scr, sum_scr = scratch[0:6], scratch[6:12], scratch[12:15], scratch[15:18]

    def begin():
        for u in range(3):
            acc_scr[u][...] = jnp.zeros((64, 256), F32)
            sum_scr[u][...] = jnp.zeros((8, 256), F32)

    def score(h, u, m, jk):
        queries = q_scr[u * 64 : (u + 1) * 64, group(m)]
        s_scr[h * 3 + u][...] = dot(k_scr[u, key_tile(jk, h), :], queries)

    def step(m, jk, next_m, next_jk, masked):
        last = last_keys(m, core, length)
        for h, u in PAIRS:
            scores, weights = s_scr[h * 3 + u], w_scr[h * 3 + u]
            total = sum_scr[u][...]
            for rows in CHUNKS:
                s = scores[rows, :]
                t = s * s + 1.0
                r = lax.rsqrt(t)
                e = jnp.exp(t * r)
                if masked:
                    e = jnp.where(allowed(jk * 512 + h * 256, rows.start, last, core), e, 0.0)
                total = total + jnp.sum(e.reshape(8, 8, 256), axis=0)
                weights[rows, :] = (s * r * e).astype(BF)
            sum_scr[u][...] = total
            score(h, u, next_m, next_jk)
            acc_scr[u][...] += dot(v_scr[u * 64 : (u + 1) * 64, key_tile(jk, h)], weights[...])

    def close(m):
        for u in range(3):
            total = jnp.sum(sum_scr[u][...], axis=0, keepdims=True)
            finish(m, u, acc_scr[u][...], total, jnp.zeros((1, 256), F32))

    sweep(length, begin, score, step, close)


def forward_any(q_scr, k_scr, v_scr, length, core, finish):
    def one(m, _):
        last = last_keys(m, core, length)

        def step(jk, carry):
            start = pl.multiple_of(jk * 256, 256)
            mask = jnp.concatenate([allowed(start, r.start, last, core) for r in CHUNKS], axis=0)
            out = []
            for u in range(3):
                top, total, accum = carry[u]
                s = dot(k_scr[u, pl.ds(start, 256), :], q_scr[u * 64 : (u + 1) * 64, group(m)])
                t = s * s + 1.0
                r = lax.rsqrt(t)
                a = jnp.where(mask, t * r, -1e30)
                fresh = jnp.maximum(top, jnp.max(a, axis=0, keepdims=True))
                e = jnp.exp(a - fresh)
                rescale = jnp.exp(top - fresh)
                total = total * rescale + jnp.sum(e, axis=0, keepdims=True)
                accum = accum * rescale + dot(
                    v_scr[u * 64 : (u + 1) * 64, pl.ds(start, 256)], (s * r * e).astype(BF)
                )
                out.append((fresh, total, accum))
            return tuple(out)

        zero = (jnp.zeros((1, 256), F32), jnp.zeros((1, 256), F32), jnp.zeros((64, 256), F32))
        carry = lax.fori_loop(0, 2 * steps(m, length), step, (zero,) * 3)
        for u in range(3):
            finish(m, u, carry[u][2], carry[u][1], carry[u][0])
        return 0

    lax.fori_loop(0, 4, one, 0)


def forward_kernel(
    lengths_ref, q_ref, own_ref, other_ref, o_ref, low_ref, lse_ref, q_scr, k_scr, v_scr, *scratch
):
    length, core = length_of(lengths_ref), core_of()
    fill_keys(own_ref, other_ref, k_scr, 0)
    fill_lanes(own_ref, other_ref, v_scr, 192)
    q_scr[...] = q_ref[...] * BF(0.125)

    def finish(m, u, accum, total, top):
        lanes = group(m)
        o = accum / total
        o_ref[u * 64 : (u + 1) * 64, lanes] = o
        for half in range(2):
            low_ref[2 * m + half, u * 64 : (u + 1) * 64, :] = o[
                :, half * 128 : half * 128 + 128
            ].astype(BF)
        lse_ref[u : u + 1, lanes] = top + jnp.log(total)

    def largest(ref):
        values = ref[0:192, :].astype(F32)
        return jnp.max(jnp.sum((values * values).reshape(3, 64, 1024), axis=1))

    bound = largest(q_ref) * jnp.maximum(largest(own_ref), largest(other_ref)) * (1.0 / 64.0)
    small = bound < 3600.0

    @pl.when(small)
    def _():
        forward_plain(q_scr, k_scr, v_scr, scratch, length, core, finish)

    @pl.when(jnp.logical_not(small))
    def _():
        forward_any(q_scr, k_scr, v_scr, length, core, finish)


def backward_kernel(
    lengths_ref, q_ref, own_ref, other_ref, o_ref, lse_ref, da_ref,
    dq_ref, down_ref, dother_ref,
    q_scr, k_scr, kt_scr, v_scr, da_scr, dk_scr, dv_scr, delta_scr, *scratch,
):
    s_scr, dp_scr, w_scr, ds_scr, dq_scr = (scratch[i : i + 6] for i in (0, 6, 12, 18, 24))
    length, core = length_of(lengths_ref), core_of()
    fill_keys(own_ref, other_ref, k_scr, 0)
    fill_lanes(own_ref, other_ref, kt_scr, 0)
    fill_keys(own_ref, other_ref, v_scr, 192)
    q_scr[...] = q_ref[...] * BF(0.125)
    for j in range(8):
        lanes = slice(j * 128, (j + 1) * 128)
        da_scr[:, lanes] = da_ref[j]
        for u in range(3):
            rows = slice(u * 64, (u + 1) * 64)
            delta_scr[u : u + 1, lanes] = jnp.sum(
                da_ref[j, rows, :].astype(F32) * o_ref[rows, lanes], axis=0, keepdims=True
            )
    dk_scr[...] = jnp.zeros_like(dk_scr)
    dv_scr[...] = jnp.zeros_like(dv_scr)

    def begin():
        for u in range(3):
            dq_scr[u][...] = jnp.zeros((64, 256), F32)

    def score(h, u, m, jk):
        rows, tile = slice(u * 64, (u + 1) * 64), key_tile(jk, h)
        s_scr[h * 3 + u][...] = dot(k_scr[u, tile, :], q_scr[rows, group(m)])
        dp_scr[h * 3 + u][...] = dot(v_scr[u, tile, :], da_scr[rows, group(m)])

    def step(m, jk, next_m, next_jk, masked):
        last = last_keys(m, core, length)
        for h, u in PAIRS:
            tile = key_tile(jk, h)
            heads = slice(u * 64, (u + 1) * 64)
            delta, lse = delta_scr[u : u + 1, group(m)], lse_ref[u : u + 1, group(m)]
            place = h * 3 + u
            for rows in CHUNKS:
                s = s_scr[place][rows, :]
                t = s * s + 1.0
                r = lax.rsqrt(t)
                p = jnp.exp(t * r - lse)
                if masked:
                    p = jnp.where(allowed(jk * 512 + h * 256, rows.start, last, core), p, 0.0)
                g = s * r
                w_scr[place][rows, :] = (g * p).astype(BF)
                ds = p * (dp_scr[place][rows, :] * (r * r * (r - 1.0) + 1.0) - g * delta)
                ds_scr[place][rows, :] = ds.astype(BF)
            score(h, u, next_m, next_jk)
            dv_scr[u, :, tile] += dot(da_scr[heads, group(m)], w_scr[place][...], NT)
            dk_scr[u, :, tile] += dot(q_scr[heads, group(m)], ds_scr[place][...], NT)
            dq_scr[u][...] += dot(kt_scr[heads, tile], ds_scr[place][...])

    def close(m):
        for u in range(3):
            dq_ref[u * 64 : (u + 1) * 64, group(m)] = (dq_scr[u][...] * 0.125).astype(BF)

    sweep(length, begin, score, step, close)
    for scr, base in ((dk_scr, 0), (dv_scr, 192)):
        for u in range(3):
            rows = pl.ds(base + u * 64, 64)
            for j in range(8):
                lanes = pl.ds(j * 128, 128)
                down_ref[rows, lanes] = scr[u, :, j * 256 : j * 256 + 128].astype(BF)
                dother_ref[rows, lanes] = scr[u, :, j * 256 + 128 : j * 256 + 256].astype(BF)


GELU_SCALE = math.sqrt(2.0 / math.pi)


def prepare_kernel(att_ref, order_ref, place_ref, attended_ref, attended_t_ref):
    place_ref[...] = places(order_ref[...])
    for b in range(2):
        for e in range(4):
            attended_t_ref[e * 192 : (e + 1) * 192, b * 128 : (b + 1) * 128] = att_ref[2 * e + b]
    attended_ref[...] = dot(attended_t_ref[...].T, place_ref[...]).astype(BF)


def feed_kernel(
    x_hbm, dy_hbm, att_hbm, gains_hbm, place_hbm, weights_hbm,
    y_hbm, dfirst_hbm, low_hbm, datt_hbm, dgain_hbm, grads_hbm,
    x_ref, dy_ref, att_ref, gains_ref, place_ref, down_ref, up_ref, out_ref,
    y_ref, dfirst_ref, low_ref, datt_ref, dgain_ref, gdown, gup, acc_scr, dn_scr, loads, stores,
):
    def block(ref, number):
        return ref.at[:, pl.ds(48 * number, 48), :]

    arrivals = [(att_hbm, att_ref), (block(weights_hbm, 8), out_ref), (x_hbm, x_ref)]
    arrivals += [(gains_hbm, gains_ref), (place_hbm, place_ref)]
    for k in range(4):
        arrivals.append((block(weights_hbm, 4 + k), up_ref.at[k]))
        if k == 0:
            arrivals.append((dy_hbm, dy_ref))
        arrivals.append((block(weights_hbm, k), down_ref.at[k]))
    arrivals = [pltpu.make_async_copy(*pair, loads.at[i]) for i, pair in enumerate(arrivals)]
    for copy in arrivals:
        copy.start()
    departures = []

    def send(source, target):
        copy = pltpu.make_async_copy(source, target, stores.at[len(departures)])
        copy.start()
        departures.append(copy)

    for copy in arrivals[0:4]:
        copy.wait()
    gain, bias = gains_ref[2:3], gains_ref[3:4]
    w_out = out_ref[...].reshape(768, 768)
    first = x_ref[...].astype(F32) + dot(att_ref[...], w_out)
    hat, scale = normalize(first)
    acc_scr[...] = first
    arrivals[4].wait()
    n2 = dot((hat * gain + bias).astype(BF), place_ref[...]).astype(BF)
    n2t = n2.T
    waiting = arrivals[5:]
    for k in range(4):
        waiting.pop(0).wait()
        up = up_ref[k].reshape(768, 768)
        hidden = dot(n2, up)
        if k == 0:
            waiting.pop(0).wait()
        waiting.pop(0).wait()
        down = down_ref[k].reshape(768, 768)
        dy = dy_ref[...]
        d_active = dot(dy, down, NT)
        square = hidden * hidden
        tanh = jnp.tanh(GELU_SCALE * hidden * (1.0 + 0.044715 * square))
        share = 0.5 + 0.5 * tanh
        active = (hidden * share).astype(BF)
        slope = share + 0.5 * hidden * (1.0 - tanh * tanh) * (
            GELU_SCALE * (1.0 + (3 * 0.044715) * square)
        )
        d_hidden = (slope * d_active).astype(BF)
        gdown[k] = dot(active.T, dy).astype(BF).reshape(16, 48, 768)
        send(gdown.at[k], block(grads_hbm, k))
        gup[k] = dot(n2t, d_hidden).astype(BF).reshape(16, 48, 768)
        send(gup.at[k], block(grads_hbm, 4 + k))
        acc_scr[...] += dot(active, down)
        d_n2 = dot(d_hidden, up, NT)
        dn_scr[...] = d_n2 if k == 0 else dn_scr[...] + d_n2
    y_ref[...] = acc_scr[...].astype(BF)
    send(y_ref, y_hbm)
    dn = dot(dn_scr[...].astype(BF), place_ref[...], NT)
    t = dn * gain
    part = t - jnp.mean(t, -1, keepdims=True) - hat * jnp.mean(t * hat, -1, keepdims=True)
    d_first = dy_ref[...].astype(F32) + part * scale
    low = d_first.astype(BF)
    low_ref[...] = low
    send(low_ref, low_hbm)
    dfirst_ref[...] = d_first
    send(dfirst_ref, dfirst_hbm)
    d_att = dot(w_out, low, NT).astype(BF)
    d_att = dot(place_ref[...], d_att).astype(BF)
    for b in range(2):
        for e in range(4):
            datt_ref[2 * e + b] = d_att[e * 192 : (e + 1) * 192, b * 128 : (b + 1) * 128]
    send(datt_ref, datt_hbm)
    dgain_ref[0:1, :] = jnp.sum(dn * hat, axis=0, keepdims=True)
    dgain_ref[1:2, :] = jnp.sum(dn, axis=0, keepdims=True)
    dgain_ref[2:8, :] = jnp.zeros((6, 768), F32)
    send(dgain_ref, dgain_hbm)
    for copy in departures:
        copy.wait()


def out_kernel(attended_t_ref, low_ref, grad_ref):
    grad = dot(attended_t_ref[...], low_ref[...]).reshape(8, 2, 2, 24, 768)
    half = lax.axis_index("batch") // 4
    for j in range(8):
        rows = [
            jnp.where(half == z, grad[j, c, z], grad[j ^ 1, c, z]) for c in range(2) for z in range(2)
        ]
        grad_ref[j] = jnp.concatenate(rows, axis=0).astype(BF)


def whole(*dims):
    return pl.BlockSpec(dims, lambda *_: (0,) * len(dims))


def feed(*arrays):
    outs = [
        shape((256, 768), BF), shape((256, 768), F32), shape((256, 768), BF),
        shape((8, 192, 128), BF), shape((8, 768), F32), shape((16, 384, 768), BF),
    ]
    blocks = pltpu.VMEM((4, 16, 48, 768), BF)
    held = [pltpu.VMEM(a.shape, a.dtype) for a in arrays[:-1]]
    held += [blocks, blocks, pltpu.VMEM((16, 48, 768), BF)]
    held += [pltpu.VMEM(o.shape, o.dtype) for o in outs[:-1]]
    held += [blocks, blocks] + [pltpu.VMEM((256, 768), F32)] * 2
    held += [pltpu.SemaphoreType.DMA((14,)), pltpu.SemaphoreType.DMA((13,))]
    return call(
        feed_kernel,
        outs,
        arrays,
        15,
        held,
        in_specs=[pl.BlockSpec(memory_space=pl.ANY)] * len(arrays),
        out_specs=[pl.BlockSpec(memory_space=pl.ANY)] * len(outs),
    )


def unproject_kernel(
    own_ref, dq_ref, dkv_ref, partner_ref, normed_ref, wt_ref, dgain_ref, order_ref,
    out_ref, spread_ref,
    part_ref, mine_ref, theirs_ref, dt_scr, dw_scr, p_scr, o_scr,
):
    dt_scr[0:192, :] = dq_ref[...]
    dt_scr[192:576, :] = (dkv_ref[...].astype(F32) + partner_ref[...].astype(F32)).astype(BF)
    bias_sum = jnp.zeros((1, 768), F32)
    gain_sum = jnp.zeros((1, 768), F32)
    for j in range(4):
        d_normed = dot(dt_scr[:, j * 256 : (j + 1) * 256].T, wt_ref[...])
        part_ref[2 * j : 2 * j + 2] = d_normed.astype(BF).reshape(2, 128, 768)
        pair = jnp.concatenate([own_ref[2 * j, 0:128, :], own_ref[2 * j + 1, 0:128, :]], axis=0)
        hat, _ = normalize(pair.astype(F32))
        gain_sum += jnp.sum(d_normed * hat, axis=0, keepdims=True)
        bias_sum += jnp.sum(d_normed, axis=0, keepdims=True)
    dw_scr[0:576, :] = dot(dt_scr[...], normed_ref[...])
    dw_scr[576:577, :] = gain_sum
    dw_scr[577:578, :] = bias_sum
    dw_scr[578:580, :] = dgain_ref[0:2, :]
    dw_scr[580:640, :] = jnp.zeros((60, 768), F32)
    p_scr[...] = dot(dw_scr[...].astype(BF), places(order_ref[...])).T.astype(BF)
    out = jnp.zeros((96, 768), F32)
    for j in range(8):
        out += out_ref[j].astype(F32)
    lanes = lax.broadcasted_iota(jnp.int32, (128, 96), 1)
    spread = jnp.where(lanes == spread_ref[...], 1.0, 0.0).astype(BF)
    o_scr[...] = dot(spread, out.astype(BF))
    for dc, ref in enumerate((mine_ref, theirs_ref)):
        for dx in range(4):
            for dz in range(2):
                ref[dx, dz, :, 0:640] = p_scr[rows_at(dc, dz, dx), :]
                few = o_scr[rows_at(dc, dz, dx, 8), :]
                ref[dx, dz, :, 640:768] = jnp.concatenate(
                    [few[:, q * 128 : (q + 1) * 128] for q in range(6)], axis=0
                ).astype(BF)


def slots_kernel(rest_ref, qkv_ref, order_ref, out_ref, r_scr):
    r_scr[0:384, :] = rest_ref[...]
    r_scr[384:432, :] = jnp.zeros((48, 768), BF)
    r_scr[432:480, 0:640] = qkv_ref[:, 0:640]
    r_scr[432:480, 640:768] = jnp.zeros((48, 128), BF)
    r_scr[480:512, :] = jnp.zeros((32, 768), BF)
    out_ref[...] = dot(places(order_ref[...]), r_scr[...]).astype(BF).reshape(8, 64, 768)


def finish_kernel(x_ref, dfirst_ref, gains_ref, got_ref, qkv_ref, dtok_ref, out_ref):
    for q in range(6):
        out_ref[:, q * 128 : (q + 1) * 128] = qkv_ref[q * 8 : q * 8 + 8, 640:768].astype(F32)[0:6]
    gain = gains_ref[0:1]
    for b in range(2):
        rows = slice(b * 128, (b + 1) * 128)
        dn = jnp.zeros((128, 768), F32)
        for e in range(4):
            dn += got_ref[2 * e + b].astype(F32)
        hat, scale = normalize(x_ref[rows, :].astype(F32))
        t = dn * gain
        part = t - jnp.mean(t, -1, keepdims=True) - hat * jnp.mean(t * hat, -1, keepdims=True)
        dtok_ref[rows, :] = (dfirst_ref[rows, :] + part * scale).astype(BF)


def sums_kernel(got_ref, units_ref, down_ref, up_ref, qkv_ref, g1_ref, b1_ref, g2_ref, b2_ref):
    total = jnp.zeros((64, 768), F32)
    chunks = []
    for e in range(4):
        both = got_ref[2 * e].astype(F32) + got_ref[2 * e + 1].astype(F32)
        chunks.append(both[54:60])
        total += both
    down_ref[...] = total[0:24]
    left, up, units = total[30:54], jnp.zeros((24, 768), F32), places(units_ref[...])
    for _ in range(3):
        piece = left.astype(BF)
        left = left - piece.astype(F32)
        up += dot(piece, units, NT)
    for k in range(4):
        up_ref[:, k * 768 : (k + 1) * 768] = up[k * 6 : k * 6 + 6]
    for s in range(3):
        qkv_ref[:, s * 768 : (s + 1) * 768] = jnp.concatenate(
            [chunks[e][:, s * 192 : (s + 1) * 192] for e in range(4)], axis=1
        )
    norms = total[:, 512:640].T
    for i, ref in enumerate((g1_ref, b1_ref, g2_ref, b2_ref)):
        ref[...] = norms[64 + i : 65 + i, 54:60]


def scalars(count):
    return dict(
        in_specs=[pl.BlockSpec(memory_space=pltpu.SMEM)]
        + [pl.BlockSpec(memory_space=pltpu.VMEM)] * (count - 1)
    )


def body(tokens, lengths, gain_one, bias_one, w_qkv, w_out, gain_two, bias_two, w_up, w_down, d_out):
    order, units, regroup, qkv_order = (
        jnp.asarray(v) for v in (ROW_ORDER, UNIT_ORDER, REGROUP, QKV_ORDER)
    )
    exchange = functools.partial(
        lax.all_to_all, axis_name="seq", split_axis=0, concat_axis=0, tiled=True,
        axis_index_groups=SAME_CORE,
    )

    vectors = [v.reshape(1, 6) for v in (gain_one, bias_one, gain_two, bias_two)]
    slots, raw = pl.pallas_call(
        pack_kernel,
        grid=(1,),
        in_specs=[whole(24, 768), whole(6, 768), whole(6, 3072), whole(6, 2304)]
        + [whole(1, 6)] * 4
        + [whole(1, 768)],
        out_specs=[whole(8, 64, 768), whole(24, 640)],
        out_shape=[shape((8, 64, 768), BF), shape((24, 640), BF)],
        scratch_shapes=[
            pltpu.VMEM((64, 768), F32), pltpu.VMEM((128, 128), F32), pltpu.VMEM((24, 640), F32),
        ],
        cost_estimate=about(2),
        compiler_params=pltpu.CompilerParams(vmem_limit_bytes=60 * 1024 * 1024),
    )(w_down, w_out, w_up, w_qkv, *vectors, units)
    slots = exchange(slots)
    near = jnp.stack([raw] + [lax.ppermute(raw, "batch", along_x(step)) for step in (-1, 2, 1)])
    far = lax.ppermute(near, BOTH, SWAP_HALF)
    rest = call(
        regroup_kernel,
        shape((432, 768), BF),
        (slots, regroup, far),
        2,
        mib=12,
        in_specs=[pl.BlockSpec(memory_space=pltpu.VMEM)] * 2
        + [pl.BlockSpec(memory_space=pl.ANY)],
    )
    weights = lax.all_gather(rest, BOTH, axis=0, axis_index_groups=RINGS)
    x = tokens.transpose(1, 0, 2)
    dy = d_out.transpose(1, 0, 2).reshape(256, 768)
    sent = call(
        address_kernel,
        shape((8, 176, 768), BF),
        (x, near, far),
        2,
        [pltpu.VMEM((4, 48, 640), F32)],
        mib=16,
    )
    own = exchange(sent)
    other = lax.ppermute(own[:, 128:176, 0:640], "seq", SWAP_CORE)
    x = x.reshape(256, 768)

    normed, wt, gains, q_t, kv = call(
        project_kernel,
        [
            shape((1024, 768), BF), shape((576, 768), BF), shape((8, 768), F32),
            shape((192, 1024), BF), shape((384, 1024), BF),
        ],
        (own, other, jnp.asarray(ARRIVAL)),
        5,
        [pltpu.VMEM((768, 640), BF), pltpu.VMEM((640, 768), F32)],
        mib=30,
    )
    kv_other = lax.ppermute(kv, "seq", SWAP_CORE)
    o, o_low, lse = call(
        forward_kernel,
        [shape((192, 1024), F32), shape((8, 192, 128), BF), shape((3, 1024), F32)],
        (lengths, q_t, kv, kv_other),
        12,
        [
            pltpu.VMEM((192, 1024), BF), pltpu.VMEM((3, 2048, 64), BF),
            pltpu.VMEM((192, 2048), BF),
        ]
        + [pltpu.VMEM((256, 256), F32)] * 6
        + [pltpu.VMEM((256, 256), BF)] * 6
        + [pltpu.VMEM((64, 256), F32)] * 3
        + [pltpu.VMEM((8, 256), F32)] * 3,
        mib=30,
        **scalars(4),
    )
    att = exchange(o_low)
    place, attended, attended_t = call(
        prepare_kernel,
        [shape((768, 768), BF), shape((256, 768), BF), shape((768, 256), BF)],
        (att, order),
        2,
        mib=16,
    )
    y, d_first, low, d_att, d_gain, grads = feed(x, dy, attended, gains, place, weights)
    rest_sum = lax.psum_scatter(
        grads.reshape(16 * 384, 768), BOTH, scatter_dimension=0, tiled=True,
        axis_index_groups=RINGS,
    )
    d_att = exchange(d_att)
    out_grad = exchange(call(out_kernel, shape((8, 96, 768), BF), (attended_t, low), 2))
    dq, dkv, dkv_other = call(
        backward_kernel,
        [shape((192, 1024), BF), shape((384, 1024), BF), shape((384, 1024), BF)],
        (lengths, q_t, kv, kv_other, o, lse, d_att),
        20,
        [
            pltpu.VMEM((192, 1024), BF),
            pltpu.VMEM((3, 2048, 64), BF),
            pltpu.VMEM((192, 2048), BF),
            pltpu.VMEM((3, 2048, 64), BF),
            pltpu.VMEM((192, 1024), BF),
            pltpu.VMEM((3, 64, 2048), F32),
            pltpu.VMEM((3, 64, 2048), F32),
            pltpu.VMEM((3, 1024), F32),
        ]
        + [pltpu.VMEM((256, 256), F32)] * 12
        + [pltpu.VMEM((256, 256), BF)] * 12
        + [pltpu.VMEM((64, 256), F32)] * 3,
        mib=60,
        **scalars(7),
    )
    partner = lax.ppermute(dkv_other, "seq", SWAP_CORE)
    part, mine, theirs = call(
        unproject_kernel,
        [shape((8, 128, 768), BF), shape((4, 2, 48, 768), BF), shape((4, 2, 48, 768), BF)],
        (own, dq, dkv, partner, normed, wt, d_gain, qkv_order, out_grad, jnp.asarray(SPREAD)),
        7,
        [
            pltpu.VMEM((576, 1024), BF), pltpu.VMEM((640, 768), F32),
            pltpu.VMEM((768, 640), BF), pltpu.VMEM((128, 768), F32),
        ],
        mib=60,
    )
    add = lambda *parts: sum(p.astype(F32) for p in parts).astype(BF)
    line = add(mine, lax.ppermute(theirs, "seq", SWAP_CORE))
    line = add(
        line[0],
        lax.ppermute(line[1], "batch", along_x(1)),
        lax.ppermute(line[2], "batch", along_x(2)),
        lax.ppermute(line[3], "batch", along_x(-1)),
    )
    qkv_sum = add(line[0], lax.ppermute(line[1], BOTH, SWAP_HALF))
    back = exchange(part)
    d_tokens, d_out_w = call(
        finish_kernel,
        [shape((256, 768), BF), shape((6, 768), F32)],
        (x, d_first, gains, back, qkv_sum),
        3,
        mib=16,
    )
    slots = call(
        slots_kernel,
        shape((8, 64, 768), BF),
        (rest_sum, qkv_sum, regroup),
        2,
        [pltpu.VMEM((512, 768), BF)],
        mib=12,
    )
    slots = exchange(slots)
    vector = shape((1, 6), F32)
    d_down, d_up, d_qkv, *norms = call(
        sums_kernel,
        [shape((24, 768), F32), shape((6, 3072), F32), shape((6, 2304), F32)]
        + [vector] * 4,
        (slots, units),
        2,
        mib=12,
    )
    norms = [v.reshape(6) for v in norms]
    output = y.reshape(2, 128, 768).transpose(1, 0, 2)
    d_tokens = d_tokens.reshape(2, 128, 768).transpose(1, 0, 2)
    return (
        output, d_tokens, norms[0], norms[1], d_qkv, d_out_w, norms[2], norms[3], d_up, d_down,
    )


def solution(mesh):
    rows = P(("seq", "batch"))
    tokens = P("seq", "batch", None)
    return jax.shard_map(
        body,
        mesh=mesh,
        in_specs=(tokens, P("batch"), rows, rows, rows, rows, rows, rows, rows, rows, tokens),
        out_specs=(tokens, tokens, rows, rows, rows, rows, rows, rows, rows, rows),
        check_vma=False,
    )
```

```python
import functools
import math

import jax
import jax.numpy as jnp
import numpy as np
from jax import lax
from jax.experimental import pallas as pl
from jax.experimental.pallas import tpu as pltpu
from jax.sharding import PartitionSpec as P

H = 12
HD = 64
EPSILON = 1e-05
BF = jnp.bfloat16
F32 = jnp.float32
BOTH = ("seq", "batch")
SAME_CORE = [[2 * k + c for k in range(8)] for c in range(2)]
SWAP_CORE = [(i, i ^ 1) for i in range(16)]
TURNS = [(0, 0), (0, 1), (0, 2), (0, 3), (1, 3), (1, 2), (1, 1), (1, 0)]
RING = [(c, z, x) for z, x in TURNS for c in range(2)]


RINGS = [
    [((y * 2 + (low ^ z)) * 2 + c) * 8 + z * 4 + x for c, z, x in RING]
    for y in range(4)
    for low in range(2)
]
SWAP_HALF = [(s * 8 + b, (s ^ 2) * 8 + (b ^ 4)) for s in range(16) for b in range(8)]


def along_x(step):
    return [(b, b // 4 * 4 + (b + step) % 4) for b in range(8)]


def in_order(outer, size):
    natural = np.arange(outer * 16 * size, dtype=np.int32).reshape(outer, 2, 8, size)
    return np.stack([natural[:, c, z * 4 + x] for c, z, x in RING]).reshape(1, -1)


QKV_ORDER = (
    np.arange(768, dtype=np.int32).reshape(8, 2, 8, 6).transpose(1, 2, 0, 3).reshape(1, 768)
)
ROW_ORDER = in_order(8, 6)
UNIT_ORDER = in_order(2, 24)


def regroup_order():
    slot = np.arange(448, dtype=np.int32).reshape(8, 56)
    parts = [slot[:, 0:24]] + [slot[:, f : f + 6] for f in (24, 30, 36, 42, 48)]
    return np.concatenate([p.reshape(-1) for p in parts] + [np.full(80, -1, np.int32)])[None]


REGROUP = regroup_order()


def arrival_places():
    s, j, dz, dx, r = np.indices((2, 8, 2, 4, 6), dtype=np.int32).reshape(5, 768)
    return np.stack([j ^ dz, s, dz, dx, r] + [np.zeros_like(r)] * 3)


ARRIVAL = arrival_places()
SPREAD = np.concatenate(
    [np.arange(96, dtype=np.int32).reshape(16, 6), np.full((16, 2), -1, np.int32)], axis=1
).reshape(128, 1)


def places(order, count=None):
    size = order.shape[1]
    rows = lax.broadcasted_iota(jnp.int32, (count or size, size), 0)
    return jnp.where(rows == order, 1.0, 0.0).astype(BF)


NT = (((1,), (1,)), ((), ()))
NN = (((1,), (0,)), ((), ()))
TN = (((0,), (0,)), ((), ()))


def dot(left, right, dims=NN):
    return lax.dot_general(left, right, dims, preferred_element_type=F32)


def about(us):
    return pl.CostEstimate(flops=int(us * 1.1e9), bytes_accessed=0, transcendentals=0)


def call(kernel, outs, ins, us, scratch=(), mib=60, **kwargs):
    return pl.pallas_call(
        kernel,
        out_shape=outs,
        scratch_shapes=list(scratch),
        cost_estimate=about(us),
        compiler_params=pltpu.CompilerParams(vmem_limit_bytes=mib * 1024 * 1024),
        **kwargs,
    )(*ins)


def shape(dims, dtype):
    return jax.ShapeDtypeStruct(dims, dtype)


def normalize(values):
    center = jnp.mean(values, axis=-1, keepdims=True)
    shifted = values - center
    spread = jnp.mean(shifted * shifted, axis=-1, keepdims=True)
    scale = lax.rsqrt(spread + EPSILON)
    return shifted * scale, scale


def pack_kernel(
    down_ref, out_ref, up_ref, qkv_ref, g1_ref, b1_ref, g2_ref, b2_ref, units_ref,
    slot_ref, raw_ref, scr, turn_scr, raw_scr,
):
    turn_scr[...] = jnp.zeros_like(turn_scr)
    for i, ref in enumerate((g1_ref, b1_ref, g2_ref, b2_ref)):
        turn_scr[64 + i : 65 + i, 0:6] = ref[...].astype(F32)
    norms = turn_scr[...].T[0:6, 64:128].astype(BF)
    up = jnp.concatenate(
        [up_ref[:, k * 768 : (k + 1) * 768].astype(F32) for k in range(4)], axis=0
    ).astype(BF)
    scr[0:24, :] = down_ref[...].astype(F32)
    scr[24:48, :] = dot(up, places(units_ref[...]))
    scr[48:54, :] = out_ref[...].astype(F32)
    scr[54:56, :] = jnp.zeros((2, 768), F32)
    slot = scr[...].astype(BF)
    for j in range(8):
        slot_ref[j] = slot
    for e in range(4):
        parts = [qkv_ref[:, s * 768 + e * 192 : s * 768 + (e + 1) * 192] for s in range(3)]
        row = jnp.concatenate(parts + [norms], axis=1)
        raw_scr[e * 6 : e * 6 + 6, :] = row.astype(F32)
    raw_ref[...] = raw_scr[...].astype(BF)


def regroup_kernel(slots_ref, order_ref, far_ref, rest_ref, scr):
    for j in range(8):
        scr[j * 56 : j * 56 + 56, :] = slots_ref[j].astype(F32)
    rows = dot(places(order_ref[...], 448), scr[...].astype(BF), TN).astype(BF)
    rest_ref[...] = rows[0:432]


def address_kernel(x_ref, near_ref, far_ref, out_ref, scr):
    for e in range(4):
        for dz, ref in enumerate((near_ref, far_ref)):
            for dx in range(4):
                first = (dz * 4 + dx) * 6
                scr[e, first : first + 6, :] = ref[dx].astype(F32)[e * 6 : e * 6 + 6]
        for b in range(2):
            out_ref[2 * e + b, 0:128, :] = x_ref[b]
            out_ref[2 * e + b, 128:176, 0:640] = scr[e].astype(BF)
            out_ref[2 * e + b, 128:176, 640:768] = jnp.zeros((48, 128), BF)


def core_of():
    return lax.rem(lax.axis_index("seq"), 2)


def length_of(lengths_ref):
    return jnp.where(lax.rem(lax.axis_index("seq") // 2, 2) == 0, lengths_ref[0], lengths_ref[1])


def rows_at(dc, dz, dx, size=48):
    row = lax.axis_index("batch")
    c = lax.rem(core_of() + dc, 2)
    z = lax.rem(row // 4 + dz, 2)
    x = lax.rem(row + dx, 4)
    return pl.ds(pl.multiple_of((c * 8 + z * 4 + x) * size, size), size)


def project_kernel(
    own_ref, other_ref, arrival_ref,
    normed_ref, wt_ref, gains_ref, q_ref, kv_ref, w_scr, t_scr,
):
    for j in range(8):
        w_scr[j * 48 : j * 48 + 48, :] = own_ref[j, 128:176, 0:640]
        w_scr[384 + j * 48 : 432 + j * 48, :] = other_ref[j]
    core, row = core_of(), lax.axis_index("batch")
    half, column = row // 4, lax.rem(row, 4)
    table = [arrival_ref[i : i + 1, :] for i in range(5)]
    c = jnp.where(table[1] == 0, core, 1 - core)
    z = jnp.where(table[2] == 0, half, 1 - half)
    x = jnp.bitwise_and(table[3] + column, 3)
    order = ((table[0] * 2 + c) * 8 + z * 4 + x) * 6 + table[4]
    t_scr[...] = dot(w_scr[...].T, places(order), NT)
    wt_ref[...] = t_scr[0:576].astype(BF)
    gains = t_scr[576:584]
    gains_ref[...] = gains
    gain, bias = gains[0:1], gains[1:2]
    for j in range(8):
        hat, _ = normalize(own_ref[j, 0:128, :].astype(F32))
        normed_ref[j * 128 : (j + 1) * 128, :] = (hat * gain + bias).astype(BF)
    for j in range(4):
        lanes = slice(j * 256, (j + 1) * 256)
        qkv = dot(wt_ref[...], normed_ref[lanes, :], NT).astype(BF)
        q_ref[:, lanes] = qkv[0:192]
        kv_ref[:, lanes] = qkv[192:576]


def last_keys(m, core, length):
    lane = lax.broadcasted_iota(jnp.int32, (1, 256), 1)
    query = m * 512 + 128 * core + jnp.where(lane < 128, lane, lane + 128)
    return jnp.minimum(query, length - 1)


def allowed(start, first, last, core):
    offset = start + first + (128 * core if first < 128 else -128 * core)
    return lax.broadcasted_iota(jnp.int32, (64, 256), 0) <= last - offset


def fill_keys(own_ref, other_ref, k_scr, base):
    for u in range(3):
        for j in range(8):
            rows, lanes = pl.ds(base + u * 64, 64), pl.ds(j * 128, 128)
            k_scr[u, j * 256 : j * 256 + 128, :] = own_ref[rows, lanes].T
            k_scr[u, j * 256 + 128 : j * 256 + 256, :] = other_ref[rows, lanes].T


def fill_lanes(own_ref, other_ref, scr, base):
    for j in range(8):
        scr[:, j * 256 : j * 256 + 128] = own_ref[base : base + 192, j * 128 : j * 128 + 128]
        scr[:, j * 256 + 128 : j * 256 + 256] = other_ref[
            base : base + 192, j * 128 : j * 128 + 128
        ]


PAIRS = [(h, u) for h in range(2) for u in range(3)]
CHUNKS = [slice(i * 64, i * 64 + 64) for i in range(4)]


def steps(m, length):
    return jnp.minimum(m + 1, (length + 511) // 512)


def sweep(length, begin, score, step, finish):
    def one(_, place):
        m, jk = place
        more = jk + 1 < steps(m, length)
        next_m = jnp.where(more, m, jnp.minimum(m + 1, 3))
        next_jk = jnp.where(more, jk + 1, 0)

        @pl.when(jk == 0)
        def _():
            begin()

        edge = (jk == m) | (jk * 512 + 512 > length)

        @pl.when(edge)
        def _():
            step(m, jk, next_m, next_jk, True)

        @pl.when(jnp.logical_not(edge))
        def _():
            step(m, jk, next_m, next_jk, False)

        @pl.when(jnp.logical_not(more))
        def _():
            finish(m)

        return jnp.where(more, m, m + 1), next_jk

    for h, u in PAIRS:
        score(h, u, 0, 0)
    total = sum(steps(m, length) for m in range(4))
    lax.fori_loop(0, total, one, (jnp.int32(0), jnp.int32(0)))


def group(m):
    return pl.ds(pl.multiple_of(m * 256, 256), 256)


def key_tile(jk, h):
    return pl.ds(pl.multiple_of(jk * 512, 512) + h * 256, 256)


def forward_plain(q_scr, k_scr, v_scr, scratch, length, core, finish):
    s_scr, w_scr, acc_scr, sum_scr = scratch[0:6], scratch[6:12], scratch[12:15], scratch[15:18]

    def begin():
        for u in range(3):
            acc_scr[u][...] = jnp.zeros((64, 256), F32)
            sum_scr[u][...] = jnp.zeros((8, 256), F32)

    def score(h, u, m, jk):
        queries = q_scr[u * 64 : (u + 1) * 64, group(m)]
        s_scr[h * 3 + u][...] = dot(k_scr[u, key_tile(jk, h), :], queries)

    def step(m, jk, next_m, next_jk, masked):
        last = last_keys(m, core, length)
        for h, u in PAIRS:
            scores, weights = s_scr[h * 3 + u], w_scr[h * 3 + u]
            total = sum_scr[u][...]
            for rows in CHUNKS:
                s = scores[rows, :]
                t = s * s + 1.0
                r = lax.rsqrt(t)
                e = jnp.exp(t * r)
                if masked:
                    e = jnp.where(allowed(jk * 512 + h * 256, rows.start, last, core), e, 0.0)
                total = total + jnp.sum(e.reshape(8, 8, 256), axis=0)
                weights[rows, :] = (s * r * e).astype(BF)
            sum_scr[u][...] = total
            score(h, u, next_m, next_jk)
            acc_scr[u][...] += dot(v_scr[u * 64 : (u + 1) * 64, key_tile(jk, h)], weights[...])

    def close(m):
        for u in range(3):
            total = jnp.sum(sum_scr[u][...], axis=0, keepdims=True)
            finish(m, u, acc_scr[u][...], total, jnp.zeros((1, 256), F32))

    sweep(length, begin, score, step, close)


def forward_any(q_scr, k_scr, v_scr, length, core, finish):
    def one(m, _):
        last = last_keys(m, core, length)

        def step(jk, carry):
            start = pl.multiple_of(jk * 256, 256)
            mask = jnp.concatenate([allowed(start, r.start, last, core) for r in CHUNKS], axis=0)
            out = []
            for u in range(3):
                top, total, accum = carry[u]
                s = dot(k_scr[u, pl.ds(start, 256), :], q_scr[u * 64 : (u + 1) * 64, group(m)])
                t = s * s + 1.0
                r = lax.rsqrt(t)
                a = jnp.where(mask, t * r, -1e30)
                fresh = jnp.maximum(top, jnp.max(a, axis=0, keepdims=True))
                e = jnp.exp(a - fresh)
                rescale = jnp.exp(top - fresh)
                total = total * rescale + jnp.sum(e, axis=0, keepdims=True)
                accum = accum * rescale + dot(
                    v_scr[u * 64 : (u + 1) * 64, pl.ds(start, 256)], (s * r * e).astype(BF)
                )
                out.append((fresh, total, accum))
            return tuple(out)

        zero = (jnp.zeros((1, 256), F32), jnp.zeros((1, 256), F32), jnp.zeros((64, 256), F32))
        carry = lax.fori_loop(0, 2 * steps(m, length), step, (zero,) * 3)
        for u in range(3):
            finish(m, u, carry[u][2], carry[u][1], carry[u][0])
        return 0

    lax.fori_loop(0, 4, one, 0)


def forward_kernel(
    lengths_ref, q_ref, own_ref, other_ref, o_ref, low_ref, lse_ref, q_scr, k_scr, v_scr, *scratch
):
    length, core = length_of(lengths_ref), core_of()
    fill_keys(own_ref, other_ref, k_scr, 0)
    fill_lanes(own_ref, other_ref, v_scr, 192)
    q_scr[...] = q_ref[...] * BF(0.125)

    def finish(m, u, accum, total, top):
        lanes = group(m)
        o = accum / total
        o_ref[u * 64 : (u + 1) * 64, lanes] = o
        for half in range(2):
            low_ref[2 * m + half, u * 64 : (u + 1) * 64, :] = o[
                :, half * 128 : half * 128 + 128
            ].astype(BF)
        lse_ref[u : u + 1, lanes] = top + jnp.log(total)

    def largest(ref):
        values = ref[0:192, :].astype(F32)
        return jnp.max(jnp.sum((values * values).reshape(3, 64, 1024), axis=1))

    bound = largest(q_ref) * jnp.maximum(largest(own_ref), largest(other_ref)) * (1.0 / 64.0)
    small = bound < 3600.0

    @pl.when(small)
    def _():
        forward_plain(q_scr, k_scr, v_scr, scratch, length, core, finish)

    @pl.when(jnp.logical_not(small))
    def _():
        forward_any(q_scr, k_scr, v_scr, length, core, finish)


def backward_kernel(
    lengths_ref, q_ref, own_ref, other_ref, o_ref, lse_ref, da_ref,
    dq_ref, down_ref, dother_ref,
    q_scr, k_scr, kt_scr, v_scr, da_scr, dk_scr, dv_scr, delta_scr, *scratch,
):
    s_scr, dp_scr, w_scr, ds_scr, dq_scr = (scratch[i : i + 6] for i in (0, 6, 12, 18, 24))
    length, core = length_of(lengths_ref), core_of()
    fill_keys(own_ref, other_ref, k_scr, 0)
    fill_lanes(own_ref, other_ref, kt_scr, 0)
    fill_keys(own_ref, other_ref, v_scr, 192)
    q_scr[...] = q_ref[...] * BF(0.125)
    for j in range(8):
        lanes = slice(j * 128, (j + 1) * 128)
        da_scr[:, lanes] = da_ref[j]
        for u in range(3):
            rows = slice(u * 64, (u + 1) * 64)
            delta_scr[u : u + 1, lanes] = jnp.sum(
                da_ref[j, rows, :].astype(F32) * o_ref[rows, lanes], axis=0, keepdims=True
            )
    dk_scr[...] = jnp.zeros_like(dk_scr)
    dv_scr[...] = jnp.zeros_like(dv_scr)

    def begin():
        for u in range(3):
            dq_scr[u][...] = jnp.zeros((64, 256), F32)

    def score(h, u, m, jk):
        rows, tile = slice(u * 64, (u + 1) * 64), key_tile(jk, h)
        s_scr[h * 3 + u][...] = dot(k_scr[u, tile, :], q_scr[rows, group(m)])
        dp_scr[h * 3 + u][...] = dot(v_scr[u, tile, :], da_scr[rows, group(m)])

    def step(m, jk, next_m, next_jk, masked):
        last = last_keys(m, core, length)
        for h, u in PAIRS:
            tile = key_tile(jk, h)
            heads = slice(u * 64, (u + 1) * 64)
            delta, lse = delta_scr[u : u + 1, group(m)], lse_ref[u : u + 1, group(m)]
            place = h * 3 + u
            for rows in CHUNKS:
                s = s_scr[place][rows, :]
                t = s * s + 1.0
                r = lax.rsqrt(t)
                p = jnp.exp(t * r - lse)
                if masked:
                    p = jnp.where(allowed(jk * 512 + h * 256, rows.start, last, core), p, 0.0)
                g = s * r
                w_scr[place][rows, :] = (g * p).astype(BF)
                ds = p * (dp_scr[place][rows, :] * (r * r * (r - 1.0) + 1.0) - g * delta)
                ds_scr[place][rows, :] = ds.astype(BF)
            score(h, u, next_m, next_jk)
            dv_scr[u, :, tile] += dot(da_scr[heads, group(m)], w_scr[place][...], NT)
            dk_scr[u, :, tile] += dot(q_scr[heads, group(m)], ds_scr[place][...], NT)
            dq_scr[u][...] += dot(kt_scr[heads, tile], ds_scr[place][...])

    def close(m):
        for u in range(3):
            dq_ref[u * 64 : (u + 1) * 64, group(m)] = (dq_scr[u][...] * 0.125).astype(BF)

    sweep(length, begin, score, step, close)
    for scr, base in ((dk_scr, 0), (dv_scr, 192)):
        for u in range(3):
            rows = pl.ds(base + u * 64, 64)
            for j in range(8):
                lanes = pl.ds(j * 128, 128)
                down_ref[rows, lanes] = scr[u, :, j * 256 : j * 256 + 128].astype(BF)
                dother_ref[rows, lanes] = scr[u, :, j * 256 + 128 : j * 256 + 256].astype(BF)


GELU_SCALE = math.sqrt(2.0 / math.pi)


def prepare_kernel(att_ref, order_ref, place_ref, attended_ref, attended_t_ref):
    place_ref[...] = places(order_ref[...])
    for b in range(2):
        for e in range(4):
            attended_t_ref[e * 192 : (e + 1) * 192, b * 128 : (b + 1) * 128] = att_ref[2 * e + b]
    attended_ref[...] = dot(attended_t_ref[...].T, place_ref[...]).astype(BF)


def feed_kernel(
    x_hbm, dy_hbm, att_hbm, gains_hbm, place_hbm, weights_hbm,
    y_hbm, dfirst_hbm, low_hbm, datt_hbm, dgain_hbm, grads_hbm,
    x_ref, dy_ref, att_ref, gains_ref, place_ref, down_ref, up_ref, out_ref,
    y_ref, dfirst_ref, low_ref, datt_ref, dgain_ref, gdown, gup, acc_scr, dn_scr, loads, stores,
):
    def block(ref, number):
        return ref.at[:, pl.ds(48 * number, 48), :]

    arrivals = [(att_hbm, att_ref), (block(weights_hbm, 8), out_ref), (x_hbm, x_ref)]
    arrivals += [(gains_hbm, gains_ref), (place_hbm, place_ref)]
    for k in range(4):
        arrivals.append((block(weights_hbm, 4 + k), up_ref.at[k]))
        if k == 0:
            arrivals.append((dy_hbm, dy_ref))
        arrivals.append((block(weights_hbm, k), down_ref.at[k]))
    arrivals = [pltpu.make_async_copy(*pair, loads.at[i]) for i, pair in enumerate(arrivals)]
    for copy in arrivals:
        copy.start()
    departures = []

    def send(source, target):
        copy = pltpu.make_async_copy(source, target, stores.at[len(departures)])
        copy.start()
        departures.append(copy)

    for copy in arrivals[0:4]:
        copy.wait()
    gain, bias = gains_ref[2:3], gains_ref[3:4]
    w_out = out_ref[...].reshape(768, 768)
    first = x_ref[...].astype(F32) + dot(att_ref[...], w_out)
    hat, scale = normalize(first)
    acc_scr[...] = first
    arrivals[4].wait()
    n2 = dot((hat * gain + bias).astype(BF), place_ref[...]).astype(BF)
    n2t = n2.T
    waiting = arrivals[5:]
    for k in range(4):
        waiting.pop(0).wait()
        up = up_ref[k].reshape(768, 768)
        hidden = dot(n2, up)
        if k == 0:
            waiting.pop(0).wait()
        waiting.pop(0).wait()
        down = down_ref[k].reshape(768, 768)
        dy = dy_ref[...]
        d_active = dot(dy, down, NT)
        square = hidden * hidden
        tanh = jnp.tanh(GELU_SCALE * hidden * (1.0 + 0.044715 * square))
        share = 0.5 + 0.5 * tanh
        active = (hidden * share).astype(BF)
        slope = share + 0.5 * hidden * (1.0 - tanh * tanh) * (
            GELU_SCALE * (1.0 + (3 * 0.044715) * square)
        )
        d_hidden = (slope * d_active).astype(BF)
        gdown[k] = dot(active.T, dy).astype(BF).reshape(16, 48, 768)
        send(gdown.at[k], block(grads_hbm, k))
        gup[k] = dot(n2t, d_hidden).astype(BF).reshape(16, 48, 768)
        send(gup.at[k], block(grads_hbm, 4 + k))
        acc_scr[...] += dot(active, down)
        d_n2 = dot(d_hidden, up, NT)
        dn_scr[...] = d_n2 if k == 0 else dn_scr[...] + d_n2
    y_ref[...] = acc_scr[...].astype(BF)
    send(y_ref, y_hbm)
    dn = dot(dn_scr[...].astype(BF), place_ref[...], NT)
    t = dn * gain
    part = t - jnp.mean(t, -1, keepdims=True) - hat * jnp.mean(t * hat, -1, keepdims=True)
    d_first = dy_ref[...].astype(F32) + part * scale
    low = d_first.astype(BF)
    low_ref[...] = low
    send(low_ref, low_hbm)
    dfirst_ref[...] = d_first
    send(dfirst_ref, dfirst_hbm)
    d_att = dot(w_out, low, NT).astype(BF)
    d_att = dot(place_ref[...], d_att).astype(BF)
    for b in range(2):
        for e in range(4):
            datt_ref[2 * e + b] = d_att[e * 192 : (e + 1) * 192, b * 128 : (b + 1) * 128]
    send(datt_ref, datt_hbm)
    dgain_ref[0:1, :] = jnp.sum(dn * hat, axis=0, keepdims=True)
    dgain_ref[1:2, :] = jnp.sum(dn, axis=0, keepdims=True)
    dgain_ref[2:8, :] = jnp.zeros((6, 768), F32)
    send(dgain_ref, dgain_hbm)
    for copy in departures:
        copy.wait()


def out_kernel(attended_t_ref, low_ref, grad_ref):
    grad = dot(attended_t_ref[...], low_ref[...]).reshape(8, 2, 2, 24, 768)
    half = lax.axis_index("batch") // 4
    for j in range(8):
        rows = [
            jnp.where(half == z, grad[j, c, z], grad[j ^ 1, c, z]) for c in range(2) for z in range(2)
        ]
        grad_ref[j] = jnp.concatenate(rows, axis=0).astype(BF)


def whole(*dims):
    return pl.BlockSpec(dims, lambda *_: (0,) * len(dims))


def feed(*arrays):
    outs = [
        shape((256, 768), BF), shape((256, 768), F32), shape((256, 768), BF),
        shape((8, 192, 128), BF), shape((8, 768), F32), shape((16, 384, 768), BF),
    ]
    blocks = pltpu.VMEM((4, 16, 48, 768), BF)
    held = [pltpu.VMEM(a.shape, a.dtype) for a in arrays[:-1]]
    held += [blocks, blocks, pltpu.VMEM((16, 48, 768), BF)]
    held += [pltpu.VMEM(o.shape, o.dtype) for o in outs[:-1]]
    held += [blocks, blocks] + [pltpu.VMEM((256, 768), F32)] * 2
    held += [pltpu.SemaphoreType.DMA((14,)), pltpu.SemaphoreType.DMA((13,))]
    return call(
        feed_kernel,
        outs,
        arrays,
        15,
        held,
        in_specs=[pl.BlockSpec(memory_space=pl.ANY)] * len(arrays),
        out_specs=[pl.BlockSpec(memory_space=pl.ANY)] * len(outs),
    )


def unproject_kernel(
    own_ref, dq_ref, dkv_ref, partner_ref, normed_ref, wt_ref, dgain_ref, order_ref,
    out_ref, spread_ref,
    part_ref, mine_ref, theirs_ref, dt_scr, dw_scr, p_scr, o_scr,
):
    dt_scr[0:192, :] = dq_ref[...]
    dt_scr[192:576, :] = (dkv_ref[...].astype(F32) + partner_ref[...].astype(F32)).astype(BF)
    bias_sum = jnp.zeros((1, 768), F32)
    gain_sum = jnp.zeros((1, 768), F32)
    for j in range(4):
        d_normed = dot(dt_scr[:, j * 256 : (j + 1) * 256].T, wt_ref[...])
        part_ref[2 * j : 2 * j + 2] = d_normed.astype(BF).reshape(2, 128, 768)
        pair = jnp.concatenate([own_ref[2 * j, 0:128, :], own_ref[2 * j + 1, 0:128, :]], axis=0)
        hat, _ = normalize(pair.astype(F32))
        gain_sum += jnp.sum(d_normed * hat, axis=0, keepdims=True)
        bias_sum += jnp.sum(d_normed, axis=0, keepdims=True)
    dw_scr[0:576, :] = dot(dt_scr[...], normed_ref[...])
    dw_scr[576:577, :] = gain_sum
    dw_scr[577:578, :] = bias_sum
    dw_scr[578:580, :] = dgain_ref[0:2, :]
    dw_scr[580:640, :] = jnp.zeros((60, 768), F32)
    p_scr[...] = dot(dw_scr[...].astype(BF), places(order_ref[...])).T.astype(BF)
    out = jnp.zeros((96, 768), F32)
    for j in range(8):
        out += out_ref[j].astype(F32)
    lanes = lax.broadcasted_iota(jnp.int32, (128, 96), 1)
    spread = jnp.where(lanes == spread_ref[...], 1.0, 0.0).astype(BF)
    o_scr[...] = dot(spread, out.astype(BF))
    for dc, ref in enumerate((mine_ref, theirs_ref)):
        for dx in range(4):
            for dz in range(2):
                ref[dx, dz, :, 0:640] = p_scr[rows_at(dc, dz, dx), :]
                few = o_scr[rows_at(dc, dz, dx, 8), :]
                ref[dx, dz, :, 640:768] = jnp.concatenate(
                    [few[:, q * 128 : (q + 1) * 128] for q in range(6)], axis=0
                ).astype(BF)


def slots_kernel(rest_ref, qkv_ref, order_ref, out_ref, r_scr):
    r_scr[0:384, :] = rest_ref[...]
    r_scr[384:432, 0:640] = qkv_ref[:, 0:640]
    r_scr[384:432, 640:768] = jnp.zeros((48, 128), BF)
    r_scr[432:512, :] = jnp.zeros((80, 768), BF)
    rows = dot(places(order_ref[...], 448), r_scr[...])
    for j in range(8):
        out_ref[j] = rows[j * 56 : j * 56 + 56].astype(BF)


def finish_kernel(x_ref, dfirst_ref, gains_ref, got_ref, qkv_ref, dtok_ref, out_ref):
    for q in range(6):
        out_ref[:, q * 128 : (q + 1) * 128] = qkv_ref[q * 8 : q * 8 + 8, 640:768].astype(F32)[0:6]
    gain = gains_ref[0:1]
    for b in range(2):
        rows = slice(b * 128, (b + 1) * 128)
        dn = jnp.zeros((128, 768), F32)
        for e in range(4):
            dn += got_ref[2 * e + b].astype(F32)
        hat, scale = normalize(x_ref[rows, :].astype(F32))
        t = dn * gain
        part = t - jnp.mean(t, -1, keepdims=True) - hat * jnp.mean(t * hat, -1, keepdims=True)
        dtok_ref[rows, :] = (dfirst_ref[rows, :] + part * scale).astype(BF)


def sums_kernel(got_ref, units_ref, down_ref, up_ref, qkv_ref, g1_ref, b1_ref, g2_ref, b2_ref):
    total = jnp.zeros((56, 768), F32)
    chunks = []
    for e in range(4):
        both = got_ref[2 * e].astype(F32) + got_ref[2 * e + 1].astype(F32)
        chunks.append(both[48:54])
        total += both
    down_ref[...] = total[0:24]
    left, up, units = total[24:48], jnp.zeros((24, 768), F32), places(units_ref[...])
    for _ in range(3):
        piece = left.astype(BF)
        left = left - piece.astype(F32)
        up += dot(piece, units, NT)
    for k in range(4):
        up_ref[:, k * 768 : (k + 1) * 768] = up[k * 6 : k * 6 + 6]
    for s in range(3):
        qkv_ref[:, s * 768 : (s + 1) * 768] = jnp.concatenate(
            [chunks[e][:, s * 192 : (s + 1) * 192] for e in range(4)], axis=1
        )
    norms = total[:, 512:640].T
    for i, ref in enumerate((g1_ref, b1_ref, g2_ref, b2_ref)):
        ref[...] = norms[64 + i : 65 + i, 48:54]


def scalars(count):
    return dict(
        in_specs=[pl.BlockSpec(memory_space=pltpu.SMEM)]
        + [pl.BlockSpec(memory_space=pltpu.VMEM)] * (count - 1)
    )


def body(tokens, lengths, gain_one, bias_one, w_qkv, w_out, gain_two, bias_two, w_up, w_down, d_out):
    order, units, regroup, qkv_order = (
        jnp.asarray(v) for v in (ROW_ORDER, UNIT_ORDER, REGROUP, QKV_ORDER)
    )
    exchange = functools.partial(
        lax.all_to_all, axis_name="seq", split_axis=0, concat_axis=0, tiled=True,
        axis_index_groups=SAME_CORE,
    )

    vectors = [v.reshape(1, 6) for v in (gain_one, bias_one, gain_two, bias_two)]
    slots, raw = pl.pallas_call(
        pack_kernel,
        grid=(1,),
        in_specs=[whole(24, 768), whole(6, 768), whole(6, 3072), whole(6, 2304)]
        + [whole(1, 6)] * 4
        + [whole(1, 768)],
        out_specs=[whole(8, 56, 768), whole(24, 640)],
        out_shape=[shape((8, 56, 768), BF), shape((24, 640), BF)],
        scratch_shapes=[
            pltpu.VMEM((56, 768), F32), pltpu.VMEM((128, 128), F32), pltpu.VMEM((24, 640), F32),
        ],
        cost_estimate=about(2),
        compiler_params=pltpu.CompilerParams(vmem_limit_bytes=60 * 1024 * 1024),
    )(w_down, w_out, w_up, w_qkv, *vectors, units)
    slots = exchange(slots)
    near = jnp.stack([raw] + [lax.ppermute(raw, "batch", along_x(step)) for step in (-1, 2, 1)])
    far = lax.ppermute(near, BOTH, SWAP_HALF)
    rest = call(
        regroup_kernel,
        shape((432, 768), BF),
        (slots, regroup, far),
        2,
        [pltpu.VMEM((448, 768), F32)],
        mib=12,
        in_specs=[pl.BlockSpec(memory_space=pltpu.VMEM)] * 2
        + [pl.BlockSpec(memory_space=pl.ANY)],
    )
    weights = lax.all_gather(rest, BOTH, axis=0, axis_index_groups=RINGS)
    x = tokens.transpose(1, 0, 2)
    dy = d_out.transpose(1, 0, 2).reshape(256, 768)
    sent = call(
        address_kernel,
        shape((8, 176, 768), BF),
        (x, near, far),
        2,
        [pltpu.VMEM((4, 48, 640), F32)],
        mib=16,
    )
    own = exchange(sent)
    other = lax.ppermute(own[:, 128:176, 0:640], "seq", SWAP_CORE)
    x = x.reshape(256, 768)

    normed, wt, gains, q_t, kv = call(
        project_kernel,
        [
            shape((1024, 768), BF), shape((576, 768), BF), shape((8, 768), F32),
            shape((192, 1024), BF), shape((384, 1024), BF),
        ],
        (own, other, jnp.asarray(ARRIVAL)),
        5,
        [pltpu.VMEM((768, 640), BF), pltpu.VMEM((640, 768), F32)],
        mib=30,
    )
    kv_other = lax.ppermute(kv, "seq", SWAP_CORE)
    o, o_low, lse = call(
        forward_kernel,
        [shape((192, 1024), F32), shape((8, 192, 128), BF), shape((3, 1024), F32)],
        (lengths, q_t, kv, kv_other),
        12,
        [
            pltpu.VMEM((192, 1024), BF), pltpu.VMEM((3, 2048, 64), BF),
            pltpu.VMEM((192, 2048), BF),
        ]
        + [pltpu.VMEM((256, 256), F32)] * 6
        + [pltpu.VMEM((256, 256), BF)] * 6
        + [pltpu.VMEM((64, 256), F32)] * 3
        + [pltpu.VMEM((8, 256), F32)] * 3,
        mib=30,
        **scalars(4),
    )
    att = exchange(o_low)
    place, attended, attended_t = call(
        prepare_kernel,
        [shape((768, 768), BF), shape((256, 768), BF), shape((768, 256), BF)],
        (att, order),
        2,
        mib=16,
    )
    y, d_first, low, d_att, d_gain, grads = feed(x, dy, attended, gains, place, weights)
    rest_sum = lax.psum_scatter(
        grads.reshape(16 * 384, 768), BOTH, scatter_dimension=0, tiled=True,
        axis_index_groups=RINGS,
    )
    d_att = exchange(d_att)
    out_grad = exchange(call(out_kernel, shape((8, 96, 768), BF), (attended_t, low), 2))
    dq, dkv, dkv_other = call(
        backward_kernel,
        [shape((192, 1024), BF), shape((384, 1024), BF), shape((384, 1024), BF)],
        (lengths, q_t, kv, kv_other, o, lse, d_att),
        20,
        [
            pltpu.VMEM((192, 1024), BF),
            pltpu.VMEM((3, 2048, 64), BF),
            pltpu.VMEM((192, 2048), BF),
            pltpu.VMEM((3, 2048, 64), BF),
            pltpu.VMEM((192, 1024), BF),
            pltpu.VMEM((3, 64, 2048), F32),
            pltpu.VMEM((3, 64, 2048), F32),
            pltpu.VMEM((3, 1024), F32),
        ]
        + [pltpu.VMEM((256, 256), F32)] * 12
        + [pltpu.VMEM((256, 256), BF)] * 12
        + [pltpu.VMEM((64, 256), F32)] * 3,
        mib=60,
        **scalars(7),
    )
    partner = lax.ppermute(dkv_other, "seq", SWAP_CORE)
    part, mine, theirs = call(
        unproject_kernel,
        [shape((8, 128, 768), BF), shape((4, 2, 48, 768), BF), shape((4, 2, 48, 768), BF)],
        (own, dq, dkv, partner, normed, wt, d_gain, qkv_order, out_grad, jnp.asarray(SPREAD)),
        7,
        [
            pltpu.VMEM((576, 1024), BF), pltpu.VMEM((640, 768), F32),
            pltpu.VMEM((768, 640), BF), pltpu.VMEM((128, 768), F32),
        ],
        mib=60,
    )
    add = lambda *parts: sum(p.astype(F32) for p in parts).astype(BF)
    line = add(mine, lax.ppermute(theirs, "seq", SWAP_CORE))
    line = add(
        line[0],
        lax.ppermute(line[1], "batch", along_x(1)),
        lax.ppermute(line[2], "batch", along_x(2)),
        lax.ppermute(line[3], "batch", along_x(-1)),
    )
    qkv_sum = add(line[0], lax.ppermute(line[1], BOTH, SWAP_HALF))
    back = exchange(part)
    d_tokens, d_out_w = call(
        finish_kernel,
        [shape((256, 768), BF), shape((6, 768), F32)],
        (x, d_first, gains, back, qkv_sum),
        3,
        mib=16,
    )
    slots = call(
        slots_kernel,
        shape((8, 56, 768), BF),
        (rest_sum, qkv_sum, regroup),
        2,
        [pltpu.VMEM((512, 768), BF)],
        mib=12,
    )
    slots = exchange(slots)
    vector = shape((1, 6), F32)
    d_down, d_up, d_qkv, *norms = call(
        sums_kernel,
        [shape((24, 768), F32), shape((6, 3072), F32), shape((6, 2304), F32)]
        + [vector] * 4,
        (slots, units),
        2,
        mib=12,
    )
    norms = [v.reshape(6) for v in norms]
    output = y.reshape(2, 128, 768).transpose(1, 0, 2)
    d_tokens = d_tokens.reshape(2, 128, 768).transpose(1, 0, 2)
    return (
        output, d_tokens, norms[0], norms[1], d_qkv, d_out_w, norms[2], norms[3], d_up, d_down,
    )


def solution(mesh):
    rows = P(("seq", "batch"))
    tokens = P("seq", "batch", None)
    return jax.shard_map(
        body,
        mesh=mesh,
        in_specs=(tokens, P("batch"), rows, rows, rows, rows, rows, rows, rows, rows, tokens),
        out_specs=(tokens, tokens, rows, rows, rows, rows, rows, rows, rows, rows),
        check_vma=False,
    )
```

```python
import functools
import math

import jax
import jax.numpy as jnp
import numpy as np
from jax import lax
from jax.experimental import pallas as pl
from jax.experimental.pallas import tpu as pltpu
from jax.sharding import PartitionSpec as P

H = 12
HD = 64
EPSILON = 1e-05
BF = jnp.bfloat16
F32 = jnp.float32
BOTH = ("seq", "batch")
SAME_CORE = [[2 * k + c for k in range(8)] for c in range(2)]
SWAP_CORE = [(i, i ^ 1) for i in range(16)]
TURNS = [(0, 0), (0, 1), (0, 2), (0, 3), (1, 3), (1, 2), (1, 1), (1, 0)]
RING = [(c, z, x) for z, x in TURNS for c in range(2)]


RINGS = [
    [((y * 2 + (low ^ z)) * 2 + c) * 8 + z * 4 + x for c, z, x in RING]
    for y in range(4)
    for low in range(2)
]
SWAP_HALF = [(s * 8 + b, (s ^ 2) * 8 + (b ^ 4)) for s in range(16) for b in range(8)]


def along_x(step):
    return [(b, b // 4 * 4 + (b + step) % 4) for b in range(8)]


def in_order(outer, size):
    natural = np.arange(outer * 16 * size, dtype=np.int32).reshape(outer, 2, 8, size)
    return np.stack([natural[:, c, z * 4 + x] for c, z, x in RING]).reshape(1, -1)


QKV_ORDER = (
    np.arange(768, dtype=np.int32).reshape(8, 2, 8, 6).transpose(1, 2, 0, 3).reshape(1, 768)
)
ROW_ORDER = in_order(8, 6)
UNIT_ORDER = in_order(2, 24)


def regroup_order():
    slot = np.arange(448, dtype=np.int32).reshape(8, 56)
    parts = [slot[:, 0:24]] + [slot[:, f : f + 6] for f in (24, 30, 36, 42, 48)]
    return np.concatenate([p.reshape(-1) for p in parts] + [np.full(80, -1, np.int32)])[None]


REGROUP = regroup_order()


def arrival_places():
    s, j, dz, dx, r = np.indices((2, 8, 2, 4, 6), dtype=np.int32).reshape(5, 768)
    return np.stack([j ^ dz, s, dz, dx, r] + [np.zeros_like(r)] * 3)


ARRIVAL = arrival_places()
SPREAD = np.concatenate(
    [np.arange(96, dtype=np.int32).reshape(16, 6), np.full((16, 2), -1, np.int32)], axis=1
).reshape(128, 1)


def places(order, count=None):
    size = order.shape[1]
    rows = lax.broadcasted_iota(jnp.int32, (count or size, size), 0)
    return jnp.where(rows == order, 1.0, 0.0).astype(BF)


NT = (((1,), (1,)), ((), ()))
NN = (((1,), (0,)), ((), ()))
TN = (((0,), (0,)), ((), ()))


def dot(left, right, dims=NN):
    return lax.dot_general(left, right, dims, preferred_element_type=F32)


def about(us):
    return pl.CostEstimate(flops=int(us * 1.1e9), bytes_accessed=0, transcendentals=0)


def call(kernel, outs, ins, us, scratch=(), mib=60, **kwargs):
    return pl.pallas_call(
        kernel,
        out_shape=outs,
        scratch_shapes=list(scratch),
        cost_estimate=about(us),
        compiler_params=pltpu.CompilerParams(vmem_limit_bytes=mib * 1024 * 1024),
        **kwargs,
    )(*ins)


def shape(dims, dtype):
    return jax.ShapeDtypeStruct(dims, dtype)


def normalize(values):
    center = jnp.mean(values, axis=-1, keepdims=True)
    shifted = values - center
    spread = jnp.mean(shifted * shifted, axis=-1, keepdims=True)
    scale = lax.rsqrt(spread + EPSILON)
    return shifted * scale, scale


def pack_kernel(
    down_ref, out_ref, up_ref, qkv_ref, g1_ref, b1_ref, g2_ref, b2_ref, units_ref,
    slot_ref, raw_ref, scr, turn_scr, raw_scr,
):
    turn_scr[...] = jnp.zeros_like(turn_scr)
    for i, ref in enumerate((g1_ref, b1_ref, g2_ref, b2_ref)):
        turn_scr[64 + i : 65 + i, 0:6] = ref[...].astype(F32)
    norms = turn_scr[...].T[0:6, 64:128].astype(BF)
    up = jnp.concatenate(
        [up_ref[:, k * 768 : (k + 1) * 768].astype(F32) for k in range(4)], axis=0
    ).astype(BF)
    scr[0:24, :] = down_ref[...].astype(F32)
    scr[24:48, :] = dot(up, places(units_ref[...]))
    scr[48:54, :] = out_ref[...].astype(F32)
    scr[54:56, :] = jnp.zeros((2, 768), F32)
    slot = scr[...].astype(BF)
    for j in range(8):
        slot_ref[j] = slot
    for e in range(4):
        parts = [qkv_ref[:, s * 768 + e * 192 : s * 768 + (e + 1) * 192] for s in range(3)]
        row = jnp.concatenate(parts + [norms], axis=1)
        raw_scr[e * 6 : e * 6 + 6, :] = row.astype(F32)
    raw_ref[...] = raw_scr[...].astype(BF)


def regroup_kernel(slots_ref, order_ref, near_ref, rest_ref, scr):
    for j in range(8):
        scr[j * 56 : j * 56 + 56, :] = slots_ref[j].astype(F32)
    rows = dot(places(order_ref[...], 448), scr[...].astype(BF), TN).astype(BF)
    rest_ref[...] = rows[0:432]


def address_kernel(x_ref, near_ref, far_ref, out_ref, scr):
    for e in range(4):
        for dz, ref in enumerate((near_ref, far_ref)):
            for dx in range(4):
                first = (dz * 4 + dx) * 6
                scr[e, first : first + 6, :] = ref[dx].astype(F32)[e * 6 : e * 6 + 6]
        for b in range(2):
            out_ref[2 * e + b, 0:128, :] = x_ref[b]
            out_ref[2 * e + b, 128:176, 0:640] = scr[e].astype(BF)
            out_ref[2 * e + b, 128:176, 640:768] = jnp.zeros((48, 128), BF)


def core_of():
    return lax.rem(lax.axis_index("seq"), 2)


def length_of(lengths_ref):
    return jnp.where(lax.rem(lax.axis_index("seq") // 2, 2) == 0, lengths_ref[0], lengths_ref[1])


def rows_at(dc, dz, dx, size=48):
    row = lax.axis_index("batch")
    c = lax.rem(core_of() + dc, 2)
    z = lax.rem(row // 4 + dz, 2)
    x = lax.rem(row + dx, 4)
    return pl.ds(pl.multiple_of((c * 8 + z * 4 + x) * size, size), size)


def project_kernel(
    own_ref, other_ref, arrival_ref,
    normed_ref, wt_ref, gains_ref, q_ref, kv_ref, w_scr, t_scr,
):
    for j in range(8):
        w_scr[j * 48 : j * 48 + 48, :] = own_ref[j, 128:176, 0:640]
        w_scr[384 + j * 48 : 432 + j * 48, :] = other_ref[j]
    core, row = core_of(), lax.axis_index("batch")
    half, column = row // 4, lax.rem(row, 4)
    table = [arrival_ref[i : i + 1, :] for i in range(5)]
    c = jnp.where(table[1] == 0, core, 1 - core)
    z = jnp.where(table[2] == 0, half, 1 - half)
    x = jnp.bitwise_and(table[3] + column, 3)
    order = ((table[0] * 2 + c) * 8 + z * 4 + x) * 6 + table[4]
    t_scr[...] = dot(w_scr[...].T, places(order), NT)
    wt_ref[...] = t_scr[0:576].astype(BF)
    gains = t_scr[576:584]
    gains_ref[...] = gains
    gain, bias = gains[0:1], gains[1:2]
    for j in range(8):
        hat, _ = normalize(own_ref[j, 0:128, :].astype(F32))
        normed_ref[j * 128 : (j + 1) * 128, :] = (hat * gain + bias).astype(BF)
    for j in range(4):
        lanes = slice(j * 256, (j + 1) * 256)
        qkv = dot(wt_ref[...], normed_ref[lanes, :], NT).astype(BF)
        q_ref[:, lanes] = qkv[0:192]
        kv_ref[:, lanes] = qkv[192:576]


def last_keys(m, core, length):
    lane = lax.broadcasted_iota(jnp.int32, (1, 256), 1)
    query = m * 512 + 128 * core + jnp.where(lane < 128, lane, lane + 128)
    return jnp.minimum(query, length - 1)


def allowed(start, first, last, core):
    offset = start + first + (128 * core if first < 128 else -128 * core)
    return lax.broadcasted_iota(jnp.int32, (64, 256), 0) <= last - offset


def fill_keys(own_ref, other_ref, k_scr, base):
    for u in range(3):
        for j in range(8):
            rows, lanes = pl.ds(base + u * 64, 64), pl.ds(j * 128, 128)
            k_scr[u, j * 256 : j * 256 + 128, :] = own_ref[rows, lanes].T
            k_scr[u, j * 256 + 128 : j * 256 + 256, :] = other_ref[rows, lanes].T


def fill_lanes(own_ref, other_ref, scr, base):
    for j in range(8):
        scr[:, j * 256 : j * 256 + 128] = own_ref[base : base + 192, j * 128 : j * 128 + 128]
        scr[:, j * 256 + 128 : j * 256 + 256] = other_ref[
            base : base + 192, j * 128 : j * 128 + 128
        ]


PAIRS = [(h, u) for h in range(2) for u in range(3)]
CHUNKS = [slice(i * 64, i * 64 + 64) for i in range(4)]


def steps(m, length):
    return jnp.minimum(m + 1, (length + 511) // 512)


def sweep(length, begin, score, step, finish):
    def one(_, place):
        m, jk = place
        more = jk + 1 < steps(m, length)
        next_m = jnp.where(more, m, jnp.minimum(m + 1, 3))
        next_jk = jnp.where(more, jk + 1, 0)

        @pl.when(jk == 0)
        def _():
            begin()

        edge = (jk == m) | (jk * 512 + 512 > length)

        @pl.when(edge)
        def _():
            step(m, jk, next_m, next_jk, True)

        @pl.when(jnp.logical_not(edge))
        def _():
            step(m, jk, next_m, next_jk, False)

        @pl.when(jnp.logical_not(more))
        def _():
            finish(m)

        return jnp.where(more, m, m + 1), next_jk

    for h, u in PAIRS:
        score(h, u, 0, 0)
    total = sum(steps(m, length) for m in range(4))
    lax.fori_loop(0, total, one, (jnp.int32(0), jnp.int32(0)))


def group(m):
    return pl.ds(pl.multiple_of(m * 256, 256), 256)


def key_tile(jk, h):
    return pl.ds(pl.multiple_of(jk * 512, 512) + h * 256, 256)


def forward_plain(q_scr, k_scr, v_scr, scratch, length, core, finish):
    s_scr, w_scr, acc_scr, sum_scr = scratch[0:6], scratch[6:12], scratch[12:15], scratch[15:18]

    def begin():
        for u in range(3):
            acc_scr[u][...] = jnp.zeros((64, 256), F32)
            sum_scr[u][...] = jnp.zeros((8, 256), F32)

    def score(h, u, m, jk):
        queries = q_scr[u * 64 : (u + 1) * 64, group(m)]
        s_scr[h * 3 + u][...] = dot(k_scr[u, key_tile(jk, h), :], queries)

    def step(m, jk, next_m, next_jk, masked):
        last = last_keys(m, core, length)
        for h, u in PAIRS:
            scores, weights = s_scr[h * 3 + u], w_scr[h * 3 + u]
            total = sum_scr[u][...]
            for rows in CHUNKS:
                s = scores[rows, :]
                t = s * s + 1.0
                r = lax.rsqrt(t)
                e = jnp.exp(t * r)
                if masked:
                    e = jnp.where(allowed(jk * 512 + h * 256, rows.start, last, core), e, 0.0)
                total = total + jnp.sum(e.reshape(8, 8, 256), axis=0)
                weights[rows, :] = (s * r * e).astype(BF)
            sum_scr[u][...] = total
            score(h, u, next_m, next_jk)
            acc_scr[u][...] += dot(v_scr[u * 64 : (u + 1) * 64, key_tile(jk, h)], weights[...])

    def close(m):
        for u in range(3):
            total = jnp.sum(sum_scr[u][...], axis=0, keepdims=True)
            finish(m, u, acc_scr[u][...], total, jnp.zeros((1, 256), F32))

    sweep(length, begin, score, step, close)


def forward_any(q_scr, k_scr, v_scr, length, core, finish):
    def one(m, _):
        last = last_keys(m, core, length)

        def step(jk, carry):
            start = pl.multiple_of(jk * 256, 256)
            mask = jnp.concatenate([allowed(start, r.start, last, core) for r in CHUNKS], axis=0)
            out = []
            for u in range(3):
                top, total, accum = carry[u]
                s = dot(k_scr[u, pl.ds(start, 256), :], q_scr[u * 64 : (u + 1) * 64, group(m)])
                t = s * s + 1.0
                r = lax.rsqrt(t)
                a = jnp.where(mask, t * r, -1e30)
                fresh = jnp.maximum(top, jnp.max(a, axis=0, keepdims=True))
                e = jnp.exp(a - fresh)
                rescale = jnp.exp(top - fresh)
                total = total * rescale + jnp.sum(e, axis=0, keepdims=True)
                accum = accum * rescale + dot(
                    v_scr[u * 64 : (u + 1) * 64, pl.ds(start, 256)], (s * r * e).astype(BF)
                )
                out.append((fresh, total, accum))
            return tuple(out)

        zero = (jnp.zeros((1, 256), F32), jnp.zeros((1, 256), F32), jnp.zeros((64, 256), F32))
        carry = lax.fori_loop(0, 2 * steps(m, length), step, (zero,) * 3)
        for u in range(3):
            finish(m, u, carry[u][2], carry[u][1], carry[u][0])
        return 0

    lax.fori_loop(0, 4, one, 0)


def forward_kernel(
    lengths_ref, q_ref, own_ref, other_ref, o_ref, low_ref, lse_ref, q_scr, k_scr, v_scr, *scratch
):
    length, core = length_of(lengths_ref), core_of()
    fill_keys(own_ref, other_ref, k_scr, 0)
    fill_lanes(own_ref, other_ref, v_scr, 192)
    q_scr[...] = q_ref[...] * BF(0.125)

    def finish(m, u, accum, total, top):
        lanes = group(m)
        o = accum / total
        o_ref[u * 64 : (u + 1) * 64, lanes] = o
        for half in range(2):
            low_ref[2 * m + half, u * 64 : (u + 1) * 64, :] = o[
                :, half * 128 : half * 128 + 128
            ].astype(BF)
        lse_ref[u : u + 1, lanes] = top + jnp.log(total)

    def largest(ref):
        values = ref[0:192, :].astype(F32)
        return jnp.max(jnp.sum((values * values).reshape(3, 64, 1024), axis=1))

    bound = largest(q_ref) * jnp.maximum(largest(own_ref), largest(other_ref)) * (1.0 / 64.0)
    small = bound < 3600.0

    @pl.when(small)
    def _():
        forward_plain(q_scr, k_scr, v_scr, scratch, length, core, finish)

    @pl.when(jnp.logical_not(small))
    def _():
        forward_any(q_scr, k_scr, v_scr, length, core, finish)


def backward_kernel(
    lengths_ref, q_ref, own_ref, other_ref, o_ref, lse_ref, da_ref,
    dq_ref, down_ref, dother_ref,
    q_scr, k_scr, kt_scr, v_scr, da_scr, dk_scr, dv_scr, delta_scr, *scratch,
):
    s_scr, dp_scr, w_scr, ds_scr, dq_scr = (scratch[i : i + 6] for i in (0, 6, 12, 18, 24))
    length, core = length_of(lengths_ref), core_of()
    fill_keys(own_ref, other_ref, k_scr, 0)
    fill_lanes(own_ref, other_ref, kt_scr, 0)
    fill_keys(own_ref, other_ref, v_scr, 192)
    q_scr[...] = q_ref[...] * BF(0.125)
    for j in range(8):
        lanes = slice(j * 128, (j + 1) * 128)
        da_scr[:, lanes] = da_ref[j]
        for u in range(3):
            rows = slice(u * 64, (u + 1) * 64)
            delta_scr[u : u + 1, lanes] = jnp.sum(
                da_ref[j, rows, :].astype(F32) * o_ref[rows, lanes], axis=0, keepdims=True
            )
    dk_scr[...] = jnp.zeros_like(dk_scr)
    dv_scr[...] = jnp.zeros_like(dv_scr)

    def begin():
        for u in range(3):
            dq_scr[u][...] = jnp.zeros((64, 256), F32)

    def score(h, u, m, jk):
        rows, tile = slice(u * 64, (u + 1) * 64), key_tile(jk, h)
        s_scr[h * 3 + u][...] = dot(k_scr[u, tile, :], q_scr[rows, group(m)])
        dp_scr[h * 3 + u][...] = dot(v_scr[u, tile, :], da_scr[rows, group(m)])

    def step(m, jk, next_m, next_jk, masked):
        last = last_keys(m, core, length)
        for h, u in PAIRS:
            tile = key_tile(jk, h)
            heads = slice(u * 64, (u + 1) * 64)
            delta, lse = delta_scr[u : u + 1, group(m)], lse_ref[u : u + 1, group(m)]
            place = h * 3 + u
            for rows in CHUNKS:
                s = s_scr[place][rows, :]
                t = s * s + 1.0
                r = lax.rsqrt(t)
                p = jnp.exp(t * r - lse)
                if masked:
                    p = jnp.where(allowed(jk * 512 + h * 256, rows.start, last, core), p, 0.0)
                g = s * r
                w_scr[place][rows, :] = (g * p).astype(BF)
                ds = p * (dp_scr[place][rows, :] * (r * r * (r - 1.0) + 1.0) - g * delta)
                ds_scr[place][rows, :] = ds.astype(BF)
            score(h, u, next_m, next_jk)
            dv_scr[u, :, tile] += dot(da_scr[heads, group(m)], w_scr[place][...], NT)
            dk_scr[u, :, tile] += dot(q_scr[heads, group(m)], ds_scr[place][...], NT)
            dq_scr[u][...] += dot(kt_scr[heads, tile], ds_scr[place][...])

    def close(m):
        for u in range(3):
            dq_ref[u * 64 : (u + 1) * 64, group(m)] = (dq_scr[u][...] * 0.125).astype(BF)

    sweep(length, begin, score, step, close)
    for scr, base in ((dk_scr, 0), (dv_scr, 192)):
        for u in range(3):
            rows = pl.ds(base + u * 64, 64)
            for j in range(8):
                lanes = pl.ds(j * 128, 128)
                down_ref[rows, lanes] = scr[u, :, j * 256 : j * 256 + 128].astype(BF)
                dother_ref[rows, lanes] = scr[u, :, j * 256 + 128 : j * 256 + 256].astype(BF)


GELU_SCALE = math.sqrt(2.0 / math.pi)


def prepare_kernel(att_ref, order_ref, place_ref, attended_ref, attended_t_ref):
    place_ref[...] = places(order_ref[...])
    for b in range(2):
        for e in range(4):
            attended_t_ref[e * 192 : (e + 1) * 192, b * 128 : (b + 1) * 128] = att_ref[2 * e + b]
    attended_ref[...] = dot(attended_t_ref[...].T, place_ref[...]).astype(BF)


def feed_kernel(
    x_hbm, dy_hbm, att_hbm, gains_hbm, place_hbm, weights_hbm,
    y_hbm, dfirst_hbm, low_hbm, datt_hbm, dgain_hbm, grads_hbm,
    x_ref, dy_ref, att_ref, gains_ref, place_ref, down_ref, up_ref, out_ref,
    y_ref, dfirst_ref, low_ref, datt_ref, dgain_ref, gdown, gup, acc_scr, dn_scr, loads, stores,
):
    def block(ref, number):
        return ref.at[:, pl.ds(48 * number, 48), :]

    arrivals = [(att_hbm, att_ref), (block(weights_hbm, 8), out_ref), (x_hbm, x_ref)]
    arrivals += [(gains_hbm, gains_ref), (place_hbm, place_ref)]
    for k in range(4):
        arrivals.append((block(weights_hbm, 4 + k), up_ref.at[k]))
        if k == 0:
            arrivals.append((dy_hbm, dy_ref))
        arrivals.append((block(weights_hbm, k), down_ref.at[k]))
    arrivals = [pltpu.make_async_copy(*pair, loads.at[i]) for i, pair in enumerate(arrivals)]
    for copy in arrivals:
        copy.start()
    departures = []

    def send(source, target):
        copy = pltpu.make_async_copy(source, target, stores.at[len(departures)])
        copy.start()
        departures.append(copy)

    for copy in arrivals[0:4]:
        copy.wait()
    gain, bias = gains_ref[2:3], gains_ref[3:4]
    w_out = out_ref[...].reshape(768, 768)
    first = x_ref[...].astype(F32) + dot(att_ref[...], w_out)
    hat, scale = normalize(first)
    acc_scr[...] = first
    arrivals[4].wait()
    n2 = dot((hat * gain + bias).astype(BF), place_ref[...]).astype(BF)
    n2t = n2.T
    waiting = arrivals[5:]
    for k in range(4):
        waiting.pop(0).wait()
        up = up_ref[k].reshape(768, 768)
        hidden = dot(n2, up)
        if k == 0:
            waiting.pop(0).wait()
        waiting.pop(0).wait()
        down = down_ref[k].reshape(768, 768)
        dy = dy_ref[...]
        d_active = dot(dy, down, NT)
        square = hidden * hidden
        tanh = jnp.tanh(GELU_SCALE * hidden * (1.0 + 0.044715 * square))
        share = 0.5 + 0.5 * tanh
        active = (hidden * share).astype(BF)
        slope = share + 0.5 * hidden * (1.0 - tanh * tanh) * (
            GELU_SCALE * (1.0 + (3 * 0.044715) * square)
        )
        d_hidden = (slope * d_active).astype(BF)
        gdown[k] = dot(active.T, dy).astype(BF).reshape(16, 48, 768)
        send(gdown.at[k], block(grads_hbm, k))
        gup[k] = dot(n2t, d_hidden).astype(BF).reshape(16, 48, 768)
        send(gup.at[k], block(grads_hbm, 4 + k))
        acc_scr[...] += dot(active, down)
        d_n2 = dot(d_hidden, up, NT)
        dn_scr[...] = d_n2 if k == 0 else dn_scr[...] + d_n2
    y_ref[...] = acc_scr[...].astype(BF)
    send(y_ref, y_hbm)
    dn = dot(dn_scr[...].astype(BF), place_ref[...], NT)
    t = dn * gain
    part = t - jnp.mean(t, -1, keepdims=True) - hat * jnp.mean(t * hat, -1, keepdims=True)
    d_first = dy_ref[...].astype(F32) + part * scale
    low = d_first.astype(BF)
    low_ref[...] = low
    send(low_ref, low_hbm)
    dfirst_ref[...] = d_first
    send(dfirst_ref, dfirst_hbm)
    d_att = dot(w_out, low, NT).astype(BF)
    d_att = dot(place_ref[...], d_att).astype(BF)
    for b in range(2):
        for e in range(4):
            datt_ref[2 * e + b] = d_att[e * 192 : (e + 1) * 192, b * 128 : (b + 1) * 128]
    send(datt_ref, datt_hbm)
    dgain_ref[0:1, :] = jnp.sum(dn * hat, axis=0, keepdims=True)
    dgain_ref[1:2, :] = jnp.sum(dn, axis=0, keepdims=True)
    dgain_ref[2:8, :] = jnp.zeros((6, 768), F32)
    send(dgain_ref, dgain_hbm)
    for copy in departures:
        copy.wait()


def out_kernel(attended_t_ref, low_ref, grad_ref):
    grad = dot(attended_t_ref[...], low_ref[...]).reshape(8, 2, 2, 24, 768)
    half = lax.axis_index("batch") // 4
    for j in range(8):
        rows = [
            jnp.where(half == z, grad[j, c, z], grad[j ^ 1, c, z]) for c in range(2) for z in range(2)
        ]
        grad_ref[j] = jnp.concatenate(rows, axis=0).astype(BF)


def whole(*dims):
    return pl.BlockSpec(dims, lambda *_: (0,) * len(dims))


def feed(*arrays):
    outs = [
        shape((256, 768), BF), shape((256, 768), F32), shape((256, 768), BF),
        shape((8, 192, 128), BF), shape((8, 768), F32), shape((16, 384, 768), BF),
    ]
    blocks = pltpu.VMEM((4, 16, 48, 768), BF)
    held = [pltpu.VMEM(a.shape, a.dtype) for a in arrays[:-1]]
    held += [blocks, blocks, pltpu.VMEM((16, 48, 768), BF)]
    held += [pltpu.VMEM(o.shape, o.dtype) for o in outs[:-1]]
    held += [blocks, blocks] + [pltpu.VMEM((256, 768), F32)] * 2
    held += [pltpu.SemaphoreType.DMA((14,)), pltpu.SemaphoreType.DMA((13,))]
    return call(
        feed_kernel,
        outs,
        arrays,
        15,
        held,
        in_specs=[pl.BlockSpec(memory_space=pl.ANY)] * len(arrays),
        out_specs=[pl.BlockSpec(memory_space=pl.ANY)] * len(outs),
    )


def unproject_kernel(
    own_ref, dq_ref, dkv_ref, partner_ref, normed_ref, wt_ref, dgain_ref, order_ref,
    out_ref, spread_ref,
    part_ref, mine_ref, theirs_ref, dt_scr, dw_scr, p_scr, o_scr,
):
    dt_scr[0:192, :] = dq_ref[...]
    dt_scr[192:576, :] = (dkv_ref[...].astype(F32) + partner_ref[...].astype(F32)).astype(BF)
    bias_sum = jnp.zeros((1, 768), F32)
    gain_sum = jnp.zeros((1, 768), F32)
    for j in range(4):
        d_normed = dot(dt_scr[:, j * 256 : (j + 1) * 256].T, wt_ref[...])
        part_ref[2 * j : 2 * j + 2] = d_normed.astype(BF).reshape(2, 128, 768)
        pair = jnp.concatenate([own_ref[2 * j, 0:128, :], own_ref[2 * j + 1, 0:128, :]], axis=0)
        hat, _ = normalize(pair.astype(F32))
        gain_sum += jnp.sum(d_normed * hat, axis=0, keepdims=True)
        bias_sum += jnp.sum(d_normed, axis=0, keepdims=True)
    dw_scr[0:576, :] = dot(dt_scr[...], normed_ref[...])
    dw_scr[576:577, :] = gain_sum
    dw_scr[577:578, :] = bias_sum
    dw_scr[578:580, :] = dgain_ref[0:2, :]
    dw_scr[580:640, :] = jnp.zeros((60, 768), F32)
    p_scr[...] = dot(dw_scr[...].astype(BF), places(order_ref[...])).T.astype(BF)
    out = jnp.zeros((96, 768), F32)
    for j in range(8):
        out += out_ref[j].astype(F32)
    lanes = lax.broadcasted_iota(jnp.int32, (128, 96), 1)
    spread = jnp.where(lanes == spread_ref[...], 1.0, 0.0).astype(BF)
    o_scr[...] = dot(spread, out.astype(BF))
    for dc, ref in enumerate((mine_ref, theirs_ref)):
        for dx in range(4):
            for dz in range(2):
                ref[dx, dz, :, 0:640] = p_scr[rows_at(dc, dz, dx), :]
                few = o_scr[rows_at(dc, dz, dx, 8), :]
                ref[dx, dz, :, 640:768] = jnp.concatenate(
                    [few[:, q * 128 : (q + 1) * 128] for q in range(6)], axis=0
                ).astype(BF)


def slots_kernel(rest_ref, qkv_ref, order_ref, out_ref, r_scr):
    r_scr[0:384, :] = rest_ref[...]
    r_scr[384:432, 0:640] = qkv_ref[:, 0:640]
    r_scr[384:432, 640:768] = jnp.zeros((48, 128), BF)
    r_scr[432:512, :] = jnp.zeros((80, 768), BF)
    rows = dot(places(order_ref[...], 448), r_scr[...])
    for j in range(8):
        out_ref[j] = rows[j * 56 : j * 56 + 56].astype(BF)


def finish_kernel(x_ref, dfirst_ref, gains_ref, got_ref, qkv_ref, dtok_ref, out_ref):
    for q in range(6):
        out_ref[:, q * 128 : (q + 1) * 128] = qkv_ref[q * 8 : q * 8 + 8, 640:768].astype(F32)[0:6]
    gain = gains_ref[0:1]
    for b in range(2):
        rows = slice(b * 128, (b + 1) * 128)
        dn = jnp.zeros((128, 768), F32)
        for e in range(4):
            dn += got_ref[2 * e + b].astype(F32)
        hat, scale = normalize(x_ref[rows, :].astype(F32))
        t = dn * gain
        part = t - jnp.mean(t, -1, keepdims=True) - hat * jnp.mean(t * hat, -1, keepdims=True)
        dtok_ref[rows, :] = (dfirst_ref[rows, :] + part * scale).astype(BF)


def sums_kernel(got_ref, units_ref, down_ref, up_ref, qkv_ref, g1_ref, b1_ref, g2_ref, b2_ref):
    total = jnp.zeros((56, 768), F32)
    chunks = []
    for e in range(4):
        both = got_ref[2 * e].astype(F32) + got_ref[2 * e + 1].astype(F32)
        chunks.append(both[48:54])
        total += both
    down_ref[...] = total[0:24]
    left, up, units = total[24:48], jnp.zeros((24, 768), F32), places(units_ref[...])
    for _ in range(3):
        piece = left.astype(BF)
        left = left - piece.astype(F32)
        up += dot(piece, units, NT)
    for k in range(4):
        up_ref[:, k * 768 : (k + 1) * 768] = up[k * 6 : k * 6 + 6]
    for s in range(3):
        qkv_ref[:, s * 768 : (s + 1) * 768] = jnp.concatenate(
            [chunks[e][:, s * 192 : (s + 1) * 192] for e in range(4)], axis=1
        )
    norms = total[:, 512:640].T
    for i, ref in enumerate((g1_ref, b1_ref, g2_ref, b2_ref)):
        ref[...] = norms[64 + i : 65 + i, 48:54]


def scalars(count):
    return dict(
        in_specs=[pl.BlockSpec(memory_space=pltpu.SMEM)]
        + [pl.BlockSpec(memory_space=pltpu.VMEM)] * (count - 1)
    )


def body(tokens, lengths, gain_one, bias_one, w_qkv, w_out, gain_two, bias_two, w_up, w_down, d_out):
    order, units, regroup, qkv_order = (
        jnp.asarray(v) for v in (ROW_ORDER, UNIT_ORDER, REGROUP, QKV_ORDER)
    )
    exchange = functools.partial(
        lax.all_to_all, axis_name="seq", split_axis=0, concat_axis=0, tiled=True,
        axis_index_groups=SAME_CORE,
    )

    vectors = [v.reshape(1, 6) for v in (gain_one, bias_one, gain_two, bias_two)]
    slots, raw = pl.pallas_call(
        pack_kernel,
        grid=(1,),
        in_specs=[whole(24, 768), whole(6, 768), whole(6, 3072), whole(6, 2304)]
        + [whole(1, 6)] * 4
        + [whole(1, 768)],
        out_specs=[whole(8, 56, 768), whole(24, 640)],
        out_shape=[shape((8, 56, 768), BF), shape((24, 640), BF)],
        scratch_shapes=[
            pltpu.VMEM((56, 768), F32), pltpu.VMEM((128, 128), F32), pltpu.VMEM((24, 640), F32),
        ],
        cost_estimate=about(2),
        compiler_params=pltpu.CompilerParams(vmem_limit_bytes=60 * 1024 * 1024),
    )(w_down, w_out, w_up, w_qkv, *vectors, units)
    slots = exchange(slots)
    near = jnp.stack([raw] + [lax.ppermute(raw, "batch", along_x(step)) for step in (-1, 2, 1)])
    far = lax.ppermute(near, BOTH, SWAP_HALF)
    rest = call(
        regroup_kernel,
        shape((432, 768), BF),
        (slots, regroup, near),
        2,
        [pltpu.VMEM((448, 768), F32)],
        mib=12,
        in_specs=[pl.BlockSpec(memory_space=pltpu.VMEM)] * 2
        + [pl.BlockSpec(memory_space=pl.ANY)],
    )
    weights = lax.all_gather(rest, BOTH, axis=0, axis_index_groups=RINGS)
    x = tokens.transpose(1, 0, 2)
    dy = d_out.transpose(1, 0, 2).reshape(256, 768)
    sent = call(
        address_kernel,
        shape((8, 176, 768), BF),
        (x, near, far),
        2,
        [pltpu.VMEM((4, 48, 640), F32)],
        mib=16,
    )
    own = exchange(sent)
    other = lax.ppermute(own[:, 128:176, 0:640], "seq", SWAP_CORE)
    x = x.reshape(256, 768)

    normed, wt, gains, q_t, kv = call(
        project_kernel,
        [
            shape((1024, 768), BF), shape((576, 768), BF), shape((8, 768), F32),
            shape((192, 1024), BF), shape((384, 1024), BF),
        ],
        (own, other, jnp.asarray(ARRIVAL)),
        5,
        [pltpu.VMEM((768, 640), BF), pltpu.VMEM((640, 768), F32)],
        mib=30,
    )
    kv_other = lax.ppermute(kv, "seq", SWAP_CORE)
    o, o_low, lse = call(
        forward_kernel,
        [shape((192, 1024), F32), shape((8, 192, 128), BF), shape((3, 1024), F32)],
        (lengths, q_t, kv, kv_other),
        12,
        [
            pltpu.VMEM((192, 1024), BF), pltpu.VMEM((3, 2048, 64), BF),
            pltpu.VMEM((192, 2048), BF),
        ]
        + [pltpu.VMEM((256, 256), F32)] * 6
        + [pltpu.VMEM((256, 256), BF)] * 6
        + [pltpu.VMEM((64, 256), F32)] * 3
        + [pltpu.VMEM((8, 256), F32)] * 3,
        mib=30,
        **scalars(4),
    )
    att = exchange(o_low)
    place, attended, attended_t = call(
        prepare_kernel,
        [shape((768, 768), BF), shape((256, 768), BF), shape((768, 256), BF)],
        (att, order),
        2,
        mib=16,
    )
    y, d_first, low, d_att, d_gain, grads = feed(x, dy, attended, gains, place, weights)
    rest_sum = lax.psum_scatter(
        grads.reshape(16 * 384, 768), BOTH, scatter_dimension=0, tiled=True,
        axis_index_groups=RINGS,
    )
    d_att = exchange(d_att)
    out_grad = exchange(call(out_kernel, shape((8, 96, 768), BF), (attended_t, low), 2))
    dq, dkv, dkv_other = call(
        backward_kernel,
        [shape((192, 1024), BF), shape((384, 1024), BF), shape((384, 1024), BF)],
        (lengths, q_t, kv, kv_other, o, lse, d_att),
        20,
        [
            pltpu.VMEM((192, 1024), BF),
            pltpu.VMEM((3, 2048, 64), BF),
            pltpu.VMEM((192, 2048), BF),
            pltpu.VMEM((3, 2048, 64), BF),
            pltpu.VMEM((192, 1024), BF),
            pltpu.VMEM((3, 64, 2048), F32),
            pltpu.VMEM((3, 64, 2048), F32),
            pltpu.VMEM((3, 1024), F32),
        ]
        + [pltpu.VMEM((256, 256), F32)] * 12
        + [pltpu.VMEM((256, 256), BF)] * 12
        + [pltpu.VMEM((64, 256), F32)] * 3,
        mib=60,
        **scalars(7),
    )
    partner = lax.ppermute(dkv_other, "seq", SWAP_CORE)
    part, mine, theirs = call(
        unproject_kernel,
        [shape((8, 128, 768), BF), shape((4, 2, 48, 768), BF), shape((4, 2, 48, 768), BF)],
        (own, dq, dkv, partner, normed, wt, d_gain, qkv_order, out_grad, jnp.asarray(SPREAD)),
        7,
        [
            pltpu.VMEM((576, 1024), BF), pltpu.VMEM((640, 768), F32),
            pltpu.VMEM((768, 640), BF), pltpu.VMEM((128, 768), F32),
        ],
        mib=60,
    )
    add = lambda *parts: sum(p.astype(F32) for p in parts).astype(BF)
    line = add(mine, lax.ppermute(theirs, "seq", SWAP_CORE))
    line = add(
        line[0],
        lax.ppermute(line[1], "batch", along_x(1)),
        lax.ppermute(line[2], "batch", along_x(2)),
        lax.ppermute(line[3], "batch", along_x(-1)),
    )
    qkv_sum = add(line[0], lax.ppermute(line[1], BOTH, SWAP_HALF))
    back = exchange(part)
    d_tokens, d_out_w = call(
        finish_kernel,
        [shape((256, 768), BF), shape((6, 768), F32)],
        (x, d_first, gains, back, qkv_sum),
        3,
        mib=16,
    )
    slots = call(
        slots_kernel,
        shape((8, 56, 768), BF),
        (rest_sum, qkv_sum, regroup),
        2,
        [pltpu.VMEM((512, 768), BF)],
        mib=12,
    )
    slots = exchange(slots)
    vector = shape((1, 6), F32)
    d_down, d_up, d_qkv, *norms = call(
        sums_kernel,
        [shape((24, 768), F32), shape((6, 3072), F32), shape((6, 2304), F32)]
        + [vector] * 4,
        (slots, units),
        2,
        mib=12,
    )
    norms = [v.reshape(6) for v in norms]
    output = y.reshape(2, 128, 768).transpose(1, 0, 2)
    d_tokens = d_tokens.reshape(2, 128, 768).transpose(1, 0, 2)
    return (
        output, d_tokens, norms[0], norms[1], d_qkv, d_out_w, norms[2], norms[3], d_up, d_down,
    )


def solution(mesh):
    rows = P(("seq", "batch"))
    tokens = P("seq", "batch", None)
    return jax.shard_map(
        body,
        mesh=mesh,
        in_specs=(tokens, P("batch"), rows, rows, rows, rows, rows, rows, rows, rows, tokens),
        out_specs=(tokens, tokens, rows, rows, rows, rows, rows, rows, rows, rows),
        check_vma=False,
    )
```

```python
import functools
import math

import jax
import jax.numpy as jnp
import numpy as np
from jax import lax
from jax.experimental import pallas as pl
from jax.experimental.pallas import tpu as pltpu
from jax.sharding import PartitionSpec as P

H = 12
HD = 64
EPSILON = 1e-05
BF = jnp.bfloat16
F32 = jnp.float32
BOTH = ("seq", "batch")
SAME_CORE = [[2 * k + c for k in range(8)] for c in range(2)]
SWAP_CORE = [(i, i ^ 1) for i in range(16)]
TURNS = [(0, 0), (0, 1), (0, 2), (0, 3), (1, 3), (1, 2), (1, 1), (1, 0)]
RING = [(c, z, x) for z, x in TURNS for c in range(2)]


RINGS = [
    [((y * 2 + (low ^ z)) * 2 + c) * 8 + z * 4 + x for c, z, x in RING]
    for y in range(4)
    for low in range(2)
]
SWAP_HALF = [(s * 8 + b, (s ^ 2) * 8 + (b ^ 4)) for s in range(16) for b in range(8)]


def along_x(step):
    return [(b, b // 4 * 4 + (b + step) % 4) for b in range(8)]


def in_order(outer, size):
    natural = np.arange(outer * 16 * size, dtype=np.int32).reshape(outer, 2, 8, size)
    return np.stack([natural[:, c, z * 4 + x] for c, z, x in RING]).reshape(1, -1)


QKV_ORDER = (
    np.arange(768, dtype=np.int32).reshape(8, 2, 8, 6).transpose(1, 2, 0, 3).reshape(1, 768)
)
ROW_ORDER = in_order(8, 6)
UNIT_ORDER = in_order(2, 24)


def regroup_order():
    slot = np.arange(448, dtype=np.int32).reshape(8, 56)
    parts = [slot[:, 0:24]] + [slot[:, f : f + 6] for f in (24, 30, 36, 42, 48)]
    return np.concatenate([p.reshape(-1) for p in parts] + [np.full(80, -1, np.int32)])[None]


REGROUP = regroup_order()


def arrival_places():
    s, j, dz, dx, r = np.indices((2, 8, 2, 4, 6), dtype=np.int32).reshape(5, 768)
    return np.stack([j ^ dz, s, dz, dx, r] + [np.zeros_like(r)] * 3)


ARRIVAL = arrival_places()
SPREAD = np.concatenate(
    [np.arange(96, dtype=np.int32).reshape(16, 6), np.full((16, 2), -1, np.int32)], axis=1
).reshape(128, 1)


def places(order, count=None):
    size = order.shape[1]
    rows = lax.broadcasted_iota(jnp.int32, (count or size, size), 0)
    return jnp.where(rows == order, 1.0, 0.0).astype(BF)


NT = (((1,), (1,)), ((), ()))
NN = (((1,), (0,)), ((), ()))
TN = (((0,), (0,)), ((), ()))


def dot(left, right, dims=NN):
    return lax.dot_general(left, right, dims, preferred_element_type=F32)


def about(us):
    return pl.CostEstimate(flops=int(us * 1.1e9), bytes_accessed=0, transcendentals=0)


def call(kernel, outs, ins, us, scratch=(), mib=60, **kwargs):
    return pl.pallas_call(
        kernel,
        out_shape=outs,
        scratch_shapes=list(scratch),
        cost_estimate=about(us),
        compiler_params=pltpu.CompilerParams(vmem_limit_bytes=mib * 1024 * 1024),
        **kwargs,
    )(*ins)


def shape(dims, dtype):
    return jax.ShapeDtypeStruct(dims, dtype)


def normalize(values):
    center = jnp.mean(values, axis=-1, keepdims=True)
    shifted = values - center
    spread = jnp.mean(shifted * shifted, axis=-1, keepdims=True)
    scale = lax.rsqrt(spread + EPSILON)
    return shifted * scale, scale


def pack_kernel(
    down_ref, out_ref, up_ref, qkv_ref, g1_ref, b1_ref, g2_ref, b2_ref, units_ref,
    slot_ref, raw_ref, scr, turn_scr, raw_scr,
):
    turn_scr[...] = jnp.zeros_like(turn_scr)
    for i, ref in enumerate((g1_ref, b1_ref, g2_ref, b2_ref)):
        turn_scr[64 + i : 65 + i, 0:6] = ref[...].astype(F32)
    norms = turn_scr[...].T[0:6, 64:128].astype(BF)
    up = jnp.concatenate(
        [up_ref[:, k * 768 : (k + 1) * 768].astype(F32) for k in range(4)], axis=0
    ).astype(BF)
    scr[0:24, :] = down_ref[...].astype(F32)
    scr[24:48, :] = dot(up, places(units_ref[...]))
    scr[48:54, :] = out_ref[...].astype(F32)
    scr[54:56, :] = jnp.zeros((2, 768), F32)
    slot = scr[...].astype(BF)
    for j in range(8):
        slot_ref[j] = slot
    for e in range(4):
        parts = [qkv_ref[:, s * 768 + e * 192 : s * 768 + (e + 1) * 192] for s in range(3)]
        row = jnp.concatenate(parts + [norms], axis=1)
        raw_scr[e * 6 : e * 6 + 6, :] = row.astype(F32)
    raw_ref[...] = raw_scr[...].astype(BF)


def regroup_kernel(slots_ref, order_ref, near_ref, rest_ref, scr):
    for j in range(8):
        scr[j * 56 : j * 56 + 56, :] = slots_ref[j].astype(F32)
    rows = dot(places(order_ref[...], 448), scr[...].astype(BF), TN).astype(BF)
    rest_ref[...] = rows[0:432]


def address_kernel(x_ref, near_ref, far_ref, out_ref, scr):
    for e in range(4):
        for dz, ref in enumerate((near_ref, far_ref)):
            for dx in range(4):
                first = (dz * 4 + dx) * 6
                scr[e, first : first + 6, :] = ref[dx].astype(F32)[e * 6 : e * 6 + 6]
        for b in range(2):
            out_ref[2 * e + b, 0:128, :] = x_ref[b]
            out_ref[2 * e + b, 128:176, 0:640] = scr[e].astype(BF)
            out_ref[2 * e + b, 128:176, 640:768] = jnp.zeros((48, 128), BF)


def core_of():
    return lax.rem(lax.axis_index("seq"), 2)


def length_of(lengths_ref):
    return jnp.where(lax.rem(lax.axis_index("seq") // 2, 2) == 0, lengths_ref[0], lengths_ref[1])


def rows_at(dc, dz, dx, size=48):
    row = lax.axis_index("batch")
    c = lax.rem(core_of() + dc, 2)
    z = lax.rem(row // 4 + dz, 2)
    x = lax.rem(row + dx, 4)
    return pl.ds(pl.multiple_of((c * 8 + z * 4 + x) * size, size), size)


def project_kernel(
    own_ref, other_ref, arrival_ref,
    normed_ref, wt_ref, gains_ref, q_ref, kv_ref, w_scr, t_scr,
):
    for j in range(8):
        w_scr[j * 48 : j * 48 + 48, :] = own_ref[j, 128:176, 0:640]
        w_scr[384 + j * 48 : 432 + j * 48, :] = other_ref[j]
    core, row = core_of(), lax.axis_index("batch")
    half, column = row // 4, lax.rem(row, 4)
    table = [arrival_ref[i : i + 1, :] for i in range(5)]
    c = jnp.where(table[1] == 0, core, 1 - core)
    z = jnp.where(table[2] == 0, half, 1 - half)
    x = jnp.bitwise_and(table[3] + column, 3)
    order = ((table[0] * 2 + c) * 8 + z * 4 + x) * 6 + table[4]
    t_scr[...] = dot(w_scr[...].T, places(order), NT)
    wt_ref[...] = t_scr[0:576].astype(BF)
    gains = t_scr[576:584]
    gains_ref[...] = gains
    gain, bias = gains[0:1], gains[1:2]
    for j in range(8):
        hat, _ = normalize(own_ref[j, 0:128, :].astype(F32))
        normed_ref[j * 128 : (j + 1) * 128, :] = (hat * gain + bias).astype(BF)
    for j in range(4):
        lanes = slice(j * 256, (j + 1) * 256)
        qkv = dot(wt_ref[...], normed_ref[lanes, :], NT).astype(BF)
        q_ref[:, lanes] = qkv[0:192]
        kv_ref[:, lanes] = qkv[192:576]


def last_keys(m, core, length):
    lane = lax.broadcasted_iota(jnp.int32, (1, 256), 1)
    query = m * 512 + 128 * core + jnp.where(lane < 128, lane, lane + 128)
    return jnp.minimum(query, length - 1)


def allowed(start, first, last, core):
    offset = start + first + (128 * core if first < 128 else -128 * core)
    return lax.broadcasted_iota(jnp.int32, (64, 256), 0) <= last - offset


def fill_keys(own_ref, other_ref, k_scr, base):
    for u in range(3):
        for j in range(8):
            rows, lanes = pl.ds(base + u * 64, 64), pl.ds(j * 128, 128)
            k_scr[u, j * 256 : j * 256 + 128, :] = own_ref[rows, lanes].T
            k_scr[u, j * 256 + 128 : j * 256 + 256, :] = other_ref[rows, lanes].T


def fill_lanes(own_ref, other_ref, scr, base):
    for j in range(8):
        scr[:, j * 256 : j * 256 + 128] = own_ref[base : base + 192, j * 128 : j * 128 + 128]
        scr[:, j * 256 + 128 : j * 256 + 256] = other_ref[
            base : base + 192, j * 128 : j * 128 + 128
        ]


PAIRS = [(h, u) for h in range(2) for u in range(3)]
CHUNKS = [slice(i * 64, i * 64 + 64) for i in range(4)]


def steps(m, length):
    return jnp.minimum(m + 1, (length + 511) // 512)


def sweep(length, begin, score, step, finish):
    def one(_, place):
        m, jk = place
        more = jk + 1 < steps(m, length)
        next_m = jnp.where(more, m, jnp.minimum(m + 1, 3))
        next_jk = jnp.where(more, jk + 1, 0)

        @pl.when(jk == 0)
        def _():
            begin()

        edge = (jk == m) | (jk * 512 + 512 > length)

        @pl.when(edge)
        def _():
            step(m, jk, next_m, next_jk, True)

        @pl.when(jnp.logical_not(edge))
        def _():
            step(m, jk, next_m, next_jk, False)

        @pl.when(jnp.logical_not(more))
        def _():
            finish(m)

        return jnp.where(more, m, m + 1), next_jk

    for h, u in PAIRS:
        score(h, u, 0, 0)
    total = sum(steps(m, length) for m in range(4))
    lax.fori_loop(0, total, one, (jnp.int32(0), jnp.int32(0)))


def group(m):
    return pl.ds(pl.multiple_of(m * 256, 256), 256)


def key_tile(jk, h):
    return pl.ds(pl.multiple_of(jk * 512, 512) + h * 256, 256)


def forward_plain(q_scr, k_scr, v_scr, scratch, length, core, finish):
    s_scr, w_scr, acc_scr, sum_scr = scratch[0:6], scratch[6:12], scratch[12:15], scratch[15:18]

    def begin():
        for u in range(3):
            acc_scr[u][...] = jnp.zeros((64, 256), F32)
            sum_scr[u][...] = jnp.zeros((8, 256), F32)

    def score(h, u, m, jk):
        queries = q_scr[u * 64 : (u + 1) * 64, group(m)]
        s_scr[h * 3 + u][...] = dot(k_scr[u, key_tile(jk, h), :], queries)

    def step(m, jk, next_m, next_jk, masked):
        last = last_keys(m, core, length)
        for h, u in PAIRS:
            scores, weights = s_scr[h * 3 + u], w_scr[h * 3 + u]
            total = sum_scr[u][...]
            for rows in CHUNKS:
                s = scores[rows, :]
                t = s * s + 1.0
                r = lax.rsqrt(t)
                e = jnp.exp(t * r)
                if masked:
                    e = jnp.where(allowed(jk * 512 + h * 256, rows.start, last, core), e, 0.0)
                total = total + jnp.sum(e.reshape(8, 8, 256), axis=0)
                weights[rows, :] = (s * r * e).astype(BF)
            sum_scr[u][...] = total
            score(h, u, next_m, next_jk)
            acc_scr[u][...] += dot(v_scr[u * 64 : (u + 1) * 64, key_tile(jk, h)], weights[...])

    def close(m):
        for u in range(3):
            total = jnp.sum(sum_scr[u][...], axis=0, keepdims=True)
            finish(m, u, acc_scr[u][...], total, jnp.zeros((1, 256), F32))

    sweep(length, begin, score, step, close)


def forward_any(q_scr, k_scr, v_scr, length, core, finish):
    def one(m, _):
        last = last_keys(m, core, length)

        def step(jk, carry):
            start = pl.multiple_of(jk * 256, 256)
            mask = jnp.concatenate([allowed(start, r.start, last, core) for r in CHUNKS], axis=0)
            out = []
            for u in range(3):
                top, total, accum = carry[u]
                s = dot(k_scr[u, pl.ds(start, 256), :], q_scr[u * 64 : (u + 1) * 64, group(m)])
                t = s * s + 1.0
                r = lax.rsqrt(t)
                a = jnp.where(mask, t * r, -1e30)
                fresh = jnp.maximum(top, jnp.max(a, axis=0, keepdims=True))
                e = jnp.exp(a - fresh)
                rescale = jnp.exp(top - fresh)
                total = total * rescale + jnp.sum(e, axis=0, keepdims=True)
                accum = accum * rescale + dot(
                    v_scr[u * 64 : (u + 1) * 64, pl.ds(start, 256)], (s * r * e).astype(BF)
                )
                out.append((fresh, total, accum))
            return tuple(out)

        zero = (jnp.zeros((1, 256), F32), jnp.zeros((1, 256), F32), jnp.zeros((64, 256), F32))
        carry = lax.fori_loop(0, 2 * steps(m, length), step, (zero,) * 3)
        for u in range(3):
            finish(m, u, carry[u][2], carry[u][1], carry[u][0])
        return 0

    lax.fori_loop(0, 4, one, 0)


def forward_kernel(
    lengths_ref, q_ref, own_ref, other_ref, o_ref, low_ref, lse_ref, q_scr, k_scr, v_scr, *scratch
):
    length, core = length_of(lengths_ref), core_of()
    fill_keys(own_ref, other_ref, k_scr, 0)
    fill_lanes(own_ref, other_ref, v_scr, 192)
    q_scr[...] = q_ref[...] * BF(0.125)

    def finish(m, u, accum, total, top):
        lanes = group(m)
        o = accum / total
        o_ref[u * 64 : (u + 1) * 64, lanes] = o
        for half in range(2):
            low_ref[2 * m + half, u * 64 : (u + 1) * 64, :] = o[
                :, half * 128 : half * 128 + 128
            ].astype(BF)
        lse_ref[u : u + 1, lanes] = top + jnp.log(total)

    def largest(ref):
        values = ref[0:192, :].astype(F32)
        return jnp.max(jnp.sum((values * values).reshape(3, 64, 1024), axis=1))

    bound = largest(q_ref) * jnp.maximum(largest(own_ref), largest(other_ref)) * (1.0 / 64.0)
    small = bound < 3600.0

    @pl.when(small)
    def _():
        forward_plain(q_scr, k_scr, v_scr, scratch, length, core, finish)

    @pl.when(jnp.logical_not(small))
    def _():
        forward_any(q_scr, k_scr, v_scr, length, core, finish)


def backward_kernel(
    lengths_ref, q_ref, own_ref, other_ref, o_ref, lse_ref, da_ref,
    dq_ref, down_ref, dother_ref,
    q_scr, k_scr, kt_scr, v_scr, da_scr, dk_scr, dv_scr, delta_scr, *scratch,
):
    s_scr, dp_scr, w_scr, ds_scr, dq_scr = (scratch[i : i + 6] for i in (0, 6, 12, 18, 24))
    length, core = length_of(lengths_ref), core_of()
    fill_keys(own_ref, other_ref, k_scr, 0)
    fill_lanes(own_ref, other_ref, kt_scr, 0)
    fill_keys(own_ref, other_ref, v_scr, 192)
    q_scr[...] = q_ref[...] * BF(0.125)
    for j in range(8):
        lanes = slice(j * 128, (j + 1) * 128)
        da_scr[:, lanes] = da_ref[j]
        for u in range(3):
            rows = slice(u * 64, (u + 1) * 64)
            delta_scr[u : u + 1, lanes] = jnp.sum(
                da_ref[j, rows, :].astype(F32) * o_ref[rows, lanes], axis=0, keepdims=True
            )
    dk_scr[...] = jnp.zeros_like(dk_scr)
    dv_scr[...] = jnp.zeros_like(dv_scr)

    def begin():
        for u in range(3):
            dq_scr[u][...] = jnp.zeros((64, 256), F32)

    def score(h, u, m, jk):
        rows, tile = slice(u * 64, (u + 1) * 64), key_tile(jk, h)
        s_scr[h * 3 + u][...] = dot(k_scr[u, tile, :], q_scr[rows, group(m)])
        dp_scr[h * 3 + u][...] = dot(v_scr[u, tile, :], da_scr[rows, group(m)])

    def step(m, jk, next_m, next_jk, masked):
        last = last_keys(m, core, length)
        for h, u in PAIRS:
            tile = key_tile(jk, h)
            heads = slice(u * 64, (u + 1) * 64)
            delta, lse = delta_scr[u : u + 1, group(m)], lse_ref[u : u + 1, group(m)]
            place = h * 3 + u
            for rows in CHUNKS:
                s = s_scr[place][rows, :]
                t = s * s + 1.0
                r = lax.rsqrt(t)
                p = jnp.exp(t * r - lse)
                if masked:
                    p = jnp.where(allowed(jk * 512 + h * 256, rows.start, last, core), p, 0.0)
                g = s * r
                w_scr[place][rows, :] = (g * p).astype(BF)
                ds = p * (dp_scr[place][rows, :] * (r * r * (r - 1.0) + 1.0) - g * delta)
                ds_scr[place][rows, :] = ds.astype(BF)
            score(h, u, next_m, next_jk)
            dv_scr[u, :, tile] += dot(da_scr[heads, group(m)], w_scr[place][...], NT)
            dk_scr[u, :, tile] += dot(q_scr[heads, group(m)], ds_scr[place][...], NT)
            dq_scr[u][...] += dot(kt_scr[heads, tile], ds_scr[place][...])

    def close(m):
        for u in range(3):
            dq_ref[u * 64 : (u + 1) * 64, group(m)] = (dq_scr[u][...] * 0.125).astype(BF)

    sweep(length, begin, score, step, close)
    for scr, base in ((dk_scr, 0), (dv_scr, 192)):
        for u in range(3):
            rows = pl.ds(base + u * 64, 64)
            for j in range(8):
                lanes = pl.ds(j * 128, 128)
                down_ref[rows, lanes] = scr[u, :, j * 256 : j * 256 + 128].astype(BF)
                dother_ref[rows, lanes] = scr[u, :, j * 256 + 128 : j * 256 + 256].astype(BF)


GELU_SCALE = math.sqrt(2.0 / math.pi)


def feed_kernel(
    att_hbm, order_hbm, x_hbm, gains_hbm, dy_hbm, weights_hbm,
    y_hbm, dfirst_hbm, low_hbm, datt_hbm, dgain_hbm, grads_hbm,
    att_ref, order_ref, x_ref, gains_ref, dy_ref, down_ref, up_ref, out_ref,
    y_ref, dfirst_ref, low_ref, datt_ref, dgain_ref, gdown, gup, acc_scr, dn_scr,
    place_ref, loads, stores,
):
    def block(ref, number):
        return ref.at[:, pl.ds(48 * number, 48), :]

    arrivals = [(att_hbm, att_ref), (order_hbm, order_ref), (x_hbm, x_ref)]
    arrivals += [(gains_hbm, gains_ref), (block(weights_hbm, 8), out_ref)]
    for k in range(4):
        arrivals.append((block(weights_hbm, 4 + k), up_ref.at[k]))
        if k == 0:
            arrivals.append((dy_hbm, dy_ref))
        arrivals.append((block(weights_hbm, k), down_ref.at[k]))
    arrivals = [pltpu.make_async_copy(*pair, loads.at[i]) for i, pair in enumerate(arrivals)]
    for copy in arrivals:
        copy.start()
    departures = []

    def send(source, target):
        copy = pltpu.make_async_copy(source, target, stores.at[len(departures)])
        copy.start()
        departures.append(copy)

    for copy in arrivals[0:4]:
        copy.wait()
    gain, bias = gains_ref[2:3], gains_ref[3:4]
    place_ref[...] = places(order_ref[...])
    natural = [
        jnp.concatenate([att_ref[2 * e + b] for e in range(4)], axis=0).T for b in range(2)
    ]
    attended = dot(jnp.concatenate(natural, axis=0), place_ref[...]).astype(BF)
    arrivals[4].wait()
    w_out = out_ref[...].reshape(768, 768)
    first = x_ref[...].astype(F32) + dot(attended, w_out)
    hat, scale = normalize(first)
    acc_scr[...] = first
    n2 = dot((hat * gain + bias).astype(BF), place_ref[...]).astype(BF)
    n2t = n2.T
    waiting = arrivals[5:]
    for k in range(4):
        waiting.pop(0).wait()
        up = up_ref[k].reshape(768, 768)
        hidden = dot(n2, up)
        if k == 0:
            waiting.pop(0).wait()
        waiting.pop(0).wait()
        down = down_ref[k].reshape(768, 768)
        dy = dy_ref[...]
        d_active = dot(dy, down, NT)
        square = hidden * hidden
        tanh = jnp.tanh(GELU_SCALE * hidden * (1.0 + 0.044715 * square))
        share = 0.5 + 0.5 * tanh
        active = (hidden * share).astype(BF)
        slope = share + 0.5 * hidden * (1.0 - tanh * tanh) * (
            GELU_SCALE * (1.0 + (3 * 0.044715) * square)
        )
        d_hidden = (slope * d_active).astype(BF)
        gdown[k] = dot(active.T, dy).astype(BF).reshape(16, 48, 768)
        send(gdown.at[k], block(grads_hbm, k))
        gup[k] = dot(n2t, d_hidden).astype(BF).reshape(16, 48, 768)
        send(gup.at[k], block(grads_hbm, 4 + k))
        acc_scr[...] += dot(active, down)
        d_n2 = dot(d_hidden, up, NT)
        dn_scr[...] = d_n2 if k == 0 else dn_scr[...] + d_n2
    y_ref[...] = acc_scr[...].astype(BF)
    send(y_ref, y_hbm)
    dn = dot(dn_scr[...].astype(BF), place_ref[...], NT)
    t = dn * gain
    part = t - jnp.mean(t, -1, keepdims=True) - hat * jnp.mean(t * hat, -1, keepdims=True)
    d_first = dy_ref[...].astype(F32) + part * scale
    low = d_first.astype(BF)
    low_ref[...] = low
    send(low_ref, low_hbm)
    dfirst_ref[...] = d_first
    send(dfirst_ref, dfirst_hbm)
    d_att = dot(w_out, low, NT).astype(BF)
    d_att = dot(place_ref[...], d_att).astype(BF)
    for b in range(2):
        for e in range(4):
            datt_ref[2 * e + b] = d_att[e * 192 : (e + 1) * 192, b * 128 : (b + 1) * 128]
    send(datt_ref, datt_hbm)
    dgain_ref[0:1, :] = jnp.sum(dn * hat, axis=0, keepdims=True)
    dgain_ref[1:2, :] = jnp.sum(dn, axis=0, keepdims=True)
    dgain_ref[2:8, :] = jnp.zeros((6, 768), F32)
    send(dgain_ref, dgain_hbm)
    for copy in departures:
        copy.wait()


def out_kernel(att_ref, low_ref, grad_ref):
    attended_t = [
        jnp.concatenate([att_ref[2 * e + b] for e in range(4)], axis=0) for b in range(2)
    ]
    grad = dot(jnp.concatenate(attended_t, axis=1), low_ref[...]).reshape(8, 2, 2, 24, 768)
    half = lax.axis_index("batch") // 4
    for j in range(8):
        rows = [
            jnp.where(half == z, grad[j, c, z], grad[j ^ 1, c, z]) for c in range(2) for z in range(2)
        ]
        grad_ref[j] = jnp.concatenate(rows, axis=0).astype(BF)


def whole(*dims):
    return pl.BlockSpec(dims, lambda *_: (0,) * len(dims))


def feed(*arrays):
    outs = [
        shape((256, 768), BF), shape((256, 768), F32), shape((256, 768), BF),
        shape((8, 192, 128), BF), shape((8, 768), F32), shape((16, 384, 768), BF),
    ]
    blocks = pltpu.VMEM((4, 16, 48, 768), BF)
    held = [pltpu.VMEM(a.shape, a.dtype) for a in arrays[:-1]]
    held += [blocks, blocks, pltpu.VMEM((16, 48, 768), BF)]
    held += [pltpu.VMEM(o.shape, o.dtype) for o in outs[:-1]]
    held += [blocks, blocks] + [pltpu.VMEM((256, 768), F32)] * 2
    held += [pltpu.VMEM((768, 768), BF)]
    held += [pltpu.SemaphoreType.DMA((14,)), pltpu.SemaphoreType.DMA((13,))]
    return call(
        feed_kernel,
        outs,
        arrays,
        15,
        held,
        in_specs=[pl.BlockSpec(memory_space=pl.ANY)] * len(arrays),
        out_specs=[pl.BlockSpec(memory_space=pl.ANY)] * len(outs),
    )


def unproject_kernel(
    own_ref, dq_ref, dkv_ref, partner_ref, normed_ref, wt_ref, dgain_ref, order_ref,
    out_ref, spread_ref,
    part_ref, mine_ref, theirs_ref, dt_scr, dw_scr, p_scr, o_scr,
):
    dt_scr[0:192, :] = dq_ref[...]
    dt_scr[192:576, :] = (dkv_ref[...].astype(F32) + partner_ref[...].astype(F32)).astype(BF)
    bias_sum = jnp.zeros((1, 768), F32)
    gain_sum = jnp.zeros((1, 768), F32)
    for j in range(4):
        d_normed = dot(dt_scr[:, j * 256 : (j + 1) * 256].T, wt_ref[...])
        part_ref[2 * j : 2 * j + 2] = d_normed.astype(BF).reshape(2, 128, 768)
        pair = jnp.concatenate([own_ref[2 * j, 0:128, :], own_ref[2 * j + 1, 0:128, :]], axis=0)
        hat, _ = normalize(pair.astype(F32))
        gain_sum += jnp.sum(d_normed * hat, axis=0, keepdims=True)
        bias_sum += jnp.sum(d_normed, axis=0, keepdims=True)
    dw_scr[0:576, :] = dot(dt_scr[...], normed_ref[...])
    dw_scr[576:577, :] = gain_sum
    dw_scr[577:578, :] = bias_sum
    dw_scr[578:580, :] = dgain_ref[0:2, :]
    dw_scr[580:640, :] = jnp.zeros((60, 768), F32)
    p_scr[...] = dot(dw_scr[...].astype(BF), places(order_ref[...])).T.astype(BF)
    out = jnp.zeros((96, 768), F32)
    for j in range(8):
        out += out_ref[j].astype(F32)
    lanes = lax.broadcasted_iota(jnp.int32, (128, 96), 1)
    spread = jnp.where(lanes == spread_ref[...], 1.0, 0.0).astype(BF)
    o_scr[...] = dot(spread, out.astype(BF))
    for dc, ref in enumerate((mine_ref, theirs_ref)):
        for dx in range(4):
            for dz in range(2):
                ref[dx, dz, :, 0:640] = p_scr[rows_at(dc, dz, dx), :]
                few = o_scr[rows_at(dc, dz, dx, 8), :]
                ref[dx, dz, :, 640:768] = jnp.concatenate(
                    [few[:, q * 128 : (q + 1) * 128] for q in range(6)], axis=0
                ).astype(BF)


def slots_kernel(rest_ref, qkv_ref, order_ref, out_ref, r_scr):
    r_scr[0:384, :] = rest_ref[...]
    r_scr[384:432, 0:640] = qkv_ref[:, 0:640]
    r_scr[384:432, 640:768] = jnp.zeros((48, 128), BF)
    r_scr[432:512, :] = jnp.zeros((80, 768), BF)
    rows = dot(places(order_ref[...], 448), r_scr[...])
    for j in range(8):
        out_ref[j] = rows[j * 56 : j * 56 + 56].astype(BF)


def finish_kernel(x_ref, dfirst_ref, gains_ref, got_ref, qkv_ref, dtok_ref, out_ref):
    for q in range(6):
        out_ref[:, q * 128 : (q + 1) * 128] = qkv_ref[q * 8 : q * 8 + 8, 640:768].astype(F32)[0:6]
    gain = gains_ref[0:1]
    for b in range(2):
        rows = slice(b * 128, (b + 1) * 128)
        dn = jnp.zeros((128, 768), F32)
        for e in range(4):
            dn += got_ref[2 * e + b].astype(F32)
        hat, scale = normalize(x_ref[rows, :].astype(F32))
        t = dn * gain
        part = t - jnp.mean(t, -1, keepdims=True) - hat * jnp.mean(t * hat, -1, keepdims=True)
        dtok_ref[rows, :] = (dfirst_ref[rows, :] + part * scale).astype(BF)


def sums_kernel(got_ref, units_ref, down_ref, up_ref, qkv_ref, g1_ref, b1_ref, g2_ref, b2_ref):
    total = jnp.zeros((56, 768), F32)
    chunks = []
    for e in range(4):
        both = got_ref[2 * e].astype(F32) + got_ref[2 * e + 1].astype(F32)
        chunks.append(both[48:54])
        total += both
    down_ref[...] = total[0:24]
    left, up, units = total[24:48], jnp.zeros((24, 768), F32), places(units_ref[...])
    for _ in range(3):
        piece = left.astype(BF)
        left = left - piece.astype(F32)
        up += dot(piece, units, NT)
    for k in range(4):
        up_ref[:, k * 768 : (k + 1) * 768] = up[k * 6 : k * 6 + 6]
    for s in range(3):
        qkv_ref[:, s * 768 : (s + 1) * 768] = jnp.concatenate(
            [chunks[e][:, s * 192 : (s + 1) * 192] for e in range(4)], axis=1
        )
    norms = total[:, 512:640].T
    for i, ref in enumerate((g1_ref, b1_ref, g2_ref, b2_ref)):
        ref[...] = norms[64 + i : 65 + i, 48:54]


def scalars(count):
    return dict(
        in_specs=[pl.BlockSpec(memory_space=pltpu.SMEM)]
        + [pl.BlockSpec(memory_space=pltpu.VMEM)] * (count - 1)
    )


def body(tokens, lengths, gain_one, bias_one, w_qkv, w_out, gain_two, bias_two, w_up, w_down, d_out):
    order, units, regroup, qkv_order = (
        jnp.asarray(v) for v in (ROW_ORDER, UNIT_ORDER, REGROUP, QKV_ORDER)
    )
    exchange = functools.partial(
        lax.all_to_all, axis_name="seq", split_axis=0, concat_axis=0, tiled=True,
        axis_index_groups=SAME_CORE,
    )

    vectors = [v.reshape(1, 6) for v in (gain_one, bias_one, gain_two, bias_two)]
    slots, raw = pl.pallas_call(
        pack_kernel,
        grid=(1,),
        in_specs=[whole(24, 768), whole(6, 768), whole(6, 3072), whole(6, 2304)]
        + [whole(1, 6)] * 4
        + [whole(1, 768)],
        out_specs=[whole(8, 56, 768), whole(24, 640)],
        out_shape=[shape((8, 56, 768), BF), shape((24, 640), BF)],
        scratch_shapes=[
            pltpu.VMEM((56, 768), F32), pltpu.VMEM((128, 128), F32), pltpu.VMEM((24, 640), F32),
        ],
        cost_estimate=about(2),
        compiler_params=pltpu.CompilerParams(vmem_limit_bytes=60 * 1024 * 1024),
    )(w_down, w_out, w_up, w_qkv, *vectors, units)
    slots = exchange(slots)
    near = jnp.stack([raw] + [lax.ppermute(raw, "batch", along_x(step)) for step in (-1, 2, 1)])
    far = lax.ppermute(near, BOTH, SWAP_HALF)
    rest = call(
        regroup_kernel,
        shape((432, 768), BF),
        (slots, regroup, near),
        2,
        [pltpu.VMEM((448, 768), F32)],
        mib=12,
        in_specs=[pl.BlockSpec(memory_space=pltpu.VMEM)] * 2
        + [pl.BlockSpec(memory_space=pl.ANY)],
    )
    weights = lax.all_gather(rest, BOTH, axis=0, axis_index_groups=RINGS)
    x = tokens.transpose(1, 0, 2)
    dy = d_out.transpose(1, 0, 2).reshape(256, 768)
    sent = call(
        address_kernel,
        shape((8, 176, 768), BF),
        (x, near, far),
        2,
        [pltpu.VMEM((4, 48, 640), F32)],
        mib=16,
    )
    own = exchange(sent)
    other = lax.ppermute(own[:, 128:176, 0:640], "seq", SWAP_CORE)
    x = x.reshape(256, 768)

    normed, wt, gains, q_t, kv = call(
        project_kernel,
        [
            shape((1024, 768), BF), shape((576, 768), BF), shape((8, 768), F32),
            shape((192, 1024), BF), shape((384, 1024), BF),
        ],
        (own, other, jnp.asarray(ARRIVAL)),
        5,
        [pltpu.VMEM((768, 640), BF), pltpu.VMEM((640, 768), F32)],
        mib=30,
    )
    kv_other = lax.ppermute(kv, "seq", SWAP_CORE)
    o, o_low, lse = call(
        forward_kernel,
        [shape((192, 1024), F32), shape((8, 192, 128), BF), shape((3, 1024), F32)],
        (lengths, q_t, kv, kv_other),
        12,
        [
            pltpu.VMEM((192, 1024), BF), pltpu.VMEM((3, 2048, 64), BF),
            pltpu.VMEM((192, 2048), BF),
        ]
        + [pltpu.VMEM((256, 256), F32)] * 6
        + [pltpu.VMEM((256, 256), BF)] * 6
        + [pltpu.VMEM((64, 256), F32)] * 3
        + [pltpu.VMEM((8, 256), F32)] * 3,
        mib=30,
        **scalars(4),
    )
    att = exchange(o_low)
    y, d_first, low, d_att, d_gain, grads = feed(att, order, x, gains, dy, weights)
    rest_sum = lax.psum_scatter(
        grads.reshape(16 * 384, 768), BOTH, scatter_dimension=0, tiled=True,
        axis_index_groups=RINGS,
    )
    d_att = exchange(d_att)
    out_grad = exchange(call(out_kernel, shape((8, 96, 768), BF), (att, low), 2))
    dq, dkv, dkv_other = call(
        backward_kernel,
        [shape((192, 1024), BF), shape((384, 1024), BF), shape((384, 1024), BF)],
        (lengths, q_t, kv, kv_other, o, lse, d_att),
        20,
        [
            pltpu.VMEM((192, 1024), BF),
            pltpu.VMEM((3, 2048, 64), BF),
            pltpu.VMEM((192, 2048), BF),
            pltpu.VMEM((3, 2048, 64), BF),
            pltpu.VMEM((192, 1024), BF),
            pltpu.VMEM((3, 64, 2048), F32),
            pltpu.VMEM((3, 64, 2048), F32),
            pltpu.VMEM((3, 1024), F32),
        ]
        + [pltpu.VMEM((256, 256), F32)] * 12
        + [pltpu.VMEM((256, 256), BF)] * 12
        + [pltpu.VMEM((64, 256), F32)] * 3,
        mib=60,
        **scalars(7),
    )
    partner = lax.ppermute(dkv_other, "seq", SWAP_CORE)
    part, mine, theirs = call(
        unproject_kernel,
        [shape((8, 128, 768), BF), shape((4, 2, 48, 768), BF), shape((4, 2, 48, 768), BF)],
        (own, dq, dkv, partner, normed, wt, d_gain, qkv_order, out_grad, jnp.asarray(SPREAD)),
        7,
        [
            pltpu.VMEM((576, 1024), BF), pltpu.VMEM((640, 768), F32),
            pltpu.VMEM((768, 640), BF), pltpu.VMEM((128, 768), F32),
        ],
        mib=60,
    )
    add = lambda *parts: sum(p.astype(F32) for p in parts).astype(BF)
    line = add(mine, lax.ppermute(theirs, "seq", SWAP_CORE))
    line = add(
        line[0],
        lax.ppermute(line[1], "batch", along_x(1)),
        lax.ppermute(line[2], "batch", along_x(2)),
        lax.ppermute(line[3], "batch", along_x(-1)),
    )
    qkv_sum = add(line[0], lax.ppermute(line[1], BOTH, SWAP_HALF))
    back = exchange(part)
    d_tokens, d_out_w = call(
        finish_kernel,
        [shape((256, 768), BF), shape((6, 768), F32)],
        (x, d_first, gains, back, qkv_sum),
        3,
        mib=16,
    )
    slots = call(
        slots_kernel,
        shape((8, 56, 768), BF),
        (rest_sum, qkv_sum, regroup),
        2,
        [pltpu.VMEM((512, 768), BF)],
        mib=12,
    )
    slots = exchange(slots)
    vector = shape((1, 6), F32)
    d_down, d_up, d_qkv, *norms = call(
        sums_kernel,
        [shape((24, 768), F32), shape((6, 3072), F32), shape((6, 2304), F32)]
        + [vector] * 4,
        (slots, units),
        2,
        mib=12,
    )
    norms = [v.reshape(6) for v in norms]
    output = y.reshape(2, 128, 768).transpose(1, 0, 2)
    d_tokens = d_tokens.reshape(2, 128, 768).transpose(1, 0, 2)
    return (
        output, d_tokens, norms[0], norms[1], d_qkv, d_out_w, norms[2], norms[3], d_up, d_down,
    )


def solution(mesh):
    rows = P(("seq", "batch"))
    tokens = P("seq", "batch", None)
    return jax.shard_map(
        body,
        mesh=mesh,
        in_specs=(tokens, P("batch"), rows, rows, rows, rows, rows, rows, rows, rows, tokens),
        out_specs=(tokens, tokens, rows, rows, rows, rows, rows, rows, rows, rows),
        check_vma=False,
    )
```

```python
import functools
import math

import jax
import jax.numpy as jnp
import numpy as np
from jax import lax
from jax.experimental import pallas as pl
from jax.experimental.pallas import tpu as pltpu
from jax.sharding import PartitionSpec as P

H = 12
HD = 64
EPSILON = 1e-05
BF = jnp.bfloat16
F32 = jnp.float32
BOTH = ("seq", "batch")
SAME_CORE = [[2 * k + c for k in range(8)] for c in range(2)]
SWAP_CORE = [(i, i ^ 1) for i in range(16)]
TURNS = [(0, 0), (0, 1), (0, 2), (0, 3), (1, 3), (1, 2), (1, 1), (1, 0)]
RING = [(c, z, x) for z, x in TURNS for c in range(2)]


RINGS = [
    [((y * 2 + (low ^ z)) * 2 + c) * 8 + z * 4 + x for c, z, x in RING]
    for y in range(4)
    for low in range(2)
]
SWAP_HALF = [(s * 8 + b, (s ^ 2) * 8 + (b ^ 4)) for s in range(16) for b in range(8)]


def along_x(step):
    return [(b, b // 4 * 4 + (b + step) % 4) for b in range(8)]


def in_order(outer, size):
    natural = np.arange(outer * 16 * size, dtype=np.int32).reshape(outer, 2, 8, size)
    return np.stack([natural[:, c, z * 4 + x] for c, z, x in RING]).reshape(1, -1)


QKV_ORDER = (
    np.arange(768, dtype=np.int32).reshape(8, 2, 8, 6).transpose(1, 2, 0, 3).reshape(1, 768)
)
ROW_ORDER = in_order(8, 6)
UNIT_ORDER = in_order(2, 24)


def regroup_order():
    slot = np.arange(448, dtype=np.int32).reshape(8, 56)
    parts = [slot[:, 0:24]] + [slot[:, f : f + 6] for f in (24, 30, 36, 42, 48)]
    return np.concatenate([p.reshape(-1) for p in parts] + [np.full(80, -1, np.int32)])[None]


REGROUP = regroup_order()


def arrival_places():
    s, j, dz, dx, r = np.indices((2, 8, 2, 4, 6), dtype=np.int32).reshape(5, 768)
    return np.stack([j ^ dz, s, dz, dx, r] + [np.zeros_like(r)] * 3)


ARRIVAL = arrival_places()
SPREAD = np.concatenate(
    [np.arange(96, dtype=np.int32).reshape(16, 6), np.full((16, 2), -1, np.int32)], axis=1
).reshape(128, 1)


def places(order, count=None):
    size = order.shape[1]
    rows = lax.broadcasted_iota(jnp.int32, (count or size, size), 0)
    return jnp.where(rows == order, 1.0, 0.0).astype(BF)


NT = (((1,), (1,)), ((), ()))
NN = (((1,), (0,)), ((), ()))
TN = (((0,), (0,)), ((), ()))


def dot(left, right, dims=NN):
    return lax.dot_general(left, right, dims, preferred_element_type=F32)


def about(us):
    return pl.CostEstimate(flops=int(us * 1.1e9), bytes_accessed=0, transcendentals=0)


def call(kernel, outs, ins, us, scratch=(), mib=60, **kwargs):
    return pl.pallas_call(
        kernel,
        out_shape=outs,
        scratch_shapes=list(scratch),
        cost_estimate=about(us),
        compiler_params=pltpu.CompilerParams(vmem_limit_bytes=mib * 1024 * 1024),
        **kwargs,
    )(*ins)


def shape(dims, dtype):
    return jax.ShapeDtypeStruct(dims, dtype)


def normalize(values):
    center = jnp.mean(values, axis=-1, keepdims=True)
    shifted = values - center
    spread = jnp.mean(shifted * shifted, axis=-1, keepdims=True)
    scale = lax.rsqrt(spread + EPSILON)
    return shifted * scale, scale


def pack_kernel(
    down_ref, out_ref, up_ref, qkv_ref, g1_ref, b1_ref, g2_ref, b2_ref, units_ref,
    slot_ref, raw_ref, scr, turn_scr, raw_scr,
):
    turn_scr[...] = jnp.zeros_like(turn_scr)
    for i, ref in enumerate((g1_ref, b1_ref, g2_ref, b2_ref)):
        turn_scr[64 + i : 65 + i, 0:6] = ref[...].astype(F32)
    norms = turn_scr[...].T[0:6, 64:128].astype(BF)
    up = jnp.concatenate(
        [up_ref[:, k * 768 : (k + 1) * 768].astype(F32) for k in range(4)], axis=0
    ).astype(BF)
    scr[0:24, :] = down_ref[...].astype(F32)
    scr[24:48, :] = dot(up, places(units_ref[...]))
    scr[48:54, :] = out_ref[...].astype(F32)
    scr[54:56, :] = jnp.zeros((2, 768), F32)
    slot = scr[...].astype(BF)
    for j in range(8):
        slot_ref[j] = slot
    for e in range(4):
        parts = [qkv_ref[:, s * 768 + e * 192 : s * 768 + (e + 1) * 192] for s in range(3)]
        row = jnp.concatenate(parts + [norms], axis=1)
        raw_scr[e * 6 : e * 6 + 6, :] = row.astype(F32)
    raw_ref[...] = raw_scr[...].astype(BF)


def regroup_kernel(slots_ref, order_ref, near_ref, rest_ref, scr):
    for j in range(8):
        scr[j * 56 : j * 56 + 56, :] = slots_ref[j].astype(F32)
    rows = dot(places(order_ref[...], 448), scr[...].astype(BF), TN).astype(BF)
    rest_ref[...] = rows[0:432]


def address_kernel(x_ref, near_ref, far_ref, out_ref, scr):
    for e in range(4):
        for dz, ref in enumerate((near_ref, far_ref)):
            for dx in range(4):
                first = (dz * 4 + dx) * 6
                scr[e, first : first + 6, :] = ref[dx].astype(F32)[e * 6 : e * 6 + 6]
        for b in range(2):
            out_ref[2 * e + b, 0:128, :] = x_ref[b]
            out_ref[2 * e + b, 128:176, 0:640] = scr[e].astype(BF)
            out_ref[2 * e + b, 128:176, 640:768] = jnp.zeros((48, 128), BF)


def core_of():
    return lax.rem(lax.axis_index("seq"), 2)


def length_of(lengths_ref):
    return jnp.where(lax.rem(lax.axis_index("seq") // 2, 2) == 0, lengths_ref[0], lengths_ref[1])


def rows_at(dc, dz, dx, size=48):
    row = lax.axis_index("batch")
    c = lax.rem(core_of() + dc, 2)
    z = lax.rem(row // 4 + dz, 2)
    x = lax.rem(row + dx, 4)
    return pl.ds(pl.multiple_of((c * 8 + z * 4 + x) * size, size), size)


def project_kernel(
    own_ref, other_ref, arrival_ref,
    normed_ref, wt_ref, gains_ref, q_ref, kv_ref, w_scr, t_scr,
):
    for j in range(8):
        w_scr[j * 48 : j * 48 + 48, :] = own_ref[j, 128:176, 0:640]
        w_scr[384 + j * 48 : 432 + j * 48, :] = other_ref[j]
    core, row = core_of(), lax.axis_index("batch")
    half, column = row // 4, lax.rem(row, 4)
    table = [arrival_ref[i : i + 1, :] for i in range(5)]
    c = jnp.where(table[1] == 0, core, 1 - core)
    z = jnp.where(table[2] == 0, half, 1 - half)
    x = jnp.bitwise_and(table[3] + column, 3)
    order = ((table[0] * 2 + c) * 8 + z * 4 + x) * 6 + table[4]
    t_scr[...] = dot(w_scr[...].T, places(order), NT)
    wt_ref[...] = t_scr[0:576].astype(BF)
    gains = t_scr[576:584]
    gains_ref[...] = gains
    gain, bias = gains[0:1], gains[1:2]
    for j in range(8):
        hat, _ = normalize(own_ref[j, 0:128, :].astype(F32))
        normed_ref[j * 128 : (j + 1) * 128, :] = (hat * gain + bias).astype(BF)
    for j in range(4):
        lanes = slice(j * 256, (j + 1) * 256)
        qkv = dot(wt_ref[...], normed_ref[lanes, :], NT).astype(BF)
        q_ref[:, lanes] = qkv[0:192]
        kv_ref[:, lanes] = qkv[192:576]


def last_keys(m, core, length):
    lane = lax.broadcasted_iota(jnp.int32, (1, 256), 1)
    query = m * 512 + 128 * core + jnp.where(lane < 128, lane, lane + 128)
    return jnp.minimum(query, length - 1)


def allowed(start, first, last, core):
    offset = start + first + (128 * core if first < 128 else -128 * core)
    return lax.broadcasted_iota(jnp.int32, (64, 256), 0) <= last - offset


def fill_keys(own_ref, other_ref, k_scr, base):
    for u in range(3):
        for j in range(8):
            rows, lanes = pl.ds(base + u * 64, 64), pl.ds(j * 128, 128)
            k_scr[u, j * 256 : j * 256 + 128, :] = own_ref[rows, lanes].T
            k_scr[u, j * 256 + 128 : j * 256 + 256, :] = other_ref[rows, lanes].T


def fill_lanes(own_ref, other_ref, scr, base):
    for j in range(8):
        scr[:, j * 256 : j * 256 + 128] = own_ref[base : base + 192, j * 128 : j * 128 + 128]
        scr[:, j * 256 + 128 : j * 256 + 256] = other_ref[
            base : base + 192, j * 128 : j * 128 + 128
        ]


PAIRS = [(h, u) for h in range(2) for u in range(3)]
CHUNKS = [slice(i * 64, i * 64 + 64) for i in range(4)]


def steps(m, length):
    return jnp.minimum(m + 1, (length + 511) // 512)


def sweep(length, begin, score, step, finish):
    def one(_, place):
        m, jk = place
        more = jk + 1 < steps(m, length)
        next_m = jnp.where(more, m, jnp.minimum(m + 1, 3))
        next_jk = jnp.where(more, jk + 1, 0)

        @pl.when(jk == 0)
        def _():
            begin()

        edge = (jk == m) | (jk * 512 + 512 > length)

        @pl.when(edge)
        def _():
            step(m, jk, next_m, next_jk, True)

        @pl.when(jnp.logical_not(edge))
        def _():
            step(m, jk, next_m, next_jk, False)

        @pl.when(jnp.logical_not(more))
        def _():
            finish(m)

        return jnp.where(more, m, m + 1), next_jk

    for h, u in PAIRS:
        score(h, u, 0, 0)
    total = sum(steps(m, length) for m in range(4))
    lax.fori_loop(0, total, one, (jnp.int32(0), jnp.int32(0)))


def group(m):
    return pl.ds(pl.multiple_of(m * 256, 256), 256)


def key_tile(jk, h):
    return pl.ds(pl.multiple_of(jk * 512, 512) + h * 256, 256)


def forward_plain(q_scr, k_scr, v_scr, scratch, length, core, finish):
    s_scr, w_scr, acc_scr, sum_scr = scratch[0:6], scratch[6:12], scratch[12:15], scratch[15:18]

    def begin():
        for u in range(3):
            acc_scr[u][...] = jnp.zeros((64, 256), F32)
            sum_scr[u][...] = jnp.zeros((8, 256), F32)

    def score(h, u, m, jk):
        queries = q_scr[u * 64 : (u + 1) * 64, group(m)]
        s_scr[h * 3 + u][...] = dot(k_scr[u, key_tile(jk, h), :], queries)

    def step(m, jk, next_m, next_jk, masked):
        last = last_keys(m, core, length)
        for h, u in PAIRS:
            scores, weights = s_scr[h * 3 + u], w_scr[h * 3 + u]
            total = sum_scr[u][...]
            for rows in CHUNKS:
                s = scores[rows, :]
                t = s * s + 1.0
                r = lax.rsqrt(t)
                e = jnp.exp(t * r)
                if masked:
                    e = jnp.where(allowed(jk * 512 + h * 256, rows.start, last, core), e, 0.0)
                total = total + jnp.sum(e.reshape(8, 8, 256), axis=0)
                weights[rows, :] = (s * r * e).astype(BF)
            sum_scr[u][...] = total
            score(h, u, next_m, next_jk)
            acc_scr[u][...] += dot(v_scr[u * 64 : (u + 1) * 64, key_tile(jk, h)], weights[...])

    def close(m):
        for u in range(3):
            total = jnp.sum(sum_scr[u][...], axis=0, keepdims=True)
            finish(m, u, acc_scr[u][...], total, jnp.zeros((1, 256), F32))

    sweep(length, begin, score, step, close)


def forward_any(q_scr, k_scr, v_scr, length, core, finish):
    def one(m, _):
        last = last_keys(m, core, length)

        def step(jk, carry):
            start = pl.multiple_of(jk * 256, 256)
            mask = jnp.concatenate([allowed(start, r.start, last, core) for r in CHUNKS], axis=0)
            out = []
            for u in range(3):
                top, total, accum = carry[u]
                s = dot(k_scr[u, pl.ds(start, 256), :], q_scr[u * 64 : (u + 1) * 64, group(m)])
                t = s * s + 1.0
                r = lax.rsqrt(t)
                a = jnp.where(mask, t * r, -1e30)
                fresh = jnp.maximum(top, jnp.max(a, axis=0, keepdims=True))
                e = jnp.exp(a - fresh)
                rescale = jnp.exp(top - fresh)
                total = total * rescale + jnp.sum(e, axis=0, keepdims=True)
                accum = accum * rescale + dot(
                    v_scr[u * 64 : (u + 1) * 64, pl.ds(start, 256)], (s * r * e).astype(BF)
                )
                out.append((fresh, total, accum))
            return tuple(out)

        zero = (jnp.zeros((1, 256), F32), jnp.zeros((1, 256), F32), jnp.zeros((64, 256), F32))
        carry = lax.fori_loop(0, 2 * steps(m, length), step, (zero,) * 3)
        for u in range(3):
            finish(m, u, carry[u][2], carry[u][1], carry[u][0])
        return 0

    lax.fori_loop(0, 4, one, 0)


def forward_kernel(
    lengths_ref, q_ref, own_ref, other_ref, o_ref, low_ref, lse_ref, q_scr, k_scr, v_scr, *scratch
):
    length, core = length_of(lengths_ref), core_of()
    fill_keys(own_ref, other_ref, k_scr, 0)
    fill_lanes(own_ref, other_ref, v_scr, 192)
    q_scr[...] = q_ref[...] * BF(0.125)

    def finish(m, u, accum, total, top):
        lanes = group(m)
        o = accum / total
        o_ref[u * 64 : (u + 1) * 64, lanes] = o
        for half in range(2):
            low_ref[2 * m + half, u * 64 : (u + 1) * 64, :] = o[
                :, half * 128 : half * 128 + 128
            ].astype(BF)
        lse_ref[u : u + 1, lanes] = top + jnp.log(total)

    def largest(ref):
        values = ref[0:192, :].astype(F32)
        return jnp.max(jnp.sum((values * values).reshape(3, 64, 1024), axis=1))

    bound = largest(q_ref) * jnp.maximum(largest(own_ref), largest(other_ref)) * (1.0 / 64.0)
    small = bound < 3600.0

    @pl.when(small)
    def _():
        forward_plain(q_scr, k_scr, v_scr, scratch, length, core, finish)

    @pl.when(jnp.logical_not(small))
    def _():
        forward_any(q_scr, k_scr, v_scr, length, core, finish)


def backward_kernel(
    lengths_ref, q_ref, own_ref, other_ref, o_ref, lse_ref, da_ref,
    dq_ref, down_ref, dother_ref,
    q_scr, k_scr, kt_scr, v_scr, da_scr, dk_scr, dv_scr, delta_scr, *scratch,
):
    s_scr, dp_scr, w_scr, ds_scr, dq_scr = (scratch[i : i + 6] for i in (0, 6, 12, 18, 24))
    length, core = length_of(lengths_ref), core_of()
    fill_keys(own_ref, other_ref, k_scr, 0)
    fill_lanes(own_ref, other_ref, kt_scr, 0)
    fill_keys(own_ref, other_ref, v_scr, 192)
    q_scr[...] = q_ref[...] * BF(0.125)
    for j in range(8):
        lanes = slice(j * 128, (j + 1) * 128)
        da_scr[:, lanes] = da_ref[j]
        for u in range(3):
            rows = slice(u * 64, (u + 1) * 64)
            delta_scr[u : u + 1, lanes] = jnp.sum(
                da_ref[j, rows, :].astype(F32) * o_ref[rows, lanes], axis=0, keepdims=True
            )
    dk_scr[...] = jnp.zeros_like(dk_scr)
    dv_scr[...] = jnp.zeros_like(dv_scr)

    def begin():
        for u in range(3):
            dq_scr[u][...] = jnp.zeros((64, 256), F32)

    def score(h, u, m, jk):
        rows, tile = slice(u * 64, (u + 1) * 64), key_tile(jk, h)
        s_scr[h * 3 + u][...] = dot(k_scr[u, tile, :], q_scr[rows, group(m)])
        dp_scr[h * 3 + u][...] = dot(v_scr[u, tile, :], da_scr[rows, group(m)])

    def step(m, jk, next_m, next_jk, masked):
        last = last_keys(m, core, length)
        for h, u in PAIRS:
            tile = key_tile(jk, h)
            heads = slice(u * 64, (u + 1) * 64)
            delta, lse = delta_scr[u : u + 1, group(m)], lse_ref[u : u + 1, group(m)]
            place = h * 3 + u
            for rows in CHUNKS:
                s = s_scr[place][rows, :]
                t = s * s + 1.0
                r = lax.rsqrt(t)
                p = jnp.exp(t * r - lse)
                if masked:
                    p = jnp.where(allowed(jk * 512 + h * 256, rows.start, last, core), p, 0.0)
                g = s * r
                w_scr[place][rows, :] = (g * p).astype(BF)
                ds = p * (dp_scr[place][rows, :] * (r * r * (r - 1.0) + 1.0) - g * delta)
                ds_scr[place][rows, :] = ds.astype(BF)
            score(h, u, next_m, next_jk)
            dv_scr[u, :, tile] += dot(da_scr[heads, group(m)], w_scr[place][...], NT)
            dk_scr[u, :, tile] += dot(q_scr[heads, group(m)], ds_scr[place][...], NT)
            dq_scr[u][...] += dot(kt_scr[heads, tile], ds_scr[place][...])

    def close(m):
        for u in range(3):
            dq_ref[u * 64 : (u + 1) * 64, group(m)] = (dq_scr[u][...] * 0.125).astype(BF)

    sweep(length, begin, score, step, close)
    for scr, base in ((dk_scr, 0), (dv_scr, 192)):
        for u in range(3):
            rows = pl.ds(base + u * 64, 64)
            for j in range(8):
                lanes = pl.ds(j * 128, 128)
                down_ref[rows, lanes] = scr[u, :, j * 256 : j * 256 + 128].astype(BF)
                dother_ref[rows, lanes] = scr[u, :, j * 256 + 128 : j * 256 + 256].astype(BF)


GELU_SCALE = math.sqrt(2.0 / math.pi)


def feed_kernel(
    att_hbm, order_hbm, x_hbm, gains_hbm, dy_hbm, weights_hbm,
    y_hbm, dfirst_hbm, low_hbm, datt_hbm, dgain_hbm, grads_hbm,
    att_ref, order_ref, x_ref, gains_ref, dy_ref, down_ref, up_ref, out_ref,
    y_ref, dfirst_ref, low_ref, datt_ref, dgain_ref, gdown, gup, acc_scr, dn_scr,
    place_ref, loads, stores,
):
    def block(ref, number):
        return ref.at[:, pl.ds(48 * number, 48), :]

    arrivals = [(att_hbm, att_ref), (order_hbm, order_ref), (x_hbm, x_ref)]
    arrivals += [(gains_hbm, gains_ref), (block(weights_hbm, 8), out_ref)]
    for k in range(4):
        arrivals.append((block(weights_hbm, 4 + k), up_ref.at[k]))
        if k == 0:
            arrivals.append((dy_hbm, dy_ref))
        arrivals.append((block(weights_hbm, k), down_ref.at[k]))
    arrivals = [pltpu.make_async_copy(*pair, loads.at[i]) for i, pair in enumerate(arrivals)]
    for copy in arrivals:
        copy.start()
    departures = []

    def send(source, target):
        copy = pltpu.make_async_copy(source, target, stores.at[len(departures)])
        copy.start()
        departures.append(copy)

    arrivals[1].wait()
    place_ref[...] = places(order_ref[...])
    for i in (0, 2, 3):
        arrivals[i].wait()
    gain, bias = gains_ref[2:3], gains_ref[3:4]
    natural = [
        jnp.concatenate([att_ref[2 * e + b] for e in range(4)], axis=0).T for b in range(2)
    ]
    attended = dot(jnp.concatenate(natural, axis=0), place_ref[...]).astype(BF)
    arrivals[4].wait()
    w_out = out_ref[...].reshape(768, 768)
    first = x_ref[...].astype(F32) + dot(attended, w_out)
    hat, scale = normalize(first)
    acc_scr[...] = first
    n2 = dot((hat * gain + bias).astype(BF), place_ref[...]).astype(BF)
    n2t = n2.T
    waiting = arrivals[5:]
    for k in range(4):
        waiting.pop(0).wait()
        up = up_ref[k].reshape(768, 768)
        hidden = dot(n2, up)
        if k == 0:
            waiting.pop(0).wait()
        waiting.pop(0).wait()
        down = down_ref[k].reshape(768, 768)
        dy = dy_ref[...]
        d_active = dot(dy, down, NT)
        square = hidden * hidden
        tanh = jnp.tanh(GELU_SCALE * hidden * (1.0 + 0.044715 * square))
        share = 0.5 + 0.5 * tanh
        active = (hidden * share).astype(BF)
        slope = share + 0.5 * hidden * (1.0 - tanh * tanh) * (
            GELU_SCALE * (1.0 + (3 * 0.044715) * square)
        )
        d_hidden = (slope * d_active).astype(BF)
        gdown[k] = dot(active.T, dy).astype(BF).reshape(16, 48, 768)
        send(gdown.at[k], block(grads_hbm, k))
        gup[k] = dot(n2t, d_hidden).astype(BF).reshape(16, 48, 768)
        send(gup.at[k], block(grads_hbm, 4 + k))
        acc_scr[...] += dot(active, down)
        d_n2 = dot(d_hidden, up, NT)
        dn_scr[...] = d_n2 if k == 0 else dn_scr[...] + d_n2
    y_ref[...] = acc_scr[...].astype(BF)
    send(y_ref, y_hbm)
    dn = dot(dn_scr[...].astype(BF), place_ref[...], NT)
    t = dn * gain
    part = t - jnp.mean(t, -1, keepdims=True) - hat * jnp.mean(t * hat, -1, keepdims=True)
    d_first = dy_ref[...].astype(F32) + part * scale
    low = d_first.astype(BF)
    low_ref[...] = low
    send(low_ref, low_hbm)
    dfirst_ref[...] = d_first
    send(dfirst_ref, dfirst_hbm)
    d_att = dot(w_out, low, NT).astype(BF)
    d_att = dot(place_ref[...], d_att).astype(BF)
    for b in range(2):
        for e in range(4):
            datt_ref[2 * e + b] = d_att[e * 192 : (e + 1) * 192, b * 128 : (b + 1) * 128]
    send(datt_ref, datt_hbm)
    dgain_ref[0:1, :] = jnp.sum(dn * hat, axis=0, keepdims=True)
    dgain_ref[1:2, :] = jnp.sum(dn, axis=0, keepdims=True)
    dgain_ref[2:8, :] = jnp.zeros((6, 768), F32)
    send(dgain_ref, dgain_hbm)
    for copy in departures:
        copy.wait()


def out_kernel(att_ref, low_ref, grad_ref):
    attended_t = [
        jnp.concatenate([att_ref[2 * e + b] for e in range(4)], axis=0) for b in range(2)
    ]
    grad = dot(jnp.concatenate(attended_t, axis=1), low_ref[...]).reshape(8, 2, 2, 24, 768)
    half = lax.axis_index("batch") // 4
    for j in range(8):
        rows = [
            jnp.where(half == z, grad[j, c, z], grad[j ^ 1, c, z]) for c in range(2) for z in range(2)
        ]
        grad_ref[j] = jnp.concatenate(rows, axis=0).astype(BF)


def whole(*dims):
    return pl.BlockSpec(dims, lambda *_: (0,) * len(dims))


def feed(*arrays):
    outs = [
        shape((256, 768), BF), shape((256, 768), F32), shape((256, 768), BF),
        shape((8, 192, 128), BF), shape((8, 768), F32), shape((16, 384, 768), BF),
    ]
    blocks = pltpu.VMEM((4, 16, 48, 768), BF)
    held = [pltpu.VMEM(a.shape, a.dtype) for a in arrays[:-1]]
    held += [blocks, blocks, pltpu.VMEM((16, 48, 768), BF)]
    held += [pltpu.VMEM(o.shape, o.dtype) for o in outs[:-1]]
    held += [blocks, blocks] + [pltpu.VMEM((256, 768), F32)] * 2
    held += [pltpu.VMEM((768, 768), BF)]
    held += [pltpu.SemaphoreType.DMA((14,)), pltpu.SemaphoreType.DMA((13,))]
    return call(
        feed_kernel,
        outs,
        arrays,
        15,
        held,
        in_specs=[pl.BlockSpec(memory_space=pl.ANY)] * len(arrays),
        out_specs=[pl.BlockSpec(memory_space=pl.ANY)] * len(outs),
    )


def unproject_kernel(
    own_ref, dq_ref, dkv_ref, partner_ref, normed_ref, wt_ref, dgain_ref, order_ref,
    out_ref, spread_ref,
    part_ref, mine_ref, theirs_ref, dt_scr, dw_scr, p_scr, o_scr,
):
    dt_scr[0:192, :] = dq_ref[...]
    dt_scr[192:576, :] = (dkv_ref[...].astype(F32) + partner_ref[...].astype(F32)).astype(BF)
    bias_sum = jnp.zeros((1, 768), F32)
    gain_sum = jnp.zeros((1, 768), F32)
    for j in range(4):
        d_normed = dot(dt_scr[:, j * 256 : (j + 1) * 256].T, wt_ref[...])
        part_ref[2 * j : 2 * j + 2] = d_normed.astype(BF).reshape(2, 128, 768)
        pair = jnp.concatenate([own_ref[2 * j, 0:128, :], own_ref[2 * j + 1, 0:128, :]], axis=0)
        hat, _ = normalize(pair.astype(F32))
        gain_sum += jnp.sum(d_normed * hat, axis=0, keepdims=True)
        bias_sum += jnp.sum(d_normed, axis=0, keepdims=True)
    dw_scr[0:576, :] = dot(dt_scr[...], normed_ref[...])
    dw_scr[576:577, :] = gain_sum
    dw_scr[577:578, :] = bias_sum
    dw_scr[578:580, :] = dgain_ref[0:2, :]
    dw_scr[580:640, :] = jnp.zeros((60, 768), F32)
    p_scr[...] = dot(dw_scr[...].astype(BF), places(order_ref[...])).T.astype(BF)
    out = jnp.zeros((96, 768), F32)
    for j in range(8):
        out += out_ref[j].astype(F32)
    lanes = lax.broadcasted_iota(jnp.int32, (128, 96), 1)
    spread = jnp.where(lanes == spread_ref[...], 1.0, 0.0).astype(BF)
    o_scr[...] = dot(spread, out.astype(BF))
    for dc, ref in enumerate((mine_ref, theirs_ref)):
        for dx in range(4):
            for dz in range(2):
                ref[dx, dz, :, 0:640] = p_scr[rows_at(dc, dz, dx), :]
                few = o_scr[rows_at(dc, dz, dx, 8), :]
                ref[dx, dz, :, 640:768] = jnp.concatenate(
                    [few[:, q * 128 : (q + 1) * 128] for q in range(6)], axis=0
                ).astype(BF)


def slots_kernel(rest_ref, qkv_ref, order_ref, out_ref, r_scr):
    r_scr[0:384, :] = rest_ref[...]
    r_scr[384:432, 0:640] = qkv_ref[:, 0:640]
    r_scr[384:432, 640:768] = jnp.zeros((48, 128), BF)
    r_scr[432:512, :] = jnp.zeros((80, 768), BF)
    rows = dot(places(order_ref[...], 448), r_scr[...])
    for j in range(8):
        out_ref[j] = rows[j * 56 : j * 56 + 56].astype(BF)


def finish_kernel(x_ref, dfirst_ref, gains_ref, got_ref, qkv_ref, dtok_ref, out_ref):
    for q in range(6):
        out_ref[:, q * 128 : (q + 1) * 128] = qkv_ref[q * 8 : q * 8 + 8, 640:768].astype(F32)[0:6]
    gain = gains_ref[0:1]
    for b in range(2):
        rows = slice(b * 128, (b + 1) * 128)
        dn = jnp.zeros((128, 768), F32)
        for e in range(4):
            dn += got_ref[2 * e + b].astype(F32)
        hat, scale = normalize(x_ref[rows, :].astype(F32))
        t = dn * gain
        part = t - jnp.mean(t, -1, keepdims=True) - hat * jnp.mean(t * hat, -1, keepdims=True)
        dtok_ref[rows, :] = (dfirst_ref[rows, :] + part * scale).astype(BF)


def sums_kernel(got_ref, units_ref, down_ref, up_ref, qkv_ref, g1_ref, b1_ref, g2_ref, b2_ref):
    total = jnp.zeros((56, 768), F32)
    chunks = []
    for e in range(4):
        both = got_ref[2 * e].astype(F32) + got_ref[2 * e + 1].astype(F32)
        chunks.append(both[48:54])
        total += both
    down_ref[...] = total[0:24]
    left, up, units = total[24:48], jnp.zeros((24, 768), F32), places(units_ref[...])
    for _ in range(3):
        piece = left.astype(BF)
        left = left - piece.astype(F32)
        up += dot(piece, units, NT)
    for k in range(4):
        up_ref[:, k * 768 : (k + 1) * 768] = up[k * 6 : k * 6 + 6]
    for s in range(3):
        qkv_ref[:, s * 768 : (s + 1) * 768] = jnp.concatenate(
            [chunks[e][:, s * 192 : (s + 1) * 192] for e in range(4)], axis=1
        )
    norms = total[:, 512:640].T
    for i, ref in enumerate((g1_ref, b1_ref, g2_ref, b2_ref)):
        ref[...] = norms[64 + i : 65 + i, 48:54]


def scalars(count):
    return dict(
        in_specs=[pl.BlockSpec(memory_space=pltpu.SMEM)]
        + [pl.BlockSpec(memory_space=pltpu.VMEM)] * (count - 1)
    )


def body(tokens, lengths, gain_one, bias_one, w_qkv, w_out, gain_two, bias_two, w_up, w_down, d_out):
    order, units, regroup, qkv_order = (
        jnp.asarray(v) for v in (ROW_ORDER, UNIT_ORDER, REGROUP, QKV_ORDER)
    )
    exchange = functools.partial(
        lax.all_to_all, axis_name="seq", split_axis=0, concat_axis=0, tiled=True,
        axis_index_groups=SAME_CORE,
    )

    vectors = [v.reshape(1, 6) for v in (gain_one, bias_one, gain_two, bias_two)]
    slots, raw = pl.pallas_call(
        pack_kernel,
        grid=(1,),
        in_specs=[whole(24, 768), whole(6, 768), whole(6, 3072), whole(6, 2304)]
        + [whole(1, 6)] * 4
        + [whole(1, 768)],
        out_specs=[whole(8, 56, 768), whole(24, 640)],
        out_shape=[shape((8, 56, 768), BF), shape((24, 640), BF)],
        scratch_shapes=[
            pltpu.VMEM((56, 768), F32), pltpu.VMEM((128, 128), F32), pltpu.VMEM((24, 640), F32),
        ],
        cost_estimate=about(2),
        compiler_params=pltpu.CompilerParams(vmem_limit_bytes=60 * 1024 * 1024),
    )(w_down, w_out, w_up, w_qkv, *vectors, units)
    slots = exchange(slots)
    near = jnp.stack([raw] + [lax.ppermute(raw, "batch", along_x(step)) for step in (-1, 2, 1)])
    far = lax.ppermute(near, BOTH, SWAP_HALF)
    rest = call(
        regroup_kernel,
        shape((432, 768), BF),
        (slots, regroup, near),
        2,
        [pltpu.VMEM((448, 768), F32)],
        mib=12,
        in_specs=[pl.BlockSpec(memory_space=pltpu.VMEM)] * 2
        + [pl.BlockSpec(memory_space=pl.ANY)],
    )
    weights = lax.all_gather(rest, BOTH, axis=0, axis_index_groups=RINGS)
    x = tokens.transpose(1, 0, 2)
    dy = d_out.transpose(1, 0, 2).reshape(256, 768)
    sent = call(
        address_kernel,
        shape((8, 176, 768), BF),
        (x, near, far),
        2,
        [pltpu.VMEM((4, 48, 640), F32)],
        mib=16,
    )
    own = exchange(sent)
    other = lax.ppermute(own[:, 128:176, 0:640], "seq", SWAP_CORE)
    x = x.reshape(256, 768)

    normed, wt, gains, q_t, kv = call(
        project_kernel,
        [
            shape((1024, 768), BF), shape((576, 768), BF), shape((8, 768), F32),
            shape((192, 1024), BF), shape((384, 1024), BF),
        ],
        (own, other, jnp.asarray(ARRIVAL)),
        5,
        [pltpu.VMEM((768, 640), BF), pltpu.VMEM((640, 768), F32)],
        mib=30,
    )
    kv_other = lax.ppermute(kv, "seq", SWAP_CORE)
    o, o_low, lse = call(
        forward_kernel,
        [shape((192, 1024), F32), shape((8, 192, 128), BF), shape((3, 1024), F32)],
        (lengths, q_t, kv, kv_other),
        12,
        [
            pltpu.VMEM((192, 1024), BF), pltpu.VMEM((3, 2048, 64), BF),
            pltpu.VMEM((192, 2048), BF),
        ]
        + [pltpu.VMEM((256, 256), F32)] * 6
        + [pltpu.VMEM((256, 256), BF)] * 6
        + [pltpu.VMEM((64, 256), F32)] * 3
        + [pltpu.VMEM((8, 256), F32)] * 3,
        mib=30,
        **scalars(4),
    )
    att = exchange(o_low)
    y, d_first, low, d_att, d_gain, grads = feed(att, order, x, gains, dy, weights)
    rest_sum = lax.psum_scatter(
        grads.reshape(16 * 384, 768), BOTH, scatter_dimension=0, tiled=True,
        axis_index_groups=RINGS,
    )
    d_att = exchange(d_att)
    out_grad = exchange(call(out_kernel, shape((8, 96, 768), BF), (att, low), 2))
    dq, dkv, dkv_other = call(
        backward_kernel,
        [shape((192, 1024), BF), shape((384, 1024), BF), shape((384, 1024), BF)],
        (lengths, q_t, kv, kv_other, o, lse, d_att),
        20,
        [
            pltpu.VMEM((192, 1024), BF),
            pltpu.VMEM((3, 2048, 64), BF),
            pltpu.VMEM((192, 2048), BF),
            pltpu.VMEM((3, 2048, 64), BF),
            pltpu.VMEM((192, 1024), BF),
            pltpu.VMEM((3, 64, 2048), F32),
            pltpu.VMEM((3, 64, 2048), F32),
            pltpu.VMEM((3, 1024), F32),
        ]
        + [pltpu.VMEM((256, 256), F32)] * 12
        + [pltpu.VMEM((256, 256), BF)] * 12
        + [pltpu.VMEM((64, 256), F32)] * 3,
        mib=60,
        **scalars(7),
    )
    partner = lax.ppermute(dkv_other, "seq", SWAP_CORE)
    part, mine, theirs = call(
        unproject_kernel,
        [shape((8, 128, 768), BF), shape((4, 2, 48, 768), BF), shape((4, 2, 48, 768), BF)],
        (own, dq, dkv, partner, normed, wt, d_gain, qkv_order, out_grad, jnp.asarray(SPREAD)),
        7,
        [
            pltpu.VMEM((576, 1024), BF), pltpu.VMEM((640, 768), F32),
            pltpu.VMEM((768, 640), BF), pltpu.VMEM((128, 768), F32),
        ],
        mib=60,
    )
    add = lambda *parts: sum(p.astype(F32) for p in parts).astype(BF)
    line = add(mine, lax.ppermute(theirs, "seq", SWAP_CORE))
    line = add(
        line[0],
        lax.ppermute(line[1], "batch", along_x(1)),
        lax.ppermute(line[2], "batch", along_x(2)),
        lax.ppermute(line[3], "batch", along_x(-1)),
    )
    qkv_sum = add(line[0], lax.ppermute(line[1], BOTH, SWAP_HALF))
    back = exchange(part)
    d_tokens, d_out_w = call(
        finish_kernel,
        [shape((256, 768), BF), shape((6, 768), F32)],
        (x, d_first, gains, back, qkv_sum),
        3,
        mib=16,
    )
    slots = call(
        slots_kernel,
        shape((8, 56, 768), BF),
        (rest_sum, qkv_sum, regroup),
        2,
        [pltpu.VMEM((512, 768), BF)],
        mib=12,
    )
    slots = exchange(slots)
    vector = shape((1, 6), F32)
    d_down, d_up, d_qkv, *norms = call(
        sums_kernel,
        [shape((24, 768), F32), shape((6, 3072), F32), shape((6, 2304), F32)]
        + [vector] * 4,
        (slots, units),
        2,
        mib=12,
    )
    norms = [v.reshape(6) for v in norms]
    output = y.reshape(2, 128, 768).transpose(1, 0, 2)
    d_tokens = d_tokens.reshape(2, 128, 768).transpose(1, 0, 2)
    return (
        output, d_tokens, norms[0], norms[1], d_qkv, d_out_w, norms[2], norms[3], d_up, d_down,
    )


def solution(mesh):
    rows = P(("seq", "batch"))
    tokens = P("seq", "batch", None)
    return jax.shard_map(
        body,
        mesh=mesh,
        in_specs=(tokens, P("batch"), rows, rows, rows, rows, rows, rows, rows, rows, tokens),
        out_specs=(tokens, tokens, rows, rows, rows, rows, rows, rows, rows, rows),
        check_vma=False,
    )
```
